32 devices in a mesh: dp: 8 (over z, x), tensor: 4 (over y, core).
Axes of the slice: x: 2, y: 2, z: 4, core: 2. Of those that a mesh axis runs over, the one named last changes fastest.
Arguments:
- tokens: bfloat16 [32768, 768], P(('dp', 'tensor')), may hold values from -6 to 6
- lengths: int32 [64], P(('dp', 'tensor')), may hold values from 16 to 512, as said below
- frozen_attention_weights: bfloat16 [2, 3072, 768], P(None, ('dp', 'tensor')), may hold values from -6 to 6
- adapter_down_weights: bfloat16 [2, 2, 768, 8], replicated, may hold values from -0.21875 to 0.21875
- adapter_up_weights: bfloat16 [2, 2, 8, 768], replicated, may hold values from -1 to 1
- frozen_expand_weight: bfloat16 [2, 768, 3072], P(None, None, 'tensor'), may hold values from -0.21875 to 0.21875
- frozen_project_weight: bfloat16 [2, 3072, 768], P(None, 'tensor'), may hold values from -0.109375 to 0.109375
- frozen_norm_gains: float32 [2, 2, 768], replicated, may hold values from 0.5 to 1.5
- cotangent: bfloat16 [32768, 768], P(('dp', 'tensor')), may hold values from -6 to 6
Outputs:
- hidden_out: bfloat16 [32768, 768], P(('dp', 'tensor'))
- input_grad: float32 [32768, 768], P(('dp', 'tensor'))
- lora_a_grad: float32 [2, 2, 768, 8], replicated
- lora_b_grad: float32 [2, 2, 8, 768], replicated
The draws below stay inside these ranges and needn't reach their ends.
Inputs may be any that keep to these rules, and one draw needn't show every extreme that they name: The first lengths[r] tokens of row r are valid, the rest are padding for keys.
All inputs are finite; a program needn't handle non-finite values.
Results may differ from the reference program's by a relative error of at most 0.033.
Values may be sent and summed in bfloat16 or wider, within the bound.
A program may use at most 256 MiB of HBM per device.

```python
import math
import jax
import jax.numpy as jnp
from jax import lax

MODEL_WIDTH = 768
HEADS = 12
HEAD_DIM = 64
FF = 3072
SEQ = 512
ADAPTER_RANK = 8
LAYER_COUNT = 2
GROUP_ROWS = 8
ROWS = 64
TOKENS = 32768


def draw_lengths(key, part):
    key_one, key_two, key_three = jax.random.split(jax.random.fold_in(key, 17), 3)
    row_index = jnp.arange(ROWS)
    group_index = row_index // GROUP_ROWS
    group_count = ROWS // GROUP_ROWS
    offset = jax.random.randint(key_one, (), 0, group_count)
    chosen = (group_index - offset) % 16 == 0
    heads_up = jax.random.randint(key_two, (ROWS,), 0, 2) == 1
    anchor = row_index == offset * GROUP_ROWS
    least_row = row_index == (offset * GROUP_ROWS + 1) % ROWS
    least_len = max(4, SEQ // 32)
    short_rows = jax.random.randint(key_three, (ROWS,), least_len, SEQ // 2 + 1)
    drawn = jnp.where(chosen & heads_up | anchor, SEQ, short_rows)
    return jnp.where(least_row, least_len, drawn).astype(jnp.int32)


def draw_frozen_attention_weights(key, part):
    row_index = jnp.arange(4 * MODEL_WIDTH)
    spread = jnp.where(row_index < 3 * MODEL_WIDTH, float(MODEL_WIDTH) ** (-0.5), float(max(1, MODEL_WIDTH // 64)) ** (-0.5))
    base = jnp.clip(jax.random.normal(jax.random.fold_in(key, 23), (LAYER_COUNT, 4 * MODEL_WIDTH, MODEL_WIDTH), jnp.float32), -6.0, 6.0)
    return (base * spread[None, :, None]).astype(jnp.bfloat16)


def steps_of(stream_key, extent, cuts, low, high):
    gain = 1.0
    for axis_at, shards_of in cuts:
        draws = jax.random.uniform(jax.random.fold_in(jax.random.fold_in(stream_key, 6), axis_at), (shards_of,), jnp.float32, low / len(cuts), high / len(cuts))
        gain = gain * jnp.repeat(jnp.exp(draws), extent[axis_at] // shards_of).reshape((-1,) + (1,) * (len(extent) - 1 - axis_at))
    return gain


def scatter_about(stream_key, shape, width, bound, shards=(), dtype=jnp.bfloat16):
    entries = width * jax.random.normal(stream_key, shape, jnp.float32)
    if shards:
        entries = entries * steps_of(stream_key, shape, shards, -0.22, 0.18)
    return jnp.clip(entries, -bound, bound).astype(dtype)


def setup_inputs(seed: int = 0) -> dict:
    streams_of = jax.random.split(jax.random.key(seed), 10)
    return {
        "tokens": scatter_about(streams_of[0], (TOKENS, MODEL_WIDTH), 1.0, 6.0, ((0, 32),)),
        "lengths": draw_lengths(jax.random.fold_in(streams_of[9], 71), 0),
        "frozen_attention_weights": draw_frozen_attention_weights(jax.random.fold_in(streams_of[9], 71), 0),
        "adapter_down_weights": scatter_about(streams_of[3], (LAYER_COUNT, 2, MODEL_WIDTH, ADAPTER_RANK), MODEL_WIDTH ** -0.5, 0.21875),
        "adapter_up_weights": scatter_about(streams_of[4], (LAYER_COUNT, 2, ADAPTER_RANK, MODEL_WIDTH), (4 * ADAPTER_RANK) ** -0.5, 1.0),
        "frozen_expand_weight": scatter_about(streams_of[5], (LAYER_COUNT, MODEL_WIDTH, FF), MODEL_WIDTH ** -0.5, 0.21875, ((2, 4),)),
        "frozen_project_weight": scatter_about(streams_of[6], (LAYER_COUNT, FF, MODEL_WIDTH), FF ** -0.5, 0.109375, ((1, 4),)),
        "frozen_norm_gains": jnp.clip(1.0 + 0.1 * jax.random.normal(streams_of[7], (LAYER_COUNT, 2, MODEL_WIDTH), jnp.float32), 0.5, 1.5),
        "cotangent": scatter_about(streams_of[8], (TOKENS, MODEL_WIDTH), 1.0, 6.0, ((0, 32),)),
    }


@jax.custom_vjp
def reduced_rows(v):
    return lax.optimization_barrier(v.astype(jnp.bfloat16)).astype(jnp.float32)

@jax.custom_vjp
def reduced_gradient(v):
    return v

def low_keep(v):
    return (reduced_rows(v), None)

def low_pass(kept, grad):
    return (grad,)

def back_keep(v):
    return (v, None)

def back_low(kept, grad):
    return (reduced_rows(grad),)
reduced_rows.defvjp(low_keep, low_pass)
reduced_gradient.defvjp(back_keep, back_low)
highest = lax.Precision.HIGHEST
epsilon = 1e-05
adapter_scale = 2.0
masked_score = -1000000000.0

def matrix_product(left_side, right_side):
    return jnp.dot(left_side, right_side, precision=highest)

def layer_norm(values, norm_gain):
    centre = lax.optimization_barrier(jnp.mean(values, axis=-1, keepdims=True))
    centred = values - centre
    spread = lax.optimization_barrier(jnp.mean(centred * centred, axis=-1, keepdims=True))
    return centred * lax.rsqrt(spread + epsilon) * norm_gain

def attend(query_rows, key_rows, value_outputs, row_length):
    q_heads = query_rows.reshape(SEQ, HEADS, HEAD_DIM)
    k_heads = key_rows.reshape(SEQ, HEADS, HEAD_DIM)
    v_heads = value_outputs.reshape(SEQ, HEADS, HEAD_DIM)
    scores = reduced_gradient(jnp.einsum('qhd,khd->hqk', q_heads, k_heads, precision=highest) * HEAD_DIM ** (-0.5))
    is_valid = jnp.arange(SEQ) < row_length
    scores = jnp.where(is_valid[None, None, :], scores, masked_score)
    row_probs = reduced_rows(jax.nn.softmax(scores, axis=-1))
    mixed_out = jnp.einsum('hqk,khd->qhd', row_probs, v_heads, precision=highest)
    return mixed_out.reshape(SEQ, MODEL_WIDTH)

def block(inputs, frozen, adapt_a, up_adapter, first_weight, second_weight, gains, row_lengths):
    query_matrix = frozen[0:MODEL_WIDTH]
    key_weight = frozen[MODEL_WIDTH:2 * MODEL_WIDTH]
    value_matrix = frozen[2 * MODEL_WIDTH:3 * MODEL_WIDTH]
    output_weight = frozen[3 * MODEL_WIDTH:4 * MODEL_WIDTH]
    rounded_result = reduced_rows(inputs)
    reduced_query = reduced_rows(reduced_gradient(matrix_product(rounded_result, adapt_a[0])))
    reduced_values = reduced_rows(reduced_gradient(matrix_product(rounded_result, adapt_a[1])))
    query_rows = reduced_rows(reduced_gradient(matrix_product(rounded_result, query_matrix) + adapter_scale * matrix_product(reduced_query, up_adapter[0])))
    key_rows = reduced_rows(reduced_gradient(matrix_product(rounded_result, key_weight)))
    value_outputs = reduced_rows(reduced_gradient(matrix_product(rounded_result, value_matrix) + adapter_scale * matrix_product(reduced_values, up_adapter[1])))
    row_total = row_lengths.shape[0]
    mixed_out = jax.vmap(jax.checkpoint(attend))(query_rows.reshape(row_total, SEQ, MODEL_WIDTH), key_rows.reshape(row_total, SEQ, MODEL_WIDTH), value_outputs.reshape(row_total, SEQ, MODEL_WIDTH), row_lengths).reshape(row_total * SEQ, MODEL_WIDTH)
    mixed_out = reduced_rows(reduced_gradient(mixed_out))
    pre_first = rounded_result + reduced_gradient(matrix_product(mixed_out, output_weight))
    normed = reduced_rows(layer_norm(pre_first, gains[0]))
    hidden_pre = reduced_gradient(matrix_product(normed, first_weight))
    ffn_result = reduced_gradient(matrix_product(reduced_rows(jax.nn.gelu(hidden_pre, approximate=False)), second_weight))
    return layer_norm(normed + ffn_result, gains[1])

def reference(tokens, lengths, frozen_attention_weights, adapter_down_weights, adapter_up_weights, frozen_expand_weight, frozen_project_weight, frozen_norm_gains, cotangent):
    scan_rows = math.gcd(ROWS, max(1, 4096 // SEQ))
    blocks = ROWS // scan_rows
    frozen = frozen_attention_weights.astype(jnp.float32)
    down_adapter_stack = adapter_down_weights.astype(jnp.float32)
    up_adapter_stack = adapter_up_weights.astype(jnp.float32)
    first_all = frozen_expand_weight.astype(jnp.float32)
    second_all = frozen_project_weight.astype(jnp.float32)

    def forward(inputs, adapt_a, up_adapter, row_lengths):
        for layer_position in range(LAYER_COUNT):
            inputs = block(inputs, frozen[layer_position], adapt_a[layer_position], up_adapter[layer_position], first_all[layer_position], second_all[layer_position], frozen_norm_gains[layer_position], row_lengths)
        return inputs

    def step(carry, pieces):
        block_tokens, block_grad, block_lengths = pieces

        def forward_fn(inputs, adapt_a, up_adapter):
            return forward(inputs, adapt_a, up_adapter, block_lengths)
        output, pull_back = jax.vjp(forward_fn, block_tokens, down_adapter_stack, up_adapter_stack)
        grad_in, grad_a, grad_b = pull_back(block_grad)
        return ((carry[0] + grad_a, carry[1] + grad_b), (output.astype(jnp.bfloat16), grad_in))
    token_blocks = tokens.astype(jnp.float32).reshape(blocks, scan_rows * SEQ, MODEL_WIDTH)
    grad_blocks = cotangent.astype(jnp.float32).reshape(blocks, scan_rows * SEQ, MODEL_WIDTH)
    length_blocks = lengths.reshape(blocks, scan_rows)
    start_carry = (jnp.zeros((LAYER_COUNT, 2, MODEL_WIDTH, ADAPTER_RANK), jnp.float32), jnp.zeros((LAYER_COUNT, 2, ADAPTER_RANK, MODEL_WIDTH), jnp.float32))
    (grad_a_sum, grad_b_sum), (outputs, input_grads) = lax.scan(step, start_carry, (token_blocks, grad_blocks, length_blocks))
    return (outputs.reshape(TOKENS, MODEL_WIDTH), input_grads.reshape(TOKENS, MODEL_WIDTH), grad_a_sum, grad_b_sum)
```

```python
import functools
import jax
import jax.numpy as jnp
from jax import lax
from jax.experimental import pallas as pl
from jax.experimental.pallas import tpu as pltpu
from jax.sharding import PartitionSpec as P

WIDTH = 768
HEADS = 12
HEAD_DIM = 64
SEQ = 512
RANK = 8
EPS = 1e-05
BF = jnp.bfloat16
F32 = jnp.float32
VMEM_LIMIT = 60 * 1024 * 1024
EXP2_SCALE = 1.4426950408889634 * HEAD_DIM ** (-0.5)


def dot(a, b):
    return jnp.dot(a, b, preferred_element_type=F32)


def dot_nt(a, b):
    return lax.dot_general(a, b, (((1,), (1,)), ((), ())), preferred_element_type=F32)


def dot_tn(a, b):
    return lax.dot_general(a, b, (((0,), (0,)), ((), ())), preferred_element_type=F32)


def mean_rows(v):
    return jnp.sum(v, axis=-1, keepdims=True) * (1.0 / WIDTH)


def params(n):
    return pltpu.CompilerParams(
        dimension_semantics=("arbitrary",) * n, vmem_limit_bytes=VMEM_LIMIT
    )


GROUP = 4


def attend_kernel(len_ref, x_ref, w_ref, a_ref, b_ref, g_ref,
                  qkv_ref, u_ref, o_ref, e_ref, rinv_ref, n1_ref, r1_ref, bound_ref):
    row, grp = pl.program_id(0), pl.program_id(1)

    @pl.when(grp == 0)
    def _():
        x = x_ref[...]
        u = dot(x, a_ref[...]).astype(BF)
        u_ref[...] = u
        for i in range(3):
            acc = dot(x, w_ref[WIDTH * i:WIDTH * (i + 1), :])
            if i != 1:
                acc += dot(u, b_ref[i // 2])
            qkv_ref[:, WIDTH * i:WIDTH * (i + 1)] = acc.astype(BF)
        key = lax.broadcasted_iota(jnp.int32, (SEQ, 128), 0)
        bound_ref[...] = jnp.where(key < len_ref[row], 3.0e38, -8.0e9)

    lane = lax.broadcasted_iota(jnp.int32, (SEQ, 128), 1)
    low = lane < HEAD_DIM
    bound = bound_ref[...]
    bound = jnp.concatenate([bound] * 4, axis=1)
    for pair in range(GROUP // 2):
        at = pl.multiple_of(grp * (GROUP * HEAD_DIM) + pair * 128, 128)
        q = qkv_ref[:, pl.ds(at, 128)]
        k = qkv_ref[:, pl.ds(WIDTH + at, 128)]
        v = qkv_ref[:, pl.ds(2 * WIDTH + at, 128)]
        outs = []
        for half in range(2):
            mine = low if half == 0 else ~low
            qh = jnp.where(mine, q, jnp.zeros_like(q))
            vh = jnp.where(mine, v, jnp.ones_like(v))
            s = jnp.minimum(dot_nt(k, qh), bound)
            top = jnp.max(s, axis=0, keepdims=True)
            e = jnp.exp2((s - top) * EXP2_SCALE).astype(BF)
            e_ref[0, pair * 2 + half] = e
            ot = dot_tn(vh, e)
            if half == 0:
                o_t, l = ot[:HEAD_DIM], ot[HEAD_DIM:HEAD_DIM + 8]
            else:
                o_t, l = ot[HEAD_DIM:], ot[0:8]
            r = 1.0 / l
            rinv_ref[0, grp * GROUP + pair * 2 + half] = r
            outs.append(o_t * r[0:1])
        both = jnp.concatenate(outs, axis=0)
        o_ref[:, pl.ds(at, 128)] = both.T.astype(BF)

    @pl.when(grp == pl.num_programs(1) - 1)
    def _():
        h = x_ref[...].astype(F32) + dot(o_ref[...], w_ref[3 * WIDTH:, :])
        c = h - mean_rows(h)
        r = lax.rsqrt(mean_rows(c * c) + EPS)
        n1_ref[...] = (c * r * g_ref[...]).astype(BF)
        r1_ref[...] = jnp.broadcast_to(r, (SEQ, 128))


def attend_forward(lengths, x, w, a, b, g):
    rows = lengths.shape[0]
    tokens = rows * SEQ
    steps = HEADS // GROUP
    row_block = lambda width: pl.BlockSpec((SEQ, width), lambda r, s: (r, 0))
    whole = lambda *shape: pl.BlockSpec(shape, lambda r, s: (0,) * len(shape), pipeline_mode=pl.Buffered(1))
    return pl.pallas_call(
        attend_kernel,
        grid=(rows, steps),
        in_specs=[
            pl.BlockSpec(memory_space=pltpu.SMEM),
            row_block(WIDTH), whole(4 * WIDTH, WIDTH), whole(WIDTH, 2 * RANK),
            whole(2, 2 * RANK, WIDTH), whole(1, WIDTH),
        ],
        out_specs=[
            row_block(3 * WIDTH), row_block(2 * RANK), row_block(WIDTH),
            pl.BlockSpec((1, GROUP, SEQ, SEQ), lambda r, s: (r, s, 0, 0)),
            pl.BlockSpec((1, HEADS, 8, SEQ), lambda r, s: (r, 0, 0, 0)),
            row_block(WIDTH), row_block(128),
        ],
        out_shape=[
            jax.ShapeDtypeStruct((tokens, 3 * WIDTH), BF),
            jax.ShapeDtypeStruct((tokens, 2 * RANK), BF),
            jax.ShapeDtypeStruct((tokens, WIDTH), BF),
            jax.ShapeDtypeStruct((rows, HEADS, SEQ, SEQ), BF),
            jax.ShapeDtypeStruct((rows, HEADS, 8, SEQ), F32),
            jax.ShapeDtypeStruct((tokens, WIDTH), BF),
            jax.ShapeDtypeStruct((tokens, 128), F32),
        ],
        scratch_shapes=[pltpu.VMEM((SEQ, 128), F32)],
        compiler_params=params(2),
        name="attend_forward",
    )(lengths, x, w, a, b, g)


BLOCK = 256
CHUNK = 768


def normal_parts(z):
    d = jnp.exp2(z * z * (-0.5 * 1.4426950408889634))
    t = 1.0 / (1.0 + jnp.abs(z) * (0.3275911 * 0.7071067811865476))
    q = t * (0.5 * 0.254829592 + t * (0.5 * -0.284496736 + t * (0.5 * 1.421413741
             + t * (0.5 * -1.453152027 + t * (0.5 * 1.061405429)))))
    tail = q * d
    cdf = jnp.where(z < 0, tail, 1.0 - tail)
    return cdf, d * 0.3989422804014327


def ffn_kernel(n1_ref, w1_ref, w2_ref, g_ref, gd_ref, x2_ref, r2_ref):
    n1 = n1_ref[...]
    f = n1.astype(F32)
    for j in range(4):
        z = dot(n1, w1_ref[j])
        cdf, pdf = normal_parts(z)
        gd_ref[:, CHUNK * j:CHUNK * (j + 1)] = (cdf + z * pdf).astype(BF)
        f = f + dot((z * cdf).astype(BF), w2_ref[j])
    c = f - mean_rows(f)
    r = lax.rsqrt(mean_rows(c * c) + EPS)
    x2_ref[...] = (c * r * g_ref[...]).astype(BF)
    r2_ref[...] = jnp.broadcast_to(r, (BLOCK, 128))


def ffn_forward(n1, w1, w2, g):
    tokens = n1.shape[0]
    block = lambda width: pl.BlockSpec((BLOCK, width), lambda s: (s, 0))
    whole = lambda *shape: pl.BlockSpec(shape, lambda s: (0,) * len(shape), pipeline_mode=pl.Buffered(1))
    return pl.pallas_call(
        ffn_kernel,
        grid=(tokens // BLOCK,),
        in_specs=[block(WIDTH), whole(4, WIDTH, CHUNK), whole(4, CHUNK, WIDTH), whole(1, WIDTH)],
        out_specs=[block(4 * CHUNK), block(WIDTH), block(128)],
        out_shape=[
            jax.ShapeDtypeStruct((tokens, 4 * CHUNK), BF),
            jax.ShapeDtypeStruct((tokens, WIDTH), BF),
            jax.ShapeDtypeStruct((tokens, 128), F32),
        ],
        compiler_params=params(1),
        name="ffn_forward",
    )(n1, w1, w2, g)


def norm_back(e, m, r):
    return r * (e - mean_rows(e) - m * mean_rows(e * m))


def ffn_back_kernel(dy_ref, x2_ref, r2_ref, n1_ref, r1_ref, gd_ref, w1_ref, w2_ref, wo_ref,
                    g1_ref, g2_ref, dh_ref, do_ref):
    g2, g1 = g2_ref[...], g1_ref[...]
    dh2 = norm_back(dy_ref[...].astype(F32) * g2, x2_ref[...].astype(F32) * (1.0 / g2), r2_ref[:, 0:1])
    df = dh2.astype(BF)
    dn = dh2
    for j in range(4):
        dz = (dot_nt(df, w2_ref[j]) * gd_ref[:, CHUNK * j:CHUNK * (j + 1)].astype(F32)).astype(BF)
        dn = dn + dot_nt(dz, w1_ref[j])
    dh = norm_back(dn * g1, n1_ref[...].astype(F32) * (1.0 / g1), r1_ref[:, 0:1])
    dh_ref[...] = dh
    do_ref[...] = dot_nt(dh.astype(BF), wo_ref[...]).astype(BF)


def ffn_backward(dy, x2, r2, n1, r1, gd, w1, w2, w, g1, g2):
    tokens = n1.shape[0]
    block = lambda width: pl.BlockSpec((BLOCK, width), lambda s: (s, 0))
    whole = lambda *shape: pl.BlockSpec(shape, lambda s: (0,) * len(shape), pipeline_mode=pl.Buffered(1))
    return pl.pallas_call(
        ffn_back_kernel,
        grid=(tokens // BLOCK,),
        in_specs=[block(WIDTH), block(WIDTH), block(128), block(WIDTH), block(128), block(4 * CHUNK),
                  whole(4, WIDTH, CHUNK), whole(4, CHUNK, WIDTH),
                  pl.BlockSpec((WIDTH, WIDTH), lambda s: (3, 0), pipeline_mode=pl.Buffered(1)),
                  whole(1, WIDTH), whole(1, WIDTH)],
        out_specs=[block(WIDTH), block(WIDTH)],
        out_shape=[jax.ShapeDtypeStruct((tokens, WIDTH), F32), jax.ShapeDtypeStruct((tokens, WIDTH), BF)],
        compiler_params=params(1),
        name="ffn_backward",
    )(dy, x2, r2, n1, r1, gd, w1, w2, w, g1, g2)


def attend_back_kernel(do_ref, dh_ref, x_ref, u_ref, qkv_ref, o_ref, e_ref, rinv_ref, w_ref, a_ref, b_ref,
                       dx_ref, ga_ref, gb_ref, d_ref):
    row, grp = pl.program_id(0), pl.program_id(1)
    lane = lax.broadcasted_iota(jnp.int32, (SEQ, 128), 1)
    low = lane < HEAD_DIM
    for pair in range(GROUP // 2):
        at = pl.multiple_of(grp * (GROUP * HEAD_DIM) + pair * 128, 128)
        q = qkv_ref[:, pl.ds(at, 128)]
        k = qkv_ref[:, pl.ds(WIDTH + at, 128)]
        v = qkv_ref[:, pl.ds(2 * WIDTH + at, 128)]
        head = grp * GROUP + pair * 2
        scale = jnp.concatenate([rinv_ref[0, head]] * 8 + [rinv_ref[0, head + 1]] * 8, axis=0).T
        dos = do_ref[:, pl.ds(at, 128)].astype(F32) * scale
        other = pltpu.roll(-dos * o_ref[:, pl.ds(at, 128)].astype(F32), HEAD_DIM, 1).astype(BF)
        dos = dos.astype(BF)
        dvs, dks, dqs = [], [], []
        for half in range(2):
            mine = low if half == 0 else ~low
            e = e_ref[0, pair * 2 + half]
            dp = dot_nt(jnp.where(mine, v, jnp.ones_like(v)), jnp.where(mine, dos, other))
            ds = (dp * e.astype(F32)).astype(BF)
            dvs.append(dot(e, dos))
            dks.append(dot(ds, q))
            dqs.append(dot_tn(k, ds)[half * HEAD_DIM:(half + 1) * HEAD_DIM])
        d_ref[:, pl.ds(2 * WIDTH + at, 128)] = jnp.where(low, dvs[0], dvs[1]).astype(BF)
        d_ref[:, pl.ds(WIDTH + at, 128)] = (jnp.where(low, dks[0], dks[1]) * HEAD_DIM ** (-0.5)).astype(BF)
        d_ref[:, pl.ds(at, 128)] = (jnp.concatenate(dqs, axis=0) * HEAD_DIM ** (-0.5)).T.astype(BF)

    @pl.when((row == 0) & (grp == 0))
    def _():
        ga_ref[...] = jnp.zeros_like(ga_ref)
        gb_ref[...] = jnp.zeros_like(gb_ref)

    @pl.when(grp == pl.num_programs(1) - 1)
    def _():
        dq, dk, dv = (d_ref[:, WIDTH * i:WIDTH * (i + 1)] for i in range(3))
        du = (dot_nt(dq, b_ref[0]) + dot_nt(dv, b_ref[1])).astype(BF)
        ga_ref[...] += dot_tn(du, x_ref[...])
        u = u_ref[...]
        u2 = u + u
        gb_ref[0] += dot_tn(u2, dq)
        gb_ref[1] += dot_tn(u2, dv)
        dx_ref[...] = (dh_ref[...] + dot_nt(dq, w_ref[0:WIDTH]) + dot_nt(dk, w_ref[WIDTH:2 * WIDTH])
                       + dot_nt(dv, w_ref[2 * WIDTH:3 * WIDTH]) + dot_nt(du, a_ref[...]))


def attend_backward(do, dh, x, u, qkv, o, e, rinv, w, a, b):
    rows = e.shape[0]
    tokens = rows * SEQ
    row_block = lambda width: pl.BlockSpec((SEQ, width), lambda r, s: (r, 0))
    whole = lambda *shape: pl.BlockSpec(shape, lambda r, s: (0,) * len(shape), pipeline_mode=pl.Buffered(1))
    return pl.pallas_call(
        attend_back_kernel,
        grid=(rows, HEADS // GROUP),
        in_specs=[
            row_block(WIDTH), row_block(WIDTH), row_block(WIDTH), row_block(2 * RANK), row_block(3 * WIDTH),
            row_block(WIDTH),
            pl.BlockSpec((1, GROUP, SEQ, SEQ), lambda r, s: (r, s, 0, 0)),
            pl.BlockSpec((1, HEADS, 8, SEQ), lambda r, s: (r, 0, 0, 0)),
            whole(3 * WIDTH, WIDTH), whole(WIDTH, 2 * RANK), whole(2, 2 * RANK, WIDTH),
        ],
        out_specs=[
            row_block(WIDTH),
            pl.BlockSpec((2 * RANK, WIDTH), lambda r, s: (0, 0)),
            pl.BlockSpec((2, 2 * RANK, WIDTH), lambda r, s: (0, 0, 0)),
        ],
        out_shape=[
            jax.ShapeDtypeStruct((tokens, WIDTH), F32),
            jax.ShapeDtypeStruct((2 * RANK, WIDTH), F32),
            jax.ShapeDtypeStruct((2, 2 * RANK, WIDTH), F32),
        ],
        scratch_shapes=[pltpu.VMEM((SEQ, 3 * WIDTH), BF)],
        compiler_params=params(2),
        name="attend_backward",
    )(do, dh, x, u, qkv, o, e, rinv, w, a, b)


def local(axes, tokens, lengths, attention, down, up, expand, project, gains, cotangent):
    layers = attention.shape[0]
    weights = []
    for l in range(layers):
        w = lax.all_gather(attention[l], axes, axis=0, tiled=True)
        w1 = lax.all_gather(expand[l], axes[1], axis=0)
        w2 = lax.all_gather(project[l], axes[1], axis=0)
        if w1.shape[0] != 4:
            w1 = w1.transpose(1, 0, 2).reshape(WIDTH, 4, CHUNK).transpose(1, 0, 2)
            w2 = w2.reshape(4, CHUNK, WIDTH)
        a = jnp.concatenate([down[l, 0], down[l, 1]], axis=1)
        twice = up[l] + up[l]
        zero = jnp.zeros_like(up[l, 0])
        b = jnp.stack([jnp.concatenate([twice[0], zero], axis=0), jnp.concatenate([zero, twice[1]], axis=0)])
        weights.append((w, w1, w2, a, b, gains[l, 0:1], gains[l, 1:2]))
    x = tokens
    saved = []
    for l in range(layers):
        w, w1, w2, a, b, g1, g2 = weights[l]
        qkv, u, o, e, rinv, n1, r1 = attend_forward(lengths, x, w, a, b, g1)
        gd, x2, r2 = ffn_forward(n1, w1, w2, g2)
        saved.append((x, qkv, u, o, e, rinv, n1, r1, gd, x2, r2))
        x = x2
    dy = cotangent
    grads = [None] * layers
    for l in reversed(range(layers)):
        w, w1, w2, a, b, g1, g2 = weights[l]
        x_in, qkv, u, o, e, rinv, n1, r1, gd, x2, r2 = saved[l]
        dh, do = ffn_backward(dy, x2, r2, n1, r1, gd, w1, w2, w, g1, g2)
        dy, ga, gb = attend_backward(do, dh, x_in, u, qkv, o, e, rinv, w, a, b)
        grads[l] = jnp.concatenate([ga, gb[0, :RANK], gb[1, RANK:]], axis=0)
    total = lax.psum(jnp.stack(grads), axes)
    a_grad = total[:, :2 * RANK].reshape(layers, 2, RANK, WIDTH).transpose(0, 1, 3, 2)
    b_grad = total[:, 2 * RANK:].reshape(layers, 2, RANK, WIDTH)
    return x, dy, a_grad, b_grad


def solution(mesh):
    axes = tuple(mesh.axis_names)
    dp, tensor = axes
    placed = (
        P(axes, None), P(axes), P(None, axes, None), P(), P(),
        P(None, None, tensor), P(None, tensor, None), P(), P(axes, None),
    )
    return jax.shard_map(
        functools.partial(local, axes),
        mesh=mesh,
        in_specs=placed,
        out_specs=(P(axes, None), P(axes, None), P(), P()),
        check_vma=False,
    )
```

```python
import functools
import jax
import jax.numpy as jnp
from jax import lax
from jax.experimental import pallas as pl
from jax.experimental.pallas import tpu as pltpu
from jax.sharding import PartitionSpec as P

WIDTH = 768
HEADS = 12
HEAD_DIM = 64
SEQ = 512
RANK = 8
EPS = 1e-05
CHUNK = 768
BF = jnp.bfloat16
F32 = jnp.float32
VMEM_LIMIT = 60 * 1024 * 1024
EXP2_SCALE = 1.4426950408889634 * HEAD_DIM ** (-0.5)


def dot(a, b):
    return jnp.dot(a, b, preferred_element_type=F32)


def dot_nt(a, b):
    return lax.dot_general(a, b, (((1,), (1,)), ((), ())), preferred_element_type=F32)


def dot_tn(a, b):
    return lax.dot_general(a, b, (((0,), (0,)), ((), ())), preferred_element_type=F32)


def mean_rows(v):
    return jnp.sum(v, axis=-1, keepdims=True) * (1.0 / WIDTH)


def params(n, collective=None):
    more = {} if collective is None else {"collective_id": collective, "has_side_effects": True}
    return pltpu.CompilerParams(
        dimension_semantics=("arbitrary",) * n, vmem_limit_bytes=VMEM_LIMIT, **more
    )


MESH = pl.DeviceIdType.MESH
Z_SIZE = 4


class Place:
    def __init__(self, axes):
        dp, t = lax.axis_index(axes[0]), lax.axis_index(axes[1])
        self.dp, self.t = dp, t
        self.z, self.x = dp // 2, dp % 2
        self.y, self.core = t // 2, t % 2
        self.to_core = (dp, t + 1 - 2 * self.core)
        self.to_y = (dp, t + 2 - 4 * self.y)
        self.to_x = (dp + 1 - 2 * self.x, t)
        self.to_zpair = (dp + 2 - 4 * (self.z % 2), t)
        self.to_up = (dp + 2, t)
        self.to_down = (dp - 2, t)


def greet(place, line):
    barrier = pltpu.get_barrier_semaphore()
    for device in (place.to_core, place.to_y, place.to_x):
        pl.semaphore_signal(barrier, inc=1, device_id=device, device_id_type=MESH)
    if line:
        @pl.when(place.z < Z_SIZE - 1)
        def _():
            pl.semaphore_signal(barrier, inc=1, device_id=place.to_up, device_id_type=MESH)

        @pl.when(place.z > 0)
        def _():
            pl.semaphore_signal(barrier, inc=1, device_id=place.to_down, device_id_type=MESH)

        inner = (place.z > 0) & (place.z < Z_SIZE - 1)

        @pl.when(inner)
        def _():
            pl.semaphore_wait(barrier, 5)

        @pl.when(jnp.logical_not(inner))
        def _():
            pl.semaphore_wait(barrier, 4)
    else:
        pl.semaphore_signal(barrier, inc=1, device_id=place.to_zpair, device_id_type=MESH)
        pl.semaphore_wait(barrier, 4)


def remote(src, dst, send, recv, device):
    return pltpu.make_async_remote_copy(
        src_ref=src, dst_ref=dst, send_sem=send, recv_sem=recv, device_id=device, device_id_type=MESH
    )


SLICE = 128
FFN_SEMS = [
    pltpu.SemaphoreType.DMA((3, 4)),
    pltpu.SemaphoreType.DMA((12,)),
    pltpu.SemaphoreType.DMA((14,)),
    pltpu.SemaphoreType.DMA((14,)),
]
FFN_TICKS = 8


def ffn_gather(place, layer, w1, w2, out, sems, tick):
    send, recv, core_send, core_recv = sems
    g = place.x * 2 + place.z % 2
    gx, gz, gd = 3 - 2 * place.x - (1 - place.z % 2), 0, 3 - g
    gx = (1 - place.x) * 2 + place.z % 2
    gz = place.x * 2 + 1 - place.z % 2

    def spot(slot, s):
        return out.at[slot, s // 6, pl.ds(pl.multiple_of((s % 6) * SLICE, SLICE), SLICE)]

    def over_y(i):
        s = 3 * g + i if i < 3 else 3 * gd
        first = place.x == (0 if i < 3 else 1)
        for here, ref in ((first, w1), (jnp.logical_not(first), w2)):
            @pl.when(here)
            def _():
                src = ref.at[layer, pl.ds(pl.multiple_of((s % 6) * SLICE, SLICE), SLICE)]
                remote(src, spot(1, s), send.at[0, i], recv.at[s], place.to_y).start()

    def arrived(s):
        remote(spot(1, s), spot(1, s), send.at[0, 0], recv.at[s], place.to_y).wait_recv()

    def over(way, i, s):
        device = place.to_x if way == 1 else place.to_zpair
        remote(spot(1, s), spot(1, s), send.at[way, i], recv.at[s], device).start()

    def share(s):
        remote(spot(1, s), spot(2, s), core_send.at[s], core_recv.at[s], place.to_core).start()

    if tick == 0:
        for i in range(4):
            over_y(i)
        for m, ref in enumerate((w1, w2)):
            remote(ref.at[layer], out.at[0, m], core_send.at[12 + m], core_recv.at[12 + m], place.to_core).start()
    elif tick < 4:
        s = 3 * g + tick - 1
        arrived(s)
        over(1, tick - 1, s)
        over(2, tick - 1, s)
        share(s)
        if tick == 3:
            for s in (3 * gx, 3 * gz):
                arrived(s)
                share(s)
    elif tick == 4:
        s = 3 * gz + 1
        arrived(s)
        over(1, 3, s)
        share(s)
        for s in (3 * gd, 3 * gx + 1):
            arrived(s)
            share(s)
    elif tick == 5:
        s = 3 * gx + 2
        arrived(s)
        over(2, 3, s)
        share(s)
        s = 3 * gz + 2
        arrived(s)
        share(s)
    elif tick == 6:
        for s in (3 * gd + 1, 3 * gd + 2):
            arrived(s)
            share(s)
    else:
        for s in range(12):
            remote(spot(1, s), spot(2, s), core_send.at[s], core_recv.at[s], place.to_core).wait()
        for m, ref in enumerate((w1, w2)):
            remote(ref.at[layer], out.at[0, m], core_send.at[12 + m], core_recv.at[12 + m], place.to_core).wait()
        for way in range(3):
            for i in range(4):
                remote(spot(1, 0), spot(1, 0), send.at[way, i], recv.at[0], place.to_y).wait_send()


ATT_SEMS = [
    pltpu.SemaphoreType.DMA((2, 4)),
    pltpu.SemaphoreType.DMA((4,)),
    pltpu.SemaphoreType.DMA((2, 4)),
    pltpu.SemaphoreType.DMA((2, 4)),
    pltpu.SemaphoreType.DMA((2, 4)),
    pltpu.SemaphoreType.DMA((2, 4)),
    pltpu.SemaphoreType.DMA((5, 4)),
    pltpu.SemaphoreType.DMA((5, 4)),
    pltpu.SemaphoreType.DMA,
]
ATT_TICKS = 7


def attention_gather(place, layer, block, out, sems, tick):
    z_send, z_recv, n_send, n_recv, h_send, h_recv, c_send, c_recv, own_sem = sems
    rows = block.shape[1]
    half = rows // 2
    z, x, y, core = place.z, place.x, place.y, place.core

    def spot(sz, sx, sy, sc, start=0, size=rows):
        at = ((sz * 2 + sx) * 4 + sy * 2 + sc) * rows + start
        return out.at[pl.ds(pl.multiple_of(at, 16), size)]

    def line(sz):
        return spot(sz, x, y, core)

    def side(way, sz):
        return spot(sz, 1 - x, y, core) if way == 0 else spot(sz, x, 1 - y, core)

    def far(way, sz):
        return spot(sz, 1 - x, 1 - y, core, way * half, half)

    devices = (place.to_x, place.to_y)

    def at_distance(d, action):
        if d == 0:
            action(z)
            return
        @pl.when(z >= d)
        def _():
            action(z - d)

        @pl.when(z + d < Z_SIZE)
        def _():
            action(z + d)

    def line_step(sz, own):
        mine = block.at[layer] if own else line(sz)
        if not own:
            remote(line(sz), line(sz), z_send.at[0, sz], z_recv.at[sz], place.to_core).wait_recv()

        @pl.when((sz <= z) & (z < Z_SIZE - 1))
        def _():
            remote(mine, line(sz), z_send.at[0, sz], z_recv.at[sz], place.to_up).start()

        @pl.when((sz >= z) & (z > 0))
        def _():
            remote(mine, line(sz), z_send.at[1, sz], z_recv.at[sz], place.to_down).start()

        for way in range(2):
            remote(mine, line(sz), n_send.at[way, sz], n_recv.at[way, sz], devices[way]).start()
        remote(mine, line(sz), c_send.at[0, sz], c_recv.at[0, sz], place.to_core).start()

    def side_step(sz):
        for way in range(2):
            remote(side(way, sz), side(way, sz), n_send.at[way, sz], n_recv.at[way, sz], devices[way]).wait_recv()
            at = spot(sz, 1 - x, y, core, 0, half) if way == 0 else spot(sz, x, 1 - y, core, half, half)
            remote(at, at, h_send.at[way, sz], h_recv.at[way, sz], devices[1 - way]).start()
            remote(side(way, sz), side(way, sz), c_send.at[1 + way, sz], c_recv.at[1 + way, sz], place.to_core).start()

    def far_step(sz):
        for way in range(2):
            remote(far(way, sz), far(way, sz), h_send.at[way, sz], h_recv.at[way, sz], place.to_core).wait_recv()
            remote(far(way, sz), far(way, sz), c_send.at[3 + way, sz], c_recv.at[3 + way, sz], place.to_core).start()

    if tick == 0:
        pltpu.make_async_copy(block.at[layer], line(z), own_sem).start()
    if tick < 4:
        at_distance(tick, functools.partial(line_step, own=tick == 0))
    if 1 <= tick < 5:
        at_distance(tick - 1, side_step)
    if 2 <= tick < 6:
        at_distance(tick - 2, far_step)
    if tick == 6:
        pltpu.make_async_copy(block.at[layer], line(z), own_sem).wait()
        for sz in range(Z_SIZE):
            @pl.when((sz <= z) & (z < Z_SIZE - 1))
            def _():
                remote(line(sz), line(sz), z_send.at[0, sz], z_recv.at[sz], place.to_core).wait_send()

            @pl.when((sz >= z) & (z > 0))
            def _():
                remote(line(sz), line(sz), z_send.at[1, sz], z_recv.at[sz], place.to_core).wait_send()

            for way in range(2):
                remote(line(sz), line(sz), n_send.at[way, sz], n_recv.at[way, sz], place.to_core).wait_send()
                remote(far(way, sz), far(way, sz), h_send.at[way, sz], h_recv.at[way, sz], place.to_core).wait_send()
            parts = (
                (line(sz), spot(sz, x, y, 1 - core)),
                (side(0, sz), spot(sz, 1 - x, y, 1 - core)),
                (side(1, sz), spot(sz, x, 1 - y, 1 - core)),
                (far(0, sz), spot(sz, 1 - x, 1 - y, 1 - core, 0, half)),
                (far(1, sz), spot(sz, 1 - x, 1 - y, 1 - core, half, half)),
            )
            for i, (mine, theirs) in enumerate(parts):
                remote(mine, theirs, c_send.at[i, sz], c_recv.at[i, sz], place.to_core).wait()


def gather_attention_alone(axes, attention, layer, collective):
    count = attention.shape[1]

    def kernel(block, out, *sems):
        place = Place(axes)
        greet(place, True)
        for tick in range(ATT_TICKS):
            attention_gather(place, layer, block, out, sems, tick)

    return pl.pallas_call(
        kernel,
        in_specs=[pl.BlockSpec(memory_space=pl.ANY)],
        out_specs=pl.BlockSpec(memory_space=pl.ANY),
        out_shape=jax.ShapeDtypeStruct((32 * count, WIDTH), BF),
        scratch_shapes=ATT_SEMS,
        compiler_params=pltpu.CompilerParams(collective_id=collective, has_side_effects=True),
        name="gather_attention",
    )(attention)


def gather_ffn_alone(axes, w1, w2, layer, collective):
    def kernel(w1, w2, out, *sems):
        place = Place(axes)
        greet(place, False)
        for tick in range(FFN_TICKS):
            ffn_gather(place, layer, w1, w2, out, sems, tick)

    return pl.pallas_call(
        kernel,
        in_specs=[pl.BlockSpec(memory_space=pl.ANY)] * 2,
        out_specs=pl.BlockSpec(memory_space=pl.ANY),
        out_shape=jax.ShapeDtypeStruct((3, 2, WIDTH, CHUNK), BF),
        scratch_shapes=FFN_SEMS,
        compiler_params=pltpu.CompilerParams(collective_id=collective, has_side_effects=True),
        name="gather_ffn",
    )(w1, w2)


def all_sum(axes, values, collective):
    parts, high, wide = values.shape

    def kernel(v_ref, out_ref, box, send, recv, send2, recv2):
        place = Place(axes)
        me = place.dp * 4 + place.t
        barrier = pltpu.get_barrier_semaphore()

        def peer(i):
            other = lax.rem(me + i, parts)
            return other, (other // 4, other % 4)

        def signal(i, _):
            pl.semaphore_signal(barrier, inc=1, device_id=peer(i)[1], device_id_type=MESH)
            return 0

        lax.fori_loop(1, parts, signal, 0)
        pl.semaphore_wait(barrier, parts - 1)

        def first(i, act):
            other, device = peer(i)
            act(remote(v_ref.at[other], box.at[i], send.at[i], recv.at[i], device))
            return 0

        lax.fori_loop(1, parts, lambda i, _: first(i, lambda c: c.start()), 0)
        lax.fori_loop(1, parts, lambda i, _: first(i, lambda c: c.wait()), 0)
        out_ref[me] = v_ref[me] + jnp.sum(box[1:], axis=0)

        def second(i, act):
            other, device = peer(i)
            act(remote(out_ref.at[me], out_ref.at[me], send2.at[i], recv2.at[i], device))
            return 0

        lax.fori_loop(1, parts, lambda i, _: second(i, lambda c: c.start()), 0)

        def finish(i, _):
            other = lax.rem(me + parts - i, parts)
            c = remote(out_ref.at[me], out_ref.at[other], send2.at[i], recv2.at[i], peer(i)[1])
            c.wait()
            return 0

        lax.fori_loop(1, parts, finish, 0)

    sem = pltpu.SemaphoreType.DMA((parts,))
    return pl.pallas_call(
        kernel,
        in_specs=[pl.BlockSpec(memory_space=pltpu.VMEM)],
        out_specs=pl.BlockSpec(memory_space=pltpu.VMEM),
        out_shape=jax.ShapeDtypeStruct(values.shape, F32),
        scratch_shapes=[pltpu.VMEM(values.shape, F32), sem, sem, sem, sem],
        compiler_params=pltpu.CompilerParams(collective_id=collective, has_side_effects=True),
        name="all_sum",
    )(values)


GROUP = 4


def attend_kernel(axes, layer, len_ref, x_ref, w_ref, a_ref, b_ref, g_ref, *refs):
    row, grp = pl.program_id(0), pl.program_id(1)
    step = row * pl.num_programs(1) + grp
    place = None
    if axes is None:
        qkv_ref, u_ref, o_ref, e_ref, rinv_ref, n1_ref, r1_ref, bound_ref = refs
    else:
        w1, w2, qkv_ref, u_ref, o_ref, e_ref, rinv_ref, n1_ref, r1_ref, out, bound_ref, *sems = refs
        place = Place(axes)
        for tick in range(FFN_TICKS - 2):
            @pl.when(step == tick)
            def _():
                if tick == 0:
                    greet(place, False)
                ffn_gather(place, layer, w1, w2, out, sems, tick)

    @pl.when(grp == 0)
    def _():
        x = x_ref[...]
        u = dot(x, a_ref[...]).astype(BF)
        u_ref[...] = u
        for i in range(3):
            acc = dot(x, w_ref[WIDTH * i:WIDTH * (i + 1), :])
            if i != 1:
                acc += dot(u, b_ref[i // 2])
            qkv_ref[:, WIDTH * i:WIDTH * (i + 1)] = acc.astype(BF)
        key = lax.broadcasted_iota(jnp.int32, (SEQ, 128), 0)
        bound_ref[...] = jnp.where(key < len_ref[row], 3.0e38, -8.0e9)

    lane = lax.broadcasted_iota(jnp.int32, (SEQ, 128), 1)
    low = lane < HEAD_DIM
    bound = bound_ref[...]
    bound = jnp.concatenate([bound] * 4, axis=1)
    for pair in range(GROUP // 2):
        at = pl.multiple_of(grp * (GROUP * HEAD_DIM) + pair * 128, 128)
        q = qkv_ref[:, pl.ds(at, 128)]
        k = qkv_ref[:, pl.ds(WIDTH + at, 128)]
        v = qkv_ref[:, pl.ds(2 * WIDTH + at, 128)]
        outs = []
        for half in range(2):
            mine = low if half == 0 else ~low
            qh = jnp.where(mine, q, jnp.zeros_like(q))
            vh = jnp.where(mine, v, jnp.ones_like(v))
            s = jnp.minimum(dot_nt(k, qh), bound)
            top = jnp.max(s, axis=0, keepdims=True)
            e = jnp.exp2((s - top) * EXP2_SCALE).astype(BF)
            e_ref[0, pair * 2 + half] = e
            ot = dot_tn(vh, e)
            if half == 0:
                o_t, l = ot[:HEAD_DIM], ot[HEAD_DIM:HEAD_DIM + 8]
            else:
                o_t, l = ot[HEAD_DIM:], ot[0:8]
            r = 1.0 / l
            rinv_ref[0, grp * GROUP + pair * 2 + half] = r
            outs.append(o_t * r[0:1])
        both = jnp.concatenate(outs, axis=0)
        o_ref[:, pl.ds(at, 128)] = both.T.astype(BF)

    @pl.when(grp == pl.num_programs(1) - 1)
    def _():
        h = x_ref[...].astype(F32) + dot(o_ref[...], w_ref[3 * WIDTH:, :])
        c = h - mean_rows(h)
        r = lax.rsqrt(mean_rows(c * c) + EPS)
        n1_ref[...] = (c * r * g_ref[...]).astype(BF)
        r1_ref[...] = jnp.broadcast_to(r, (SEQ, 128))

    if axes is not None:
        @pl.when(step == FFN_TICKS - 3)
        def _():
            for tick in range(FFN_TICKS - 2, FFN_TICKS):
                ffn_gather(place, layer, w1, w2, out, sems, tick)


def attend_forward(lengths, x, w, a, b, g, axes=None, layer=0, mine=(), collective=None):
    rows = lengths.shape[0]
    anywhere = pl.BlockSpec(memory_space=pl.ANY)
    tokens = rows * SEQ
    steps = HEADS // GROUP
    row_block = lambda width: pl.BlockSpec((SEQ, width), lambda r, s: (r, 0))
    whole = lambda *shape: pl.BlockSpec(shape, lambda r, s: (0,) * len(shape), pipeline_mode=pl.Buffered(1))
    gathered = [jax.ShapeDtypeStruct((3, 2, WIDTH, CHUNK), BF)] if mine else []
    return pl.pallas_call(
        functools.partial(attend_kernel, axes, layer),
        grid=(rows, steps),
        in_specs=[
            pl.BlockSpec(memory_space=pltpu.SMEM),
            row_block(WIDTH), whole(4 * WIDTH, WIDTH), whole(WIDTH, 2 * RANK),
            whole(2, 2 * RANK, WIDTH), whole(1, WIDTH),
        ] + [anywhere] * len(mine),
        out_specs=[
            row_block(3 * WIDTH), row_block(2 * RANK), row_block(WIDTH),
            pl.BlockSpec((1, GROUP, SEQ, SEQ), lambda r, s: (r, s, 0, 0)),
            pl.BlockSpec((1, HEADS, 8, SEQ), lambda r, s: (r, 0, 0, 0)),
            row_block(WIDTH), row_block(128),
        ] + [anywhere] * len(gathered),
        out_shape=[
            jax.ShapeDtypeStruct((tokens, 3 * WIDTH), BF),
            jax.ShapeDtypeStruct((tokens, 2 * RANK), BF),
            jax.ShapeDtypeStruct((tokens, WIDTH), BF),
            jax.ShapeDtypeStruct((rows, HEADS, SEQ, SEQ), BF),
            jax.ShapeDtypeStruct((rows, HEADS, 8, SEQ), F32),
            jax.ShapeDtypeStruct((tokens, WIDTH), BF),
            jax.ShapeDtypeStruct((tokens, 128), F32),
        ] + gathered,
        scratch_shapes=[pltpu.VMEM((SEQ, 128), F32)] + (FFN_SEMS if mine else []),
        compiler_params=params(2, collective),
        name="attend_forward",
    )(lengths, x, w, a, b, g, *mine)


BLOCK = 256

def normal_parts(z):
    d = jnp.exp2(z * z * (-0.5 * 1.4426950408889634))
    t = 1.0 / (1.0 + jnp.abs(z) * (0.3275911 * 0.7071067811865476))
    q = t * (0.5 * 0.254829592 + t * (0.5 * -0.284496736 + t * (0.5 * 1.421413741
             + t * (0.5 * -1.453152027 + t * (0.5 * 1.061405429)))))
    tail = q * d
    cdf = jnp.where(z < 0, tail, 1.0 - tail)
    return cdf, d * 0.3989422804014327


def ffn_kernel(axes, layer, n1_ref, w1_ref, w2_ref, more_ref, g_ref, *refs):
    step = pl.program_id(0)
    if axes is None:
        gd_ref, x2_ref, r2_ref = refs
    else:
        block, gd_ref, x2_ref, r2_ref, out, *sems = refs
        place = Place(axes)

    def transfer(slot):
        if axes is None:
            return
        for tick in range(slot, ATT_TICKS - 1, 2):
            @pl.when(step == tick // 2)
            def _():
                if tick == 0:
                    greet(place, True)
                attention_gather(place, layer, block, out, sems, tick)

    transfer(0)
    n1 = n1_ref[...]
    f = n1.astype(F32)
    for j in range(4):
        if j == 2:
            transfer(1)
        z = dot(n1, w1_ref[0] if j == 0 else more_ref[j - 1, 0])
        cdf, pdf = normal_parts(z)
        gd_ref[:, CHUNK * j:CHUNK * (j + 1)] = (cdf + z * pdf).astype(BF)
        f = f + dot((z * cdf).astype(BF), w2_ref[0] if j == 0 else more_ref[j - 1, 1])
    c = f - mean_rows(f)
    r = lax.rsqrt(mean_rows(c * c) + EPS)
    x2_ref[...] = (c * r * g_ref[...]).astype(BF)
    r2_ref[...] = jnp.broadcast_to(r, (BLOCK, 128))
    if axes is not None:
        @pl.when(step == pl.num_programs(0) - 1)
        def _():
            attention_gather(place, layer, block, out, sems, ATT_TICKS - 1)


def ffn_forward(n1, w1, w2, more, at, g, axes=None, layer=0, mine=(), collective=None):
    tokens = n1.shape[0]
    anywhere = pl.BlockSpec(memory_space=pl.ANY)
    block = lambda width: pl.BlockSpec((BLOCK, width), lambda s: (s, 0))
    whole = lambda *shape: pl.BlockSpec(shape, lambda s: (0,) * len(shape), pipeline_mode=pl.Buffered(1))
    own = pl.BlockSpec((1, WIDTH, CHUNK), lambda s: (at, 0, 0), pipeline_mode=pl.Buffered(1))
    gathered = [jax.ShapeDtypeStruct((4 * WIDTH, WIDTH), BF)] if mine else []
    return pl.pallas_call(
        functools.partial(ffn_kernel, axes, layer),
        grid=(tokens // BLOCK,),
        in_specs=[block(WIDTH), own, own, whole(3, 2, WIDTH, CHUNK), whole(1, WIDTH)] + [anywhere] * len(mine),
        out_specs=[block(4 * CHUNK), block(WIDTH), block(128)] + [anywhere] * len(gathered),
        out_shape=[
            jax.ShapeDtypeStruct((tokens, 4 * CHUNK), BF),
            jax.ShapeDtypeStruct((tokens, WIDTH), BF),
            jax.ShapeDtypeStruct((tokens, 128), F32),
        ] + gathered,
        scratch_shapes=ATT_SEMS if mine else [],
        compiler_params=params(1, collective),
        name="ffn_forward",
    )(n1, w1, w2, more, g, *mine)


def norm_back(e, m, r):
    return r * (e - mean_rows(e) - m * mean_rows(e * m))


def ffn_back_kernel(dy_ref, x2_ref, r2_ref, n1_ref, r1_ref, gd_ref, w1_ref, w2_ref, more_ref, wo_ref,
                    g1_ref, g2_ref, dh_ref, do_ref):
    g2, g1 = g2_ref[...], g1_ref[...]
    dh2 = norm_back(dy_ref[...].astype(F32) * g2, x2_ref[...].astype(F32) * (1.0 / g2), r2_ref[:, 0:1])
    df = dh2.astype(BF)
    dn = dh2
    for j in range(4):
        dz = (dot_nt(df, w2_ref[0] if j == 0 else more_ref[j - 1, 1]) * gd_ref[:, CHUNK * j:CHUNK * (j + 1)].astype(F32)).astype(BF)
        dn = dn + dot_nt(dz, w1_ref[0] if j == 0 else more_ref[j - 1, 0])
    dh = norm_back(dn * g1, n1_ref[...].astype(F32) * (1.0 / g1), r1_ref[:, 0:1])
    dh_ref[...] = dh
    do_ref[...] = dot_nt(dh.astype(BF), wo_ref[...]).astype(BF)


def ffn_backward(dy, x2, r2, n1, r1, gd, w1, w2, more, at, w, g1, g2):
    tokens = n1.shape[0]
    block = lambda width: pl.BlockSpec((BLOCK, width), lambda s: (s, 0))
    whole = lambda *shape: pl.BlockSpec(shape, lambda s: (0,) * len(shape), pipeline_mode=pl.Buffered(1))
    own = pl.BlockSpec((1, WIDTH, CHUNK), lambda s: (at, 0, 0), pipeline_mode=pl.Buffered(1))
    return pl.pallas_call(
        ffn_back_kernel,
        grid=(tokens // BLOCK,),
        in_specs=[block(WIDTH), block(WIDTH), block(128), block(WIDTH), block(128), block(4 * CHUNK),
                  own, own, whole(3, 2, WIDTH, CHUNK),
                  pl.BlockSpec((WIDTH, WIDTH), lambda s: (3, 0), pipeline_mode=pl.Buffered(1)),
                  whole(1, WIDTH), whole(1, WIDTH)],
        out_specs=[block(WIDTH), block(WIDTH)],
        out_shape=[jax.ShapeDtypeStruct((tokens, WIDTH), F32), jax.ShapeDtypeStruct((tokens, WIDTH), BF)],
        compiler_params=params(1),
        name="ffn_backward",
    )(dy, x2, r2, n1, r1, gd, w1, w2, more, w, g1, g2)


def attend_back_kernel(do_ref, dh_ref, x_ref, u_ref, qkv_ref, o_ref, e_ref, rinv_ref, w_ref, a_ref, b_ref,
                       dx_ref, ga_ref, gb_ref, d_ref):
    row, grp = pl.program_id(0), pl.program_id(1)
    lane = lax.broadcasted_iota(jnp.int32, (SEQ, 128), 1)
    low = lane < HEAD_DIM
    for pair in range(GROUP // 2):
        at = pl.multiple_of(grp * (GROUP * HEAD_DIM) + pair * 128, 128)
        q = qkv_ref[:, pl.ds(at, 128)]
        k = qkv_ref[:, pl.ds(WIDTH + at, 128)]
        v = qkv_ref[:, pl.ds(2 * WIDTH + at, 128)]
        head = grp * GROUP + pair * 2
        scale = jnp.concatenate([rinv_ref[0, head]] * 8 + [rinv_ref[0, head + 1]] * 8, axis=0).T
        dos = do_ref[:, pl.ds(at, 128)].astype(F32) * scale
        other = pltpu.roll(-dos * o_ref[:, pl.ds(at, 128)].astype(F32), HEAD_DIM, 1).astype(BF)
        dos = dos.astype(BF)
        dvs, dks, dqs = [], [], []
        for half in range(2):
            mine = low if half == 0 else ~low
            e = e_ref[0, pair * 2 + half]
            dp = dot_nt(jnp.where(mine, v, jnp.ones_like(v)), jnp.where(mine, dos, other))
            ds = (dp * e.astype(F32)).astype(BF)
            dvs.append(dot(e, dos))
            dks.append(dot(ds, q))
            dqs.append(dot_tn(k, ds)[half * HEAD_DIM:(half + 1) * HEAD_DIM])
        d_ref[:, pl.ds(2 * WIDTH + at, 128)] = jnp.where(low, dvs[0], dvs[1]).astype(BF)
        d_ref[:, pl.ds(WIDTH + at, 128)] = (jnp.where(low, dks[0], dks[1]) * HEAD_DIM ** (-0.5)).astype(BF)
        d_ref[:, pl.ds(at, 128)] = (jnp.concatenate(dqs, axis=0) * HEAD_DIM ** (-0.5)).T.astype(BF)

    @pl.when((row == 0) & (grp == 0))
    def _():
        ga_ref[...] = jnp.zeros_like(ga_ref)
        gb_ref[...] = jnp.zeros_like(gb_ref)

    @pl.when(grp == pl.num_programs(1) - 1)
    def _():
        dq, dk, dv = (d_ref[:, WIDTH * i:WIDTH * (i + 1)] for i in range(3))
        du = (dot_nt(dq, b_ref[0]) + dot_nt(dv, b_ref[1])).astype(BF)
        ga_ref[...] += dot_tn(du, x_ref[...])
        u = u_ref[...]
        u2 = u + u
        gb_ref[0] += dot_tn(u2, dq)
        gb_ref[1] += dot_tn(u2, dv)
        dx_ref[...] = (dh_ref[...] + dot_nt(dq, w_ref[0:WIDTH]) + dot_nt(dk, w_ref[WIDTH:2 * WIDTH])
                       + dot_nt(dv, w_ref[2 * WIDTH:3 * WIDTH]) + dot_nt(du, a_ref[...]))


def attend_backward(do, dh, x, u, qkv, o, e, rinv, w, a, b):
    rows = e.shape[0]
    tokens = rows * SEQ
    row_block = lambda width: pl.BlockSpec((SEQ, width), lambda r, s: (r, 0))
    whole = lambda *shape: pl.BlockSpec(shape, lambda r, s: (0,) * len(shape), pipeline_mode=pl.Buffered(1))
    return pl.pallas_call(
        attend_back_kernel,
        grid=(rows, HEADS // GROUP),
        in_specs=[
            row_block(WIDTH), row_block(WIDTH), row_block(WIDTH), row_block(2 * RANK), row_block(3 * WIDTH),
            row_block(WIDTH),
            pl.BlockSpec((1, GROUP, SEQ, SEQ), lambda r, s: (r, s, 0, 0)),
            pl.BlockSpec((1, HEADS, 8, SEQ), lambda r, s: (r, 0, 0, 0)),
            whole(3 * WIDTH, WIDTH), whole(WIDTH, 2 * RANK), whole(2, 2 * RANK, WIDTH),
        ],
        out_specs=[
            row_block(WIDTH),
            pl.BlockSpec((2 * RANK, WIDTH), lambda r, s: (0, 0)),
            pl.BlockSpec((2, 2 * RANK, WIDTH), lambda r, s: (0, 0, 0)),
        ],
        out_shape=[
            jax.ShapeDtypeStruct((tokens, WIDTH), F32),
            jax.ShapeDtypeStruct((2 * RANK, WIDTH), F32),
            jax.ShapeDtypeStruct((2, 2 * RANK, WIDTH), F32),
        ],
        scratch_shapes=[pltpu.VMEM((SEQ, 3 * WIDTH), BF)],
        compiler_params=params(2),
        name="attend_backward",
    )(do, dh, x, u, qkv, o, e, rinv, w, a, b)


def local(axes, direct, tokens, lengths, attention, down, up, expand, project, gains, cotangent):
    layers = attention.shape[0]
    adapters = []
    for l in range(layers):
        a = jnp.concatenate([down[l, 0], down[l, 1]], axis=1)
        twice = up[l] + up[l]
        zero = jnp.zeros_like(up[l, 0])
        b = jnp.stack([jnp.concatenate([twice[0], zero], axis=0), jnp.concatenate([zero, twice[1]], axis=0)])
        adapters.append((a, b, gains[l, 0:1], gains[l, 1:2]))
    weights, attn = [], []
    if direct:
        attn.append(gather_attention_alone(axes, attention, 0, 0))
    else:
        for l in range(layers):
            attn.append(lax.all_gather(attention[l], axes, axis=0, tiled=True))
            w1 = lax.all_gather(expand[l], axes[1], axis=1, tiled=True)
            w1 = w1.reshape(WIDTH, 4, CHUNK).transpose(1, 0, 2)
            w2 = lax.all_gather(project[l], axes[1], axis=0, tiled=True).reshape(4, CHUNK, WIDTH)
            weights.append((w1, w2, jnp.stack([w1[1:], w2[1:]], axis=1), 0))
    x = tokens
    saved = []
    for l in range(layers):
        a, b, g1, g2 = adapters[l]
        more = {}
        if direct:
            more = dict(axes=axes, layer=l, mine=(expand, project), collective=1 + 2 * l)
        qkv, u, o, e, rinv, n1, r1, *rest = attend_forward(lengths, x, attn[l], a, b, g1, **more)
        more = {}
        if direct:
            weights.append((expand, project, rest[0], l))
            if l + 1 < layers:
                more = dict(axes=axes, layer=l + 1, mine=(attention,), collective=2 + 2 * l)
        gd, x2, r2, *rest = ffn_forward(n1, *weights[l], g2, **more)
        attn += rest
        saved.append((x, qkv, u, o, e, rinv, n1, r1, gd, x2, r2))
        x = x2
    dy = cotangent
    grads = [None] * layers
    for l in reversed(range(layers)):
        a, b, g1, g2 = adapters[l]
        x_in, qkv, u, o, e, rinv, n1, r1, gd, x2, r2 = saved[l]
        dh, do = ffn_backward(dy, x2, r2, n1, r1, gd, *weights[l], attn[l], g1, g2)
        dy, ga, gb = attend_backward(do, dh, x_in, u, qkv, o, e, rinv, attn[l], a, b)
        grads[l] = jnp.concatenate([ga, gb[0, :RANK], gb[1, RANK:]], axis=0)
    total = jnp.stack(grads)
    if direct:
        total = all_sum(axes, total.reshape(32, -1, 128), 9).reshape(total.shape)
    else:
        total = lax.psum(total, axes)
    a_grad = total[:, :2 * RANK].reshape(layers, 2, RANK, WIDTH).transpose(0, 1, 3, 2)
    b_grad = total[:, 2 * RANK:].reshape(layers, 2, RANK, WIDTH)
    return x, dy, a_grad, b_grad


def solution(mesh):
    axes = tuple(mesh.axis_names)
    dp, tensor = axes
    direct = mesh.shape[dp] == 2 * Z_SIZE and mesh.shape[tensor] == 4
    placed = (
        P(axes, None), P(axes), P(None, axes, None), P(), P(),
        P(None, None, tensor), P(None, tensor, None), P(), P(axes, None),
    )
    return jax.shard_map(
        functools.partial(local, axes, direct),
        mesh=mesh,
        in_specs=placed,
        out_specs=(P(axes, None), P(axes, None), P(), P()),
        check_vma=False,
    )
```

```python
import functools
import jax
import jax.numpy as jnp
from jax import lax
from jax.experimental import pallas as pl
from jax.experimental.pallas import tpu as pltpu
from jax.sharding import PartitionSpec as P

WIDTH = 768
HEADS = 12
HEAD_DIM = 64
SEQ = 512
RANK = 8
EPS = 1e-05
CHUNK = 768
BF = jnp.bfloat16
F32 = jnp.float32
VMEM_LIMIT = 60 * 1024 * 1024
EXP2_SCALE = 1.4426950408889634 * HEAD_DIM ** (-0.5)


def dot(a, b):
    return jnp.dot(a, b, preferred_element_type=F32)


def dot_nt(a, b):
    return lax.dot_general(a, b, (((1,), (1,)), ((), ())), preferred_element_type=F32)


def dot_tn(a, b):
    return lax.dot_general(a, b, (((0,), (0,)), ((), ())), preferred_element_type=F32)


def mean_rows(v):
    return jnp.sum(v, axis=-1, keepdims=True) * (1.0 / WIDTH)


def params(n, collective=None):
    more = {} if collective is None else {"collective_id": collective, "has_side_effects": True}
    return pltpu.CompilerParams(
        dimension_semantics=("arbitrary",) * n, vmem_limit_bytes=VMEM_LIMIT, **more
    )


MESH = pl.DeviceIdType.MESH
Z_SIZE = 4


class Place:
    def __init__(self, axes):
        dp, t = lax.axis_index(axes[0]), lax.axis_index(axes[1])
        self.dp, self.t = dp, t
        self.z, self.x = dp // 2, dp % 2
        self.y, self.core = t // 2, t % 2
        self.to_core = (dp, t + 1 - 2 * self.core)
        self.to_y = (dp, t + 2 - 4 * self.y)
        self.to_x = (dp + 1 - 2 * self.x, t)
        self.to_zpair = (dp + 2 - 4 * (self.z % 2), t)
        self.to_up = (dp + 2, t)
        self.to_down = (dp - 2, t)


def greet(place, line):
    barrier = pltpu.get_barrier_semaphore()
    for device in (place.to_core, place.to_y, place.to_x):
        pl.semaphore_signal(barrier, inc=1, device_id=device, device_id_type=MESH)
    if line:
        @pl.when(place.z < Z_SIZE - 1)
        def _():
            pl.semaphore_signal(barrier, inc=1, device_id=place.to_up, device_id_type=MESH)

        @pl.when(place.z > 0)
        def _():
            pl.semaphore_signal(barrier, inc=1, device_id=place.to_down, device_id_type=MESH)

        inner = (place.z > 0) & (place.z < Z_SIZE - 1)

        @pl.when(inner)
        def _():
            pl.semaphore_wait(barrier, 5)

        @pl.when(jnp.logical_not(inner))
        def _():
            pl.semaphore_wait(barrier, 4)
    else:
        pl.semaphore_signal(barrier, inc=1, device_id=place.to_zpair, device_id_type=MESH)
        pl.semaphore_wait(barrier, 4)


def remote(src, dst, send, recv, device):
    return pltpu.make_async_remote_copy(
        src_ref=src, dst_ref=dst, send_sem=send, recv_sem=recv, device_id=device, device_id_type=MESH
    )


SLICE = 128
FFN_SEMS = [
    pltpu.SemaphoreType.DMA((3, 4)),
    pltpu.SemaphoreType.DMA((12,)),
    pltpu.SemaphoreType.DMA((14,)),
    pltpu.SemaphoreType.DMA((14,)),
]
FFN_TICKS = 8


def ffn_gather(place, layer, w1, w2, out, sems, tick):
    send, recv, core_send, core_recv = sems
    g = place.x * 2 + place.z % 2
    gd = 3 - g
    gx = (1 - place.x) * 2 + place.z % 2
    gz = place.x * 2 + 1 - place.z % 2

    def spot(slot, s):
        return out.at[slot + 1, s // 6, pl.ds(pl.multiple_of((s % 6) * SLICE, SLICE), SLICE)]

    def over_y(i):
        s = 3 * g + i if i < 3 else 3 * gd
        first = place.x == (0 if i < 3 else 1)
        for here, ref in ((first, w1), (jnp.logical_not(first), w2)):
            @pl.when(here)
            def _():
                src = ref.at[layer, pl.ds(pl.multiple_of((s % 6) * SLICE, SLICE), SLICE)]
                remote(src, spot(1, s), send.at[0, i], recv.at[s], place.to_y).start()

    def arrived(s):
        remote(spot(1, s), spot(1, s), send.at[0, 0], recv.at[s], place.to_y).wait_recv()

    def over(way, i, s):
        device = place.to_x if way == 1 else place.to_zpair
        remote(spot(1, s), spot(1, s), send.at[way, i], recv.at[s], device).start()

    def share(s):
        remote(spot(1, s), spot(2, s), core_send.at[s], core_recv.at[s], place.to_core).start()

    if tick == 0:
        for i in range(4):
            over_y(i)
        for m, ref in enumerate((w1, w2)):
            remote(ref.at[layer], out.at[1, m], core_send.at[12 + m], core_recv.at[12 + m], place.to_core).start()
    elif tick < 4:
        s = 3 * g + tick - 1
        arrived(s)
        over(1, tick - 1, s)
        over(2, tick - 1, s)
        share(s)
        if tick == 3:
            for s in (3 * gx, 3 * gz):
                arrived(s)
                share(s)
    elif tick == 4:
        s = 3 * gz + 1
        arrived(s)
        over(1, 3, s)
        share(s)
        for s in (3 * gd, 3 * gx + 1):
            arrived(s)
            share(s)
    elif tick == 5:
        s = 3 * gx + 2
        arrived(s)
        over(2, 3, s)
        share(s)
        s = 3 * gz + 2
        arrived(s)
        share(s)
    elif tick == 6:
        for s in (3 * gd + 1, 3 * gd + 2):
            arrived(s)
            share(s)
    else:
        for s in range(12):
            remote(spot(1, s), spot(2, s), core_send.at[s], core_recv.at[s], place.to_core).wait()
        for m, ref in enumerate((w1, w2)):
            remote(ref.at[layer], out.at[1, m], core_send.at[12 + m], core_recv.at[12 + m], place.to_core).wait()
        for way in range(3):
            for i in range(4):
                remote(spot(1, 0), spot(1, 0), send.at[way, i], recv.at[0], place.to_y).wait_send()


ATT_SEMS = [
    pltpu.SemaphoreType.DMA((2, 4)),
    pltpu.SemaphoreType.DMA((4,)),
    pltpu.SemaphoreType.DMA((2, 4)),
    pltpu.SemaphoreType.DMA((2, 4)),
    pltpu.SemaphoreType.DMA((2, 4)),
    pltpu.SemaphoreType.DMA((2, 4)),
    pltpu.SemaphoreType.DMA((5, 4)),
    pltpu.SemaphoreType.DMA((5, 4)),
    pltpu.SemaphoreType.DMA,
]
ATT_TICKS = 7


def attention_gather(place, layer, block, out, sems, tick):
    z_send, z_recv, n_send, n_recv, h_send, h_recv, c_send, c_recv, own_sem = sems
    rows = block.shape[1]
    half = rows // 2
    z, x, y, core = place.z, place.x, place.y, place.core

    def spot(sz, sx, sy, sc, start=0, size=rows):
        at = ((sz * 2 + sx) * 4 + sy * 2 + sc) * rows + start
        return out.at[pl.ds(pl.multiple_of(at, 16), size)]

    def line(sz):
        return spot(sz, x, y, core)

    def side(way, sz):
        return spot(sz, 1 - x, y, core) if way == 0 else spot(sz, x, 1 - y, core)

    def far(way, sz):
        return spot(sz, 1 - x, 1 - y, core, way * half, half)

    devices = (place.to_x, place.to_y)

    def at_distance(d, action):
        if d == 0:
            action(z)
            return
        @pl.when(z >= d)
        def _():
            action(z - d)

        @pl.when(z + d < Z_SIZE)
        def _():
            action(z + d)

    def line_step(sz, own):
        mine = block.at[layer] if own else line(sz)
        if not own:
            remote(line(sz), line(sz), z_send.at[0, sz], z_recv.at[sz], place.to_core).wait_recv()

        @pl.when((sz <= z) & (z < Z_SIZE - 1))
        def _():
            remote(mine, line(sz), z_send.at[0, sz], z_recv.at[sz], place.to_up).start()

        @pl.when((sz >= z) & (z > 0))
        def _():
            remote(mine, line(sz), z_send.at[1, sz], z_recv.at[sz], place.to_down).start()

        for way in range(2):
            remote(mine, line(sz), n_send.at[way, sz], n_recv.at[way, sz], devices[way]).start()
        remote(mine, line(sz), c_send.at[0, sz], c_recv.at[0, sz], place.to_core).start()

    def side_step(sz):
        for way in range(2):
            remote(side(way, sz), side(way, sz), n_send.at[way, sz], n_recv.at[way, sz], devices[way]).wait_recv()
            at = spot(sz, 1 - x, y, core, 0, half) if way == 0 else spot(sz, x, 1 - y, core, half, half)
            remote(at, at, h_send.at[way, sz], h_recv.at[way, sz], devices[1 - way]).start()
            remote(side(way, sz), side(way, sz), c_send.at[1 + way, sz], c_recv.at[1 + way, sz], place.to_core).start()

    def far_step(sz):
        for way in range(2):
            remote(far(way, sz), far(way, sz), h_send.at[way, sz], h_recv.at[way, sz], place.to_core).wait_recv()
            remote(far(way, sz), far(way, sz), c_send.at[3 + way, sz], c_recv.at[3 + way, sz], place.to_core).start()

    if tick == 0:
        pltpu.make_async_copy(block.at[layer], line(z), own_sem).start()
    if tick < 4:
        at_distance(tick, functools.partial(line_step, own=tick == 0))
    if 1 <= tick < 5:
        at_distance(tick - 1, side_step)
    if 2 <= tick < 6:
        at_distance(tick - 2, far_step)
    if tick == 6:
        pltpu.make_async_copy(block.at[layer], line(z), own_sem).wait()
        for sz in range(Z_SIZE):
            @pl.when((sz <= z) & (z < Z_SIZE - 1))
            def _():
                remote(line(sz), line(sz), z_send.at[0, sz], z_recv.at[sz], place.to_core).wait_send()

            @pl.when((sz >= z) & (z > 0))
            def _():
                remote(line(sz), line(sz), z_send.at[1, sz], z_recv.at[sz], place.to_core).wait_send()

            for way in range(2):
                remote(line(sz), line(sz), n_send.at[way, sz], n_recv.at[way, sz], place.to_core).wait_send()
                remote(far(way, sz), far(way, sz), h_send.at[way, sz], h_recv.at[way, sz], place.to_core).wait_send()
            parts = (
                (line(sz), spot(sz, x, y, 1 - core)),
                (side(0, sz), spot(sz, 1 - x, y, 1 - core)),
                (side(1, sz), spot(sz, x, 1 - y, 1 - core)),
                (far(0, sz), spot(sz, 1 - x, 1 - y, 1 - core, 0, half)),
                (far(1, sz), spot(sz, 1 - x, 1 - y, 1 - core, half, half)),
            )
            for i, (mine, theirs) in enumerate(parts):
                remote(mine, theirs, c_send.at[i, sz], c_recv.at[i, sz], place.to_core).wait()


def all_sum(axes, values, collective):
    parts, high, wide = values.shape

    def kernel(v_ref, out_ref, box, send, recv, send2, recv2):
        place = Place(axes)
        me = place.dp * 4 + place.t
        barrier = pltpu.get_barrier_semaphore()

        def peer(i):
            other = lax.rem(me + i, parts)
            return other, (other // 4, other % 4)

        def signal(i, _):
            pl.semaphore_signal(barrier, inc=1, device_id=peer(i)[1], device_id_type=MESH)
            return 0

        lax.fori_loop(1, parts, signal, 0)
        pl.semaphore_wait(barrier, parts - 1)

        def first(i, act):
            other, device = peer(i)
            act(remote(v_ref.at[other], box.at[i], send.at[i], recv.at[i], device))
            return 0

        lax.fori_loop(1, parts, lambda i, _: first(i, lambda c: c.start()), 0)
        lax.fori_loop(1, parts, lambda i, _: first(i, lambda c: c.wait()), 0)
        out_ref[me] = v_ref[me] + jnp.sum(box[1:], axis=0)

        def second(i, act):
            other, device = peer(i)
            act(remote(out_ref.at[me], out_ref.at[me], send2.at[i], recv2.at[i], device))
            return 0

        lax.fori_loop(1, parts, lambda i, _: second(i, lambda c: c.start()), 0)

        def finish(i, _):
            other = lax.rem(me + parts - i, parts)
            c = remote(out_ref.at[me], out_ref.at[other], send2.at[i], recv2.at[i], peer(i)[1])
            c.wait()
            return 0

        lax.fori_loop(1, parts, finish, 0)

    sem = pltpu.SemaphoreType.DMA((parts,))
    return pl.pallas_call(
        kernel,
        in_specs=[pl.BlockSpec(memory_space=pltpu.VMEM)],
        out_specs=pl.BlockSpec(memory_space=pltpu.VMEM),
        out_shape=jax.ShapeDtypeStruct(values.shape, F32),
        scratch_shapes=[pltpu.VMEM(values.shape, F32), sem, sem, sem, sem],
        compiler_params=pltpu.CompilerParams(collective_id=collective, has_side_effects=True),
        name="all_sum",
    )(values)


GROUP = 4
BLOCK = 256
GROUPS = HEADS // GROUP
TOKENS = 1024
ROWS = TOKENS // SEQ
ATT_STEPS = ROWS * GROUPS
FFN_STEPS = TOKENS // BLOCK
LAYER_STEPS = ATT_STEPS + FFN_STEPS
LAYERS = 2


def norm_parts(v):
    c = v - mean_rows(v)
    r = lax.rsqrt(mean_rows(c * c) + EPS)
    return c * r, r


def attend_unit(row, grp, length, xs, w, a, b, gain, qkv_ref, u_ref, o_ref, e_ref, rinv_ref, n1_ref, r1_ref,
                n1s, bound_ref):
    here = pl.ds(pl.multiple_of(row * SEQ, SEQ), SEQ)

    @pl.when(grp == 0)
    def _():
        x = xs[here, :]
        u = dot(x, a[...]).astype(BF)
        u_ref[0] = u
        for i in range(3):
            acc = dot(x, w[WIDTH * i:WIDTH * (i + 1), :])
            if i != 1:
                acc += dot(u, b[i // 2])
            qkv_ref[0, :, WIDTH * i:WIDTH * (i + 1)] = acc.astype(BF)
        key = lax.broadcasted_iota(jnp.int32, (SEQ, 128), 0)
        bound_ref[...] = jnp.where(key < length, 3.0e38, -8.0e9)

    lane = lax.broadcasted_iota(jnp.int32, (SEQ, 128), 1)
    low = lane < HEAD_DIM
    bound = bound_ref[...]
    bound = jnp.concatenate([bound] * 4, axis=1)
    for pair in range(GROUP // 2):
        at = pl.multiple_of(grp * (GROUP * HEAD_DIM) + pair * 128, 128)
        q = qkv_ref[0, :, pl.ds(at, 128)]
        k = qkv_ref[0, :, pl.ds(WIDTH + at, 128)]
        v = qkv_ref[0, :, pl.ds(2 * WIDTH + at, 128)]
        outs = []
        for half in range(2):
            mine = low if half == 0 else ~low
            qh = jnp.where(mine, q, jnp.zeros_like(q))
            vh = jnp.where(mine, v, jnp.ones_like(v))
            s = jnp.minimum(dot_nt(k, qh), bound)
            top = jnp.max(s, axis=0, keepdims=True)
            e = jnp.exp2((s - top) * EXP2_SCALE).astype(BF)
            e_ref[0, 0, pair * 2 + half] = e
            ot = dot_tn(vh, e)
            if half == 0:
                o_t, l = ot[:HEAD_DIM], ot[HEAD_DIM:HEAD_DIM + 8]
            else:
                o_t, l = ot[HEAD_DIM:], ot[0:8]
            r = 1.0 / l
            rinv_ref[0, 0, grp * GROUP + pair * 2 + half] = r
            outs.append(o_t * r[0:1])
        both = jnp.concatenate(outs, axis=0)
        o_ref[0, :, pl.ds(at, 128)] = both.T.astype(BF)

    @pl.when(grp == GROUPS - 1)
    def _():
        m, r = norm_parts(xs[here, :].astype(F32) + dot(o_ref[0], w[3 * WIDTH:, :]))
        n1 = (m * gain).astype(BF)
        n1_ref[0] = n1
        n1s[here, :] = n1
        r1_ref[0] = jnp.broadcast_to(r, (SEQ, 128))


def ffn_unit(block, w, gain, n1s, xs, gd_ref, r2_ref):
    here = pl.ds(pl.multiple_of(block * BLOCK, BLOCK), BLOCK)
    n1 = n1s[here, :]
    f = n1.astype(F32)
    for j in range(4):
        z = dot(n1, w[j, 0])
        cdf = 0.5 + 0.5 * lax.erf(z * 0.7071067811865476)
        pdf = jnp.exp2(z * (z * (-0.5 * 1.4426950408889634))) * 0.3989422804014327
        gd_ref[0, :, CHUNK * j:CHUNK * (j + 1)] = (cdf + z * pdf).astype(BF)
        f = f + dot((z * cdf).astype(BF), w[j, 1])
    m, r = norm_parts(f)
    xs[here, :] = (m * gain).astype(BF)
    r2_ref[0] = jnp.broadcast_to(r, (BLOCK, 128))


def forward_kernel(axes, direct, len_ref, tok, att, ex, pr, a_ref, b_ref, gain_ref,
                   qkv_ref, u_ref, o_ref, e_ref, rinv_ref, n1_ref, r1_ref, gd_ref, r2_ref, xall, wat_out, wf_out,
                   xs, n1s, wat, wf, bound, x_sem, xo_sem, wa_sem, wf_sem, own_sem, *sems):
    step = pl.program_id(0)
    layer = step // LAYER_STEPS
    part = step % LAYER_STEPS
    x_in = pltpu.make_async_copy(tok, xs, x_sem.at[0])
    x_out = pltpu.make_async_copy(tok, xall.at[0], x_sem.at[1])

    def save_x(l, b):
        rows = pl.ds(pl.multiple_of(b * BLOCK, BLOCK), BLOCK)
        return pltpu.make_async_copy(xs.at[rows], xall.at[l + 1, rows], xo_sem.at[b])

    def save_attention(l):
        return pltpu.make_async_copy(wat.at[l], wat_out.at[l], wa_sem.at[l])

    def save_ffn(l):
        return pltpu.make_async_copy(wf.at[l], wf_out.at[l], wf_sem.at[l])

    def own_ffn(l):
        return [pltpu.make_async_copy(r.at[l], wf.at[l, 0, m], own_sem.at[l, m]) for m, r in enumerate((ex, pr))]

    if direct:
        place = Place(axes)
        n_att = len(ATT_SEMS)
        n_ffn = len(FFN_SEMS)
        att_sems = [sems[:n_att], sems[n_att:2 * n_att]]
        sems = sems[2 * n_att:]
        ffn_sems = [sems[:n_ffn], sems[n_ffn:]]

        def run(job):
            kind, l, tick = job
            if kind == "a":
                attention_gather(place, l, att, wat.at[l], att_sems[l], tick)
            else:
                ffn_gather(place, l, ex, pr, wf.at[l], ffn_sems[l], tick)

    @pl.when(step == 0)
    def _():
        x_in.start()
        x_out.start()
        if direct:
            greet(place, True)
            for l in range(LAYERS):
                for c in own_ffn(l):
                    c.start()
            for job in SCHEDULE[0]:
                run(job)
            for l in range(LAYERS):
                for c in own_ffn(l):
                    c.wait()
            save_attention(0).start()
        else:
            whole = [pltpu.make_async_copy(att, wat, own_sem.at[0, 0]), pltpu.make_async_copy(ex, wf, own_sem.at[0, 1])]
            for c in whole:
                c.start()
            for c in whole:
                c.wait()
        x_in.wait()

    if direct:
        for at, jobs in SCHEDULE.items():
            if at:
                @pl.when(step == at)
                def _():
                    for job in jobs:
                        run(job)
                        if job == ("a", 1, ATT_TICKS - 1):
                            save_attention(1).start()
                        if job[0] == "f" and job[2] == FFN_TICKS - 1:
                            save_ffn(job[1]).start()

    @pl.when(part < ATT_STEPS)
    def _():
        row, grp = part // GROUPS, part % GROUPS
        attend_unit(row, grp, len_ref[row], xs, wat.at[layer], a_ref.at[layer], b_ref.at[layer], gain_ref[layer, 0:1],
                    qkv_ref, u_ref, o_ref, e_ref, rinv_ref, n1_ref, r1_ref, n1s, bound)

    @pl.when(part >= ATT_STEPS)
    def _():
        block = part - ATT_STEPS

        @pl.when(layer > 0)
        def _():
            save_x(layer - 1, block).wait()

        ffn_unit(block, wf.at[layer], gain_ref[layer, 1:2], n1s, xs, gd_ref, r2_ref)
        save_x(layer, block).start()

    @pl.when(step == LAYERS * LAYER_STEPS - 1)
    def _():
        x_out.wait()
        for b in range(FFN_STEPS):
            save_x(LAYERS - 1, b).wait()
        if direct:
            for l in range(LAYERS):
                save_attention(l).wait()
                save_ffn(l).wait()


SCHEDULE = {
    0: [("a", 0, t) for t in range(5)] + [("f", 0, 0)] + [("a", 0, t) for t in range(5, 7)],
    1: [("f", 0, 1)],
    2: [("f", 0, 2)],
    3: [("f", 0, 3)],
    4: [("f", 0, 4), ("a", 1, 0)],
    5: [("f", 0, 5), ("a", 1, 1)],
    6: [("f", 0, 6), ("f", 0, 7)],
    7: [("a", 1, 2)],
    8: [("a", 1, 3)],
    9: [("a", 1, 4), ("f", 1, 0)],
    10: [("a", 1, 5), ("a", 1, 6)],
    11: [("f", 1, 1)],
    12: [("f", 1, 2)],
    13: [("f", 1, 3)],
    14: [("f", 1, 4)],
    15: [("f", 1, 5)],
    16: [("f", 1, 6), ("f", 1, 7)],
}


def forward(axes, direct, lengths, tokens, att, ex, pr, a, b, gains):
    anywhere = pl.BlockSpec(memory_space=pl.ANY)
    row_of = lambda s: jnp.minimum(s % LAYER_STEPS // GROUPS, ROWS - 1)
    block_of = lambda s: jnp.maximum(s % LAYER_STEPS - ATT_STEPS, 0)
    layer_of = lambda s: s // LAYER_STEPS
    by_row = lambda width: pl.BlockSpec((1, SEQ, width), lambda s: (layer_of(s), row_of(s), 0))
    by_block = lambda width: pl.BlockSpec((1, BLOCK, width), lambda s: (layer_of(s), block_of(s), 0))
    whole = lambda v: pl.BlockSpec(v.shape, lambda s: (0,) * v.ndim, pipeline_mode=pl.Buffered(1))
    group_of = lambda s: jnp.where(s % LAYER_STEPS < ATT_STEPS, s % LAYER_STEPS % GROUPS, GROUPS - 1)
    shape = jax.ShapeDtypeStruct
    dma = pltpu.SemaphoreType.DMA
    return pl.pallas_call(
        functools.partial(forward_kernel, axes, direct),
        grid=(LAYERS * LAYER_STEPS,),
        in_specs=[pl.BlockSpec(memory_space=pltpu.SMEM)] + [anywhere] * 4 + [whole(a), whole(b), whole(gains)],
        out_specs=[
            by_row(3 * WIDTH), by_row(2 * RANK), by_row(WIDTH),
            pl.BlockSpec((1, 1, GROUP, SEQ, SEQ), lambda s: (layer_of(s), row_of(s), group_of(s), 0, 0)),
            pl.BlockSpec((1, 1, HEADS, 8, SEQ), lambda s: (layer_of(s), row_of(s), 0, 0, 0)),
            by_row(WIDTH), by_row(128), by_block(4 * CHUNK), by_block(128), anywhere, anywhere, anywhere,
        ],
        out_shape=[
            shape((LAYERS, TOKENS, 3 * WIDTH), BF), shape((LAYERS, TOKENS, 2 * RANK), BF), shape((LAYERS, TOKENS, WIDTH), BF),
            shape((LAYERS, ROWS, HEADS, SEQ, SEQ), BF), shape((LAYERS, ROWS, HEADS, 8, SEQ), F32),
            shape((LAYERS, TOKENS, WIDTH), BF), shape((LAYERS, TOKENS, 128), F32),
            shape((LAYERS, TOKENS, 4 * CHUNK), BF), shape((LAYERS, TOKENS, 128), F32),
            shape((LAYERS + 1, TOKENS, WIDTH), BF),
            shape((LAYERS, 4 * WIDTH, WIDTH), BF), shape((LAYERS, 4, 2, WIDTH, CHUNK), BF),
        ],
        scratch_shapes=[
            pltpu.VMEM((TOKENS, WIDTH), BF), pltpu.VMEM((TOKENS, WIDTH), BF),
            pltpu.VMEM((LAYERS, 4 * WIDTH, WIDTH), BF), pltpu.VMEM((LAYERS, 4, 2, WIDTH, CHUNK), BF),
            pltpu.VMEM((SEQ, 128), F32),
            dma((2,)), dma((FFN_STEPS,)), dma((LAYERS,)), dma((LAYERS,)), dma((LAYERS, 2)),
        ] + (ATT_SEMS * 2 + FFN_SEMS * 2 if direct else []),
        compiler_params=params(1, 0 if direct else None),
        name="forward",
    )(lengths, tokens, att, ex, pr, a, b, gains)


def norm_back(e, m, r):
    return r * (e - mean_rows(e) - m * mean_rows(e * m))


def ffn_back_unit(dy, x2_ref, r2_ref, n1_ref, r1_ref, gd_ref, w, wo, gains, wait):
    g1, g2 = gains[0:1], gains[1:2]
    dh2 = norm_back(dy * g2, x2_ref[0].astype(F32) * (1.0 / g2), r2_ref[0, :, 0:1])
    df = dh2.astype(BF)
    dn = dh2
    for j in range(4):
        wait(j)
        dz = (dot_nt(df, w[j, 1]) * gd_ref[0, :, CHUNK * j:CHUNK * (j + 1)].astype(F32)).astype(BF)
        dn = dn + dot_nt(dz, w[j, 0])
    dh = norm_back(dn * g1, n1_ref[0].astype(F32) * (1.0 / g1), r1_ref[0, :, 0:1])
    wait(4)
    return dh, dot_nt(dh.astype(BF), wo[...]).astype(BF)


def attend_back_unit(grp, do_ref, qkv_ref, o_ref, e_ref, rinv_ref, d_ref):
    lane = lax.broadcasted_iota(jnp.int32, (SEQ, 128), 1)
    low = lane < HEAD_DIM
    for pair in range(GROUP // 2):
        at = pl.multiple_of(grp * (GROUP * HEAD_DIM) + pair * 128, 128)
        q = qkv_ref[0, :, pl.ds(at, 128)]
        k = qkv_ref[0, :, pl.ds(WIDTH + at, 128)]
        v = qkv_ref[0, :, pl.ds(2 * WIDTH + at, 128)]
        head = grp * GROUP + pair * 2
        scale = jnp.concatenate([rinv_ref[0, 0, head]] * 8 + [rinv_ref[0, 0, head + 1]] * 8, axis=0).T
        dos = do_ref[:, pl.ds(at, 128)].astype(F32) * scale
        other = pltpu.roll(-dos * o_ref[0, :, pl.ds(at, 128)].astype(F32), HEAD_DIM, 1).astype(BF)
        dos = dos.astype(BF)
        dvs, dks, dqs = [], [], []
        for half in range(2):
            mine = low if half == 0 else ~low
            e = e_ref[0, 0, pair * 2 + half]
            dp = dot_nt(jnp.where(mine, v, jnp.ones_like(v)), jnp.where(mine, dos, other))
            ds = (dp * e.astype(F32)).astype(BF)
            dvs.append(dot(e, dos))
            dks.append(dot(ds, q))
            dqs.append(dot_tn(k, ds)[half * HEAD_DIM:(half + 1) * HEAD_DIM])
        d_ref[:, pl.ds(2 * WIDTH + at, 128)] = jnp.where(low, dvs[0], dvs[1]).astype(BF)
        d_ref[:, pl.ds(WIDTH + at, 128)] = (jnp.where(low, dks[0], dks[1]) * HEAD_DIM ** (-0.5)).astype(BF)
        d_ref[:, pl.ds(at, 128)] = (jnp.concatenate(dqs, axis=0) * HEAD_DIM ** (-0.5)).T.astype(BF)


def backward_kernel(cot_ref, x2_ref, r2_ref, n1_ref, r1_ref, gd_ref, x_ref, u_ref, qkv_ref, o_ref, e_ref, rinv_ref,
                    a_ref, b_ref, gain_ref, wat_in, wf_in, xall,
                    dx_ref, grad_ref, hidden,
                    dhs, dos, dys, d_ref, wat, wf, wa_sem, wf_sem, h_sem):
    step = pl.program_id(0)
    layer = LAYERS - 1 - step // LAYER_STEPS
    part = step % LAYER_STEPS
    hidden_copy = pltpu.make_async_copy(xall.at[LAYERS], hidden, h_sem)

    def load_ffn(l, j):
        return pltpu.make_async_copy(wf_in.at[l, j], wf.at[j], wf_sem.at[j])

    def load_attention(l, i):
        rows = pl.ds(3 * WIDTH, WIDTH) if i == 1 else pl.ds(0, 3 * WIDTH)
        return pltpu.make_async_copy(wat_in.at[l, rows], wat.at[l, rows], wa_sem.at[l, i])

    last = LAYERS - 1

    @pl.when(step == 0)
    def _():
        for j in range(4):
            load_ffn(last, j).start()
        load_attention(last, 1).start()
        load_attention(last, 0).start()
        hidden_copy.start()
        grad_ref[...] = jnp.zeros_like(grad_ref)

    for k in range(1, LAYERS):
        @pl.when(step == k * LAYER_STEPS - ATT_STEPS)
        def _():
            for j in range(4):
                load_ffn(last - k, j).start()
            load_attention(last - k, 1).start()
            load_attention(last - k, 0).start()

        @pl.when(step == k * LAYER_STEPS)
        def _():
            for j in range(4):
                load_ffn(last - k, j).wait()
            load_attention(last - k, 1).wait()

        @pl.when(step == k * LAYER_STEPS + FFN_STEPS)
        def _():
            load_attention(last - k, 0).wait()

    @pl.when(step == FFN_STEPS)
    def _():
        load_attention(last, 0).wait()

    def ffn_part(dy, wait):
        here = pl.ds(pl.multiple_of(part * BLOCK, BLOCK), BLOCK)
        dh, do = ffn_back_unit(dy(here), x2_ref, r2_ref, n1_ref, r1_ref, gd_ref, wf, wat.at[layer, 3 * WIDTH:, :],
                               gain_ref[layer], wait)
        dhs[here, :] = dh
        dos[here, :] = do

    def wait_load(j):
        if j < 4:
            load_ffn(last, j).wait()
        else:
            load_attention(last, 1).wait()

    @pl.when(step == 0)
    def _():
        ffn_part(lambda here: cot_ref[...].astype(F32), wait_load)

    @pl.when((step > 0) & (step < FFN_STEPS))
    def _():
        ffn_part(lambda here: cot_ref[...].astype(F32), lambda j: None)

    @pl.when((step >= LAYER_STEPS) & (part < FFN_STEPS))
    def _():
        ffn_part(lambda here: dys[here, :], lambda j: None)

    @pl.when(part >= FFN_STEPS)
    def _():
        row, grp = (part - FFN_STEPS) // GROUPS, (part - FFN_STEPS) % GROUPS
        here = pl.ds(pl.multiple_of(row * SEQ, SEQ), SEQ)
        attend_back_unit(grp, dos.at[here], qkv_ref, o_ref, e_ref, rinv_ref, d_ref)

        @pl.when(grp == GROUPS - 1)
        def _():
            dq, dk, dv = (d_ref[:, WIDTH * i:WIDTH * (i + 1)] for i in range(3))
            du = (dot_nt(dq, b_ref[layer, 0]) + dot_nt(dv, b_ref[layer, 1])).astype(BF)
            u = u_ref[0]
            u2 = u + u
            ga = dot_tn(du, x_ref[0])
            gq = dot_tn(u2, dq)[:RANK]
            gv = dot_tn(u2, dv)[RANK:]
            grad_ref[layer] += jnp.concatenate([ga, gq, gv], axis=0)
            w = wat.at[layer]
            dx = (dhs[here, :] + dot_nt(dq, w[0:WIDTH, :]) + dot_nt(dk, w[WIDTH:2 * WIDTH, :])
                  + dot_nt(dv, w[2 * WIDTH:3 * WIDTH, :]) + dot_nt(du, a_ref[layer]))

            @pl.when(layer > 0)
            def _():
                dys[here, :] = dx

            @pl.when(layer == 0)
            def _():
                dx_ref[...] = dx

    @pl.when(step == LAYERS * LAYER_STEPS - 1)
    def _():
        hidden_copy.wait()


def backward(cot, saved, a, b, gains, wat, wf):
    qkv, u, o, e, rinv, n1, r1, gd, r2, xall = saved
    anywhere = pl.BlockSpec(memory_space=pl.ANY)
    layer_of = lambda s: LAYERS - 1 - s // LAYER_STEPS
    block_of = lambda s: jnp.minimum(s % LAYER_STEPS, FFN_STEPS - 1)
    unit_of = lambda s: jnp.maximum(s % LAYER_STEPS - FFN_STEPS, 0)
    row_of = lambda s: unit_of(s) // GROUPS
    group_of = lambda s: unit_of(s) % GROUPS
    by_row = lambda width: pl.BlockSpec((1, SEQ, width), lambda s: (layer_of(s), row_of(s), 0))
    by_block = lambda width: pl.BlockSpec((1, BLOCK, width), lambda s: (layer_of(s), block_of(s), 0))
    whole = lambda v: pl.BlockSpec(v.shape, lambda s: (0,) * v.ndim, pipeline_mode=pl.Buffered(1))
    shape = jax.ShapeDtypeStruct
    dma = pltpu.SemaphoreType.DMA
    return pl.pallas_call(
        backward_kernel,
        grid=(LAYERS * LAYER_STEPS,),
        in_specs=[
            pl.BlockSpec((BLOCK, WIDTH), lambda s: (jnp.minimum(s, FFN_STEPS - 1), 0)),
            pl.BlockSpec((1, BLOCK, WIDTH), lambda s: (layer_of(s) + 1, block_of(s), 0)),
            by_block(128), by_block(WIDTH), by_block(128), by_block(4 * CHUNK),
            by_row(WIDTH), by_row(2 * RANK), by_row(3 * WIDTH), by_row(WIDTH),
            pl.BlockSpec((1, 1, GROUP, SEQ, SEQ), lambda s: (layer_of(s), row_of(s), group_of(s), 0, 0)),
            pl.BlockSpec((1, 1, HEADS, 8, SEQ), lambda s: (layer_of(s), row_of(s), 0, 0, 0)),
            whole(a), whole(b), whole(gains), anywhere, anywhere, anywhere,
        ],
        out_specs=[
            pl.BlockSpec((SEQ, WIDTH), lambda s: (jnp.where(s < LAYER_STEPS * (LAYERS - 1), 0, row_of(s)), 0)),
            pl.BlockSpec((LAYERS, 4 * RANK, WIDTH), lambda s: (0, 0, 0)),
            anywhere,
        ],
        out_shape=[shape((TOKENS, WIDTH), F32), shape((LAYERS, 4 * RANK, WIDTH), F32), shape((TOKENS, WIDTH), BF)],
        scratch_shapes=[
            pltpu.VMEM((TOKENS, WIDTH), F32), pltpu.VMEM((TOKENS, WIDTH), BF), pltpu.VMEM((TOKENS, WIDTH), F32),
            pltpu.VMEM((SEQ, 3 * WIDTH), BF), pltpu.VMEM((LAYERS, 4 * WIDTH, WIDTH), BF),
            pltpu.VMEM((4, 2, WIDTH, CHUNK), BF),
            dma((LAYERS, 2)), dma((4,)), dma,
        ],
        compiler_params=params(1),
        name="backward",
    )(cot, xall, r2, n1, r1, gd, xall, u, qkv, o, e, rinv, a, b, gains, wat, wf, xall)


def local(axes, direct, tokens, lengths, attention, down, up, expand, project, gains, cotangent):
    a = jnp.concatenate([down[:, 0], down[:, 1]], axis=2)
    twice = up + up
    b = jnp.stack([jnp.pad(twice[:, 0], ((0, 0), (0, RANK), (0, 0))), jnp.pad(twice[:, 1], ((0, 0), (RANK, 0), (0, 0)))],
                  axis=1)
    if direct:
        att, ex, pr = attention, expand, project
    else:
        att = lax.all_gather(attention, axes, axis=1, tiled=True)
        w1 = lax.all_gather(expand, axes[1], axis=2, tiled=True).reshape(LAYERS, WIDTH, 4, CHUNK).transpose(0, 2, 1, 3)
        w2 = lax.all_gather(project, axes[1], axis=1, tiled=True).reshape(LAYERS, 4, CHUNK, WIDTH)
        ex = pr = jnp.stack([w1, w2], axis=2)
    *saved, wat, wf = forward(axes, direct, lengths, tokens, att, ex, pr, a, b, gains)
    if not direct:
        wat, wf = att, ex
    dx, grads, hidden = backward(cotangent, saved, a, b, gains, wat, wf)
    if direct:
        total = all_sum(axes, grads.reshape(32, -1, 128), 1).reshape(grads.shape)
    else:
        total = lax.psum(grads, axes)
    a_grad = total[:, :2 * RANK].reshape(LAYERS, 2, RANK, WIDTH).transpose(0, 1, 3, 2)
    b_grad = total[:, 2 * RANK:].reshape(LAYERS, 2, RANK, WIDTH)
    return hidden, dx, a_grad, b_grad


def solution(mesh):
    axes = tuple(mesh.axis_names)
    dp, tensor = axes
    direct = mesh.shape[dp] == 2 * Z_SIZE and mesh.shape[tensor] == 4
    placed = (
        P(axes, None), P(axes), P(None, axes, None), P(), P(),
        P(None, None, tensor), P(None, tensor, None), P(), P(axes, None),
    )
    return jax.shard_map(
        functools.partial(local, axes, direct),
        mesh=mesh,
        in_specs=placed,
        out_specs=(P(axes, None), P(axes, None), P(), P()),
        check_vma=False,
    )
```

```python
import functools
import jax
import jax.numpy as jnp
from jax import lax
from jax.experimental import pallas as pl
from jax.experimental.pallas import tpu as pltpu
from jax.sharding import PartitionSpec as P

WIDTH = 768
HEADS = 12
HEAD_DIM = 64
SEQ = 512
RANK = 8
EPS = 1e-05
CHUNK = 768
BF = jnp.bfloat16
F32 = jnp.float32
VMEM_LIMIT = 60 * 1024 * 1024
EXP2_SCALE = 1.4426950408889634 * HEAD_DIM ** (-0.5)


def dot(a, b):
    return jnp.dot(a, b, preferred_element_type=F32)


def dot_nt(a, b):
    return lax.dot_general(a, b, (((1,), (1,)), ((), ())), preferred_element_type=F32)


def dot_tn(a, b):
    return lax.dot_general(a, b, (((0,), (0,)), ((), ())), preferred_element_type=F32)


def mean_rows(v):
    return jnp.sum(v, axis=-1, keepdims=True) * (1.0 / WIDTH)


def params(n, collective=None):
    more = {} if collective is None else {"collective_id": collective, "has_side_effects": True}
    return pltpu.CompilerParams(
        dimension_semantics=("arbitrary",) * n, vmem_limit_bytes=VMEM_LIMIT, **more
    )


MESH = pl.DeviceIdType.MESH
Z_SIZE = 4


class Place:
    def __init__(self, axes):
        dp, t = lax.axis_index(axes[0]), lax.axis_index(axes[1])
        self.dp, self.t = dp, t
        self.z, self.x = dp // 2, dp % 2
        self.y, self.core = t // 2, t % 2
        self.to_core = (dp, t + 1 - 2 * self.core)
        self.to_y = (dp, t + 2 - 4 * self.y)
        self.to_x = (dp + 1 - 2 * self.x, t)
        self.to_zpair = (dp + 2 - 4 * (self.z % 2), t)
        self.to_up = (dp + 2, t)
        self.to_down = (dp - 2, t)


def greet(place, line):
    barrier = pltpu.get_barrier_semaphore()
    for device in (place.to_core, place.to_y, place.to_x):
        pl.semaphore_signal(barrier, inc=1, device_id=device, device_id_type=MESH)
    if line:
        @pl.when(place.z < Z_SIZE - 1)
        def _():
            pl.semaphore_signal(barrier, inc=1, device_id=place.to_up, device_id_type=MESH)

        @pl.when(place.z > 0)
        def _():
            pl.semaphore_signal(barrier, inc=1, device_id=place.to_down, device_id_type=MESH)

        inner = (place.z > 0) & (place.z < Z_SIZE - 1)

        @pl.when(inner)
        def _():
            pl.semaphore_wait(barrier, 5)

        @pl.when(jnp.logical_not(inner))
        def _():
            pl.semaphore_wait(barrier, 4)
    else:
        pl.semaphore_signal(barrier, inc=1, device_id=place.to_zpair, device_id_type=MESH)
        pl.semaphore_wait(barrier, 4)


def remote(src, dst, send, recv, device):
    return pltpu.make_async_remote_copy(
        src_ref=src, dst_ref=dst, send_sem=send, recv_sem=recv, device_id=device, device_id_type=MESH
    )


SLICE = 128
FFN_SEMS = [
    pltpu.SemaphoreType.DMA((3, 4)),
    pltpu.SemaphoreType.DMA((12,)),
    pltpu.SemaphoreType.DMA((14,)),
    pltpu.SemaphoreType.DMA((14,)),
]


def ffn_gather(place, layer, w1, w2, out, sems, what, tick=0):
    send, recv, core_send, core_recv = sems
    g = place.x * 2 + place.z % 2
    gd = 3 - g
    gx = (1 - place.x) * 2 + place.z % 2
    gz = place.x * 2 + 1 - place.z % 2

    def spot(slot, s):
        return out.at[slot + 1, s // 6, pl.ds(pl.multiple_of((s % 6) * SLICE, SLICE), SLICE)]

    def over_y(i):
        s = 3 * g + i if i < 3 else 3 * gd
        first = place.x == (0 if i < 3 else 1)
        for here, ref in ((first, w1), (jnp.logical_not(first), w2)):
            @pl.when(here)
            def _():
                src = ref.at[layer, pl.ds(pl.multiple_of((s % 6) * SLICE, SLICE), SLICE)]
                remote(src, spot(1, s), send.at[0, i], recv.at[s], place.to_y).start()

    def arrived(s):
        remote(spot(1, s), spot(1, s), send.at[0, 0], recv.at[s], place.to_y).wait_recv()

    def over(way, i, s):
        device = place.to_x if way == 1 else place.to_zpair
        remote(spot(1, s), spot(1, s), send.at[way, i], recv.at[s], device).start()

    def share(s):
        remote(spot(1, s), spot(2, s), core_send.at[s], core_recv.at[s], place.to_core).start()

    if what == "fy":
        over_y(tick)
    elif what == "fown":
        for m, ref in enumerate((w1, w2)):
            remote(ref.at[layer], out.at[1, m], core_send.at[12 + m], core_recv.at[12 + m], place.to_core).start()
    elif what == "fr" and tick < 4:
        s = 3 * g + tick - 1
        arrived(s)
        over(1, tick - 1, s)
        over(2, tick - 1, s)
        share(s)
        if tick == 3:
            for s in (3 * gx, 3 * gz):
                arrived(s)
                share(s)
    elif what == "fr" and tick == 4:
        s = 3 * gz + 1
        arrived(s)
        over(1, 3, s)
        share(s)
        for s in (3 * gd, 3 * gx + 1):
            arrived(s)
            share(s)
    elif what == "fr" and tick == 5:
        s = 3 * gx + 2
        arrived(s)
        over(2, 3, s)
        share(s)
        s = 3 * gz + 2
        arrived(s)
        share(s)
    elif what == "fr" and tick == 6:
        for s in (3 * gd + 1, 3 * gd + 2):
            arrived(s)
            share(s)
    else:
        for s in range(12):
            remote(spot(1, s), spot(2, s), core_send.at[s], core_recv.at[s], place.to_core).wait()
        for m, ref in enumerate((w1, w2)):
            remote(ref.at[layer], out.at[1, m], core_send.at[12 + m], core_recv.at[12 + m], place.to_core).wait()
        for way in range(3):
            for i in range(4):
                remote(spot(1, 0), spot(1, 0), send.at[way, i], recv.at[0], place.to_y).wait_send()


ATT_SEMS = [
    pltpu.SemaphoreType.DMA((2, 4)),
    pltpu.SemaphoreType.DMA((4,)),
    pltpu.SemaphoreType.DMA((2, 4)),
    pltpu.SemaphoreType.DMA((2, 4)),
    pltpu.SemaphoreType.DMA((2, 4)),
    pltpu.SemaphoreType.DMA((2, 4)),
    pltpu.SemaphoreType.DMA((5, 4)),
    pltpu.SemaphoreType.DMA((5, 4)),
    pltpu.SemaphoreType.DMA,
]


def attention_gather(place, layer, block, out, sems, what, d=0):
    z_send, z_recv, n_send, n_recv, h_send, h_recv, c_send, c_recv, own_sem = sems
    rows = block.shape[1]
    half = rows // 2
    z, x, y, core = place.z, place.x, place.y, place.core
    late = Z_SIZE - 1

    def spot(sz, sx, sy, sc, start=0, size=rows):
        at = ((sz * 2 + sx) * 4 + sy * 2 + sc) * rows + start
        return out.at[pl.ds(pl.multiple_of(at, 16), size)]

    def line(sz):
        return spot(sz, x, y, core)

    def side(way, sz):
        return spot(sz, 1 - x, y, core) if way == 0 else spot(sz, x, 1 - y, core)

    def far(way, sz):
        return spot(sz, 1 - x, 1 - y, core, way * half, half)

    devices = (place.to_x, place.to_y)

    def at_distance(d, action, size):
        if d == 0:
            @pl.when(z < size)
            def _():
                action(z)

            return

        @pl.when(z >= d)
        def _():
            action(z - d)

        @pl.when(z + d < size)
        def _():
            action(z + d)

    def line_step(sz, own):
        mine = block.at[layer] if own else line(sz)
        if not own:
            remote(line(sz), line(sz), z_send.at[0, sz], z_recv.at[sz], place.to_core).wait_recv()

        @pl.when((sz <= z) & (z < Z_SIZE - 1))
        def _():
            remote(mine, line(sz), z_send.at[0, sz], z_recv.at[sz], place.to_up).start()

        @pl.when((sz >= z) & (z > 0))
        def _():
            remote(mine, line(sz), z_send.at[1, sz], z_recv.at[sz], place.to_down).start()

        if own:
            @pl.when(sz < late)
            def _():
                spread(sz, mine)
        else:
            @pl.when(sz < late)
            def _():
                spread(sz, line(sz))

    def spread(sz, mine):
        for way in range(2):
            remote(mine, line(sz), n_send.at[way, sz], n_recv.at[way, sz], devices[way]).start()
        remote(mine, line(sz), c_send.at[0, sz], c_recv.at[0, sz], place.to_core).start()

    def side_step(sz):
        for way in range(2):
            remote(side(way, sz), side(way, sz), n_send.at[way, sz], n_recv.at[way, sz], devices[way]).wait_recv()
            at = spot(sz, 1 - x, y, core, 0, half) if way == 0 else spot(sz, x, 1 - y, core, half, half)
            remote(at, at, h_send.at[way, sz], h_recv.at[way, sz], devices[1 - way]).start()
            remote(side(way, sz), side(way, sz), c_send.at[1 + way, sz], c_recv.at[1 + way, sz], place.to_core).start()

    def far_step(sz):
        for way in range(2):
            remote(far(way, sz), far(way, sz), h_send.at[way, sz], h_recv.at[way, sz], place.to_core).wait_recv()
            remote(far(way, sz), far(way, sz), c_send.at[3 + way, sz], c_recv.at[3 + way, sz], place.to_core).start()

    def finish(sz):
        @pl.when((sz <= z) & (z < Z_SIZE - 1))
        def _():
            remote(line(sz), line(sz), z_send.at[0, sz], z_recv.at[sz], place.to_core).wait_send()

        @pl.when((sz >= z) & (z > 0))
        def _():
            remote(line(sz), line(sz), z_send.at[1, sz], z_recv.at[sz], place.to_core).wait_send()

        for way in range(2):
            remote(line(sz), line(sz), n_send.at[way, sz], n_recv.at[way, sz], place.to_core).wait_send()
            remote(far(way, sz), far(way, sz), h_send.at[way, sz], h_recv.at[way, sz], place.to_core).wait_send()
        parts = (
            (line(sz), spot(sz, x, y, 1 - core)),
            (side(0, sz), spot(sz, 1 - x, y, 1 - core)),
            (side(1, sz), spot(sz, x, 1 - y, 1 - core)),
            (far(0, sz), spot(sz, 1 - x, 1 - y, 1 - core, 0, half)),
            (far(1, sz), spot(sz, 1 - x, 1 - y, 1 - core, half, half)),
        )
        for i, (mine, theirs) in enumerate(parts):
            remote(mine, theirs, c_send.at[i, sz], c_recv.at[i, sz], place.to_core).wait()

    own_copy = pltpu.make_async_copy(block.at[layer], line(z), own_sem)
    if what == "line":
        if d == 0:
            own_copy.start()
        at_distance(d, functools.partial(line_step, own=d == 0), Z_SIZE)
    if what == "side":
        at_distance(d, side_step, late)
    if what == "far":
        at_distance(d, far_step, late)
    if what == "fin012":
        own_copy.wait()
        for sz in range(late):
            finish(sz)
    if what == "line3":
        @pl.when(z == late)
        def _():
            spread(late, block.at[layer])

        @pl.when(z < late)
        def _():
            spread(late, line(late))
    if what == "side3":
        side_step(late)
    if what == "far3":
        far_step(late)
    if what == "fin3":
        finish(late)


def all_sum(axes, values, collective):
    parts, high, wide = values.shape

    def kernel(v_ref, out_ref, box, send, recv, send2, recv2):
        place = Place(axes)
        me = place.dp * 4 + place.t
        barrier = pltpu.get_barrier_semaphore()

        def peer(i):
            other = lax.rem(me + i, parts)
            return other, (other // 4, other % 4)

        def signal(i, _):
            pl.semaphore_signal(barrier, inc=1, device_id=peer(i)[1], device_id_type=MESH)
            return 0

        lax.fori_loop(1, parts, signal, 0)
        pl.semaphore_wait(barrier, parts - 1)

        def first(i, act):
            other, device = peer(i)
            act(remote(v_ref.at[other], box.at[i], send.at[i], recv.at[i], device))
            return 0

        lax.fori_loop(1, parts, lambda i, _: first(i, lambda c: c.start()), 0)
        lax.fori_loop(1, parts, lambda i, _: first(i, lambda c: c.wait()), 0)
        out_ref[me] = v_ref[me] + jnp.sum(box[1:], axis=0)

        def second(i, act):
            other, device = peer(i)
            act(remote(out_ref.at[me], out_ref.at[me], send2.at[i], recv2.at[i], device))
            return 0

        lax.fori_loop(1, parts, lambda i, _: second(i, lambda c: c.start()), 0)

        def finish(i, _):
            other = lax.rem(me + parts - i, parts)
            c = remote(out_ref.at[me], out_ref.at[other], send2.at[i], recv2.at[i], peer(i)[1])
            c.wait()
            return 0

        lax.fori_loop(1, parts, finish, 0)

    sem = pltpu.SemaphoreType.DMA((parts,))
    return pl.pallas_call(
        kernel,
        in_specs=[pl.BlockSpec(memory_space=pltpu.VMEM)],
        out_specs=pl.BlockSpec(memory_space=pltpu.VMEM),
        out_shape=jax.ShapeDtypeStruct(values.shape, F32),
        scratch_shapes=[pltpu.VMEM(values.shape, F32), sem, sem, sem, sem],
        compiler_params=pltpu.CompilerParams(collective_id=collective, has_side_effects=True),
        name="all_sum",
    )(values)


GROUP = 6
BLOCK = 256
GROUPS = HEADS // GROUP
TOKENS = 1024
ROWS = TOKENS // SEQ
ATT_STEPS = ROWS * GROUPS
FFN_STEPS = TOKENS // BLOCK
LAYER_STEPS = ATT_STEPS + FFN_STEPS
FORWARD_STEPS = ROWS + FFN_STEPS
LAYERS = 2


def norm_parts(v):
    c = v - mean_rows(v)
    r = lax.rsqrt(mean_rows(c * c) + EPS)
    return c * r, r


def attend_unit(row, length, xs, w, a, b, gain, qkv_ref, u_ref, o_ref, e_ref, rinv_ref, n1_ref, r1_ref, n1s, slot):
    here = pl.ds(pl.multiple_of(row * SEQ, SEQ), SEQ)
    x = xs[here, :]
    u = dot(x, a[...]).astype(BF)
    u_ref[0] = u
    for i in range(3):
        acc = dot(x, w[WIDTH * i:WIDTH * (i + 1), :])
        if i != 1:
            acc += dot(u, b[i // 2])
        qkv_ref[0, :, WIDTH * i:WIDTH * (i + 1)] = acc.astype(BF)
    key = lax.broadcasted_iota(jnp.int32, (SEQ, 128), 0)
    bound = jnp.where(key < length, 3.0e38, -8.0e9)
    lane = lax.broadcasted_iota(jnp.int32, (SEQ, 128), 1)
    low = lane < HEAD_DIM
    bound = jnp.concatenate([bound] * 4, axis=1)
    for pair in range(HEADS // 2):
        slot(pair)
        at = pair * 128
        q = qkv_ref[0, :, at:at + 128]
        k = qkv_ref[0, :, WIDTH + at:WIDTH + at + 128]
        v = qkv_ref[0, :, 2 * WIDTH + at:2 * WIDTH + at + 128]
        outs = []
        for half in range(2):
            mine = low if half == 0 else ~low
            qh = jnp.where(mine, q, jnp.zeros_like(q))
            vh = jnp.where(mine, v, jnp.ones_like(v))
            s = jnp.minimum(dot_nt(k, qh), bound)
            top = jnp.max(s, axis=0, keepdims=True)
            e = jnp.exp2((s - top) * EXP2_SCALE).astype(BF)
            e_ref[0, 0, pair * 2 + half] = e
            ot = dot_tn(vh, e)
            if half == 0:
                o_t, l = ot[:HEAD_DIM], ot[HEAD_DIM:HEAD_DIM + 8]
            else:
                o_t, l = ot[HEAD_DIM:], ot[0:8]
            r = 1.0 / l
            rinv_ref[0, 0, pair * 2 + half] = r
            outs.append(o_t * r[0:1])
        both = jnp.concatenate(outs, axis=0)
        o_ref[0, :, at:at + 128] = both.T.astype(BF)
    slot(HEADS // 2)
    m, r = norm_parts(xs[here, :].astype(F32) + dot(o_ref[0], w[3 * WIDTH:, :]))
    n1 = (m * gain).astype(BF)
    n1_ref[0] = n1
    n1s[here, :] = n1
    r1_ref[0] = jnp.broadcast_to(r, (SEQ, 128))


def ffn_unit(block, w, gain, n1s, xs, gd_ref, r2_ref):
    here = pl.ds(pl.multiple_of(block * BLOCK, BLOCK), BLOCK)
    n1 = n1s[here, :]
    f = n1.astype(F32)
    for j in range(4):
        z = dot(n1, w[j, 0])
        cdf = 0.5 + 0.5 * lax.erf(z * 0.7071067811865476)
        pdf = jnp.exp2(z * (z * (-0.5 * 1.4426950408889634))) * 0.3989422804014327
        gd_ref[0, :, CHUNK * j:CHUNK * (j + 1)] = (cdf + z * pdf).astype(BF)
        f = f + dot((z * cdf).astype(BF), w[j, 1])
    m, r = norm_parts(f)
    xs[here, :] = (m * gain).astype(BF)
    r2_ref[0] = jnp.broadcast_to(r, (BLOCK, 128))


def forward_kernel(axes, direct, len_ref, tok, att, ex, pr, a_ref, b_ref, gain_ref,
                   qkv_ref, u_ref, o_ref, e_ref, rinv_ref, n1_ref, r1_ref, gd_ref, r2_ref, xall, wat_out, wf_out,
                   xs, n1s, wat, wf, x_sem, xo_sem, wa_sem, wf_sem, own_sem, *sems):
    layer, part = pl.program_id(0), pl.program_id(1)
    step = layer * FORWARD_STEPS + part
    x_in = pltpu.make_async_copy(tok, xs, x_sem.at[0])
    x_out = pltpu.make_async_copy(xs, xall.at[0], x_sem.at[1])

    def save_x(l, b):
        rows = pl.ds(pl.multiple_of(b * BLOCK, BLOCK), BLOCK)
        return pltpu.make_async_copy(xs.at[rows], xall.at[l + 1, rows], xo_sem.at[b])

    def save_attention(l):
        return pltpu.make_async_copy(wat.at[l], wat_out.at[l], wa_sem.at[l])

    def save_ffn(l):
        return pltpu.make_async_copy(wf.at[l], wf_out.at[l], wf_sem.at[l])

    def own_ffn(l):
        return [pltpu.make_async_copy(r.at[l], wf.at[l, 0, m], own_sem.at[l, m]) for m, r in enumerate((ex, pr))]

    if direct:
        place = Place(axes)
        n_att = len(ATT_SEMS)
        n_ffn = len(FFN_SEMS)
        att_sems = [sems[:n_att], sems[n_att:2 * n_att]]
        sems = sems[2 * n_att:]
        ffn_sems = [sems[:n_ffn], sems[n_ffn:]]

        def run(job):
            what, l, *more = job
            if what in ("fy", "fown", "fr", "ffin"):
                ffn_gather(place, l, ex, pr, wf.at[l], ffn_sems[l], what, *more)
            else:
                attention_gather(place, l, att, wat.at[l], att_sems[l], what, *more)
            if what == "fin3":
                save_attention(l).start()
            if what == "ffin":
                save_ffn(l).start()

    @pl.when(step == 0)
    def _():
        x_in.start()
        if direct:
            greet(place, True)
            for l in range(LAYERS):
                for c in own_ffn(l):
                    c.start()
            for job in SCHEDULE[0, 0]:
                run(job)
            for l in range(LAYERS):
                for c in own_ffn(l):
                    c.wait()
        else:
            whole = [pltpu.make_async_copy(att, wat, own_sem.at[0, 0]), pltpu.make_async_copy(ex, wf, own_sem.at[0, 1])]
            for c in whole:
                c.start()
            for c in whole:
                c.wait()
        x_in.wait()
        x_out.start()

    def slot(within):
        for (at, where), jobs in SCHEDULE.items():
            if direct and where == within and (at, where) != (0, 0):
                @pl.when(step == at)
                def _():
                    for job in jobs:
                        run(job)

    slot(0)

    @pl.when(part < ROWS)
    def _():
        attend_unit(part, len_ref[part], xs, wat.at[layer], a_ref.at[layer], b_ref.at[layer], gain_ref[layer, 0:1],
                    qkv_ref, u_ref, o_ref, e_ref, rinv_ref, n1_ref, r1_ref, n1s, lambda pair: slot(pair) if pair else None)

    @pl.when(part >= ROWS)
    def _():
        block = part - ROWS

        @pl.when(step == ROWS)
        def _():
            x_out.wait()

        @pl.when(layer > 0)
        def _():
            save_x(layer - 1, block).wait()

        ffn_unit(block, wf.at[layer], gain_ref[layer, 1:2], n1s, xs, gd_ref, r2_ref)
        save_x(layer, block).start()

    @pl.when(step == LAYERS * FORWARD_STEPS - 1)
    def _():
        for b in range(FFN_STEPS):
            save_x(LAYERS - 1, b).wait()
        if direct:
            for l in range(LAYERS):
                save_attention(l).wait()
                save_ffn(l).wait()


SCHEDULE = {
    (0, 0): [
        ("line", 0, 0), ("fy", 0, 0), ("line", 0, 1), ("fr", 0, 1), ("fy", 0, 1), ("line", 0, 2),
        ("side", 0, 0), ("side", 0, 1), ("side", 0, 2), ("fown", 0), ("line", 0, 3), ("line3", 0),
        ("side", 0, 3), ("line", 1, 0), ("fy", 0, 2), ("fr", 0, 2), ("fy", 0, 3), ("far", 0, 0),
        ("far", 0, 1), ("far", 0, 2), ("far", 0, 3), ("side3", 0), ("fin012", 0), ("line", 1, 1),
        ("line", 1, 2),
    ],
    (0, 2): [
        ("fr", 0, 3), ("side", 1, 0), ("far3", 0), ("line", 1, 3),
    ],
    (0, 4): [
        ("fin3", 0),
    ],
    (1, 0): [
        ("fr", 0, 4), ("fy", 1, 0), ("fr", 0, 5), ("fy", 1, 1), ("fown", 1),
    ],
    (1, 2): [
        ("side", 1, 1), ("side", 1, 2), ("line3", 1), ("far", 1, 0),
    ],
    (1, 4): [
        ("fr", 0, 6), ("fr", 1, 1), ("side", 1, 3),
    ],
    (2, 0): [
        ("fr", 1, 2), ("ffin", 0),
    ],
    (3, 0): [
        ("fy", 1, 2),
    ],
    (5, 0): [
        ("far", 1, 1), ("side3", 1), ("far", 1, 2), ("fy", 1, 3), ("far", 1, 3),
    ],
    (6, 0): [
        ("fr", 1, 3), ("fin012", 1),
    ],
    (6, 2): [
        ("far3", 1),
    ],
    (6, 4): [
        ("fin3", 1), ("fr", 1, 4), ("fr", 1, 5),
    ],
    (7, 2): [
        ("fr", 1, 6),
    ],
    (8, 0): [
        ("ffin", 1),
    ],
}


def forward(axes, direct, lengths, tokens, att, ex, pr, a, b, gains):
    anywhere = pl.BlockSpec(memory_space=pl.ANY)
    row_of = lambda p: jnp.minimum(p, ROWS - 1)
    block_of = lambda p: jnp.maximum(p - ROWS, 0)
    by_row = lambda width: pl.BlockSpec((1, SEQ, width), lambda l, p: (l, row_of(p), 0))
    by_block = lambda width: pl.BlockSpec((1, BLOCK, width), lambda l, p: (l, block_of(p), 0))
    whole = lambda v: pl.BlockSpec(v.shape, lambda l, p: (0,) * v.ndim, pipeline_mode=pl.Buffered(1))
    shape = jax.ShapeDtypeStruct
    dma = pltpu.SemaphoreType.DMA
    return pl.pallas_call(
        functools.partial(forward_kernel, axes, direct),
        grid=(LAYERS, FORWARD_STEPS),
        in_specs=[pl.BlockSpec(memory_space=pltpu.SMEM)] + [anywhere] * 4 + [whole(a), whole(b), whole(gains)],
        out_specs=[
            by_row(3 * WIDTH), by_row(2 * RANK), by_row(WIDTH),
            pl.BlockSpec((1, 1, HEADS, SEQ, SEQ), lambda l, p: (l, row_of(p), 0, 0, 0)),
            pl.BlockSpec((1, 1, HEADS, 8, SEQ), lambda l, p: (l, row_of(p), 0, 0, 0)),
            by_row(WIDTH), by_row(128), by_block(4 * CHUNK), by_block(128), anywhere, anywhere, anywhere,
        ],
        out_shape=[
            shape((LAYERS, TOKENS, 3 * WIDTH), BF), shape((LAYERS, TOKENS, 2 * RANK), BF), shape((LAYERS, TOKENS, WIDTH), BF),
            shape((LAYERS, ROWS, HEADS, SEQ, SEQ), BF), shape((LAYERS, ROWS, HEADS, 8, SEQ), F32),
            shape((LAYERS, TOKENS, WIDTH), BF), shape((LAYERS, TOKENS, 128), F32),
            shape((LAYERS, TOKENS, 4 * CHUNK), BF), shape((LAYERS, TOKENS, 128), F32),
            shape((LAYERS + 1, TOKENS, WIDTH), BF),
            shape((LAYERS, 4 * WIDTH, WIDTH), BF), shape((LAYERS, 4, 2, WIDTH, CHUNK), BF),
        ],
        scratch_shapes=[
            pltpu.VMEM((TOKENS, WIDTH), BF), pltpu.VMEM((TOKENS, WIDTH), BF),
            pltpu.VMEM((LAYERS, 4 * WIDTH, WIDTH), BF), pltpu.VMEM((LAYERS, 4, 2, WIDTH, CHUNK), BF),
            dma((2,)), dma((FFN_STEPS,)), dma((LAYERS,)), dma((LAYERS,)), dma((LAYERS, 2)),
        ] + (ATT_SEMS * 2 + FFN_SEMS * 2 if direct else []),
        compiler_params=params(2, 0 if direct else None),
        name="forward",
    )(lengths, tokens, att, ex, pr, a, b, gains)


def norm_back(e, m, r):
    return r * (e - mean_rows(e) - m * mean_rows(e * m))


def ffn_back_unit(dy, x2_ref, r2_ref, n1_ref, r1_ref, gd_ref, w, wo, gains, wait):
    g1, g2 = gains[0:1], gains[1:2]
    dh2 = norm_back(dy * g2, x2_ref[0].astype(F32) * (1.0 / g2), r2_ref[0, :, 0:1])
    df = dh2.astype(BF)
    dn = dh2
    for j in range(4):
        wait(j)
        dz = (dot_nt(df, w[j, 1]) * gd_ref[0, :, CHUNK * j:CHUNK * (j + 1)].astype(F32)).astype(BF)
        dn = dn + dot_nt(dz, w[j, 0])
    dh = norm_back(dn * g1, n1_ref[0].astype(F32) * (1.0 / g1), r1_ref[0, :, 0:1])
    wait(4)
    return dh, dot_nt(dh.astype(BF), wo[...]).astype(BF)


def attend_back_unit(grp, do_ref, qkv_ref, o_ref, e_ref, rinv_ref, d_ref):
    lane = lax.broadcasted_iota(jnp.int32, (SEQ, 128), 1)
    low = lane < HEAD_DIM
    for pair in range(GROUP // 2):
        at = pl.multiple_of(grp * (GROUP * HEAD_DIM) + pair * 128, 128)
        q = qkv_ref[0, :, pl.ds(at, 128)]
        k = qkv_ref[0, :, pl.ds(WIDTH + at, 128)]
        v = qkv_ref[0, :, pl.ds(2 * WIDTH + at, 128)]
        head = grp * GROUP + pair * 2
        scale = jnp.concatenate([rinv_ref[0, 0, head]] * 8 + [rinv_ref[0, 0, head + 1]] * 8, axis=0).T
        dos = do_ref[:, pl.ds(at, 128)].astype(F32) * scale
        other = pltpu.roll(-dos * o_ref[0, :, pl.ds(at, 128)].astype(F32), HEAD_DIM, 1).astype(BF)
        dos = dos.astype(BF)
        dvs, dks, dqs = [], [], []
        for half in range(2):
            mine = low if half == 0 else ~low
            e = e_ref[0, 0, pair * 2 + half]
            dp = dot_nt(jnp.where(mine, v, jnp.ones_like(v)), jnp.where(mine, dos, other))
            ds = (dp * e.astype(F32)).astype(BF)
            dvs.append(dot(e, dos))
            dks.append(dot(ds, q))
            dqs.append(dot_tn(k, ds)[half * HEAD_DIM:(half + 1) * HEAD_DIM])
        d_ref[:, pl.ds(2 * WIDTH + at, 128)] = jnp.where(low, dvs[0], dvs[1]).astype(BF)
        d_ref[:, pl.ds(WIDTH + at, 128)] = (jnp.where(low, dks[0], dks[1]) * HEAD_DIM ** (-0.5)).astype(BF)
        d_ref[:, pl.ds(at, 128)] = (jnp.concatenate(dqs, axis=0) * HEAD_DIM ** (-0.5)).T.astype(BF)


def split(unit):
    row = sum(jnp.where(unit >= GROUPS * r, 1, 0) for r in range(1, ROWS))
    return row, unit - row * GROUPS


def backward_kernel(cot_ref, x2_ref, r2_ref, n1_ref, r1_ref, gd_ref, x_ref, u_ref, qkv_ref, o_ref, e_ref, rinv_ref,
                    a_ref, b_ref, gain_ref, wat_in, wf_in, xall,
                    dx_ref, grad_ref, hidden,
                    dhs, dos, dys, d_ref, wat, wf, wa_sem, wf_sem, h_sem):
    turn, part = pl.program_id(0), pl.program_id(1)
    layer = LAYERS - 1 - turn
    step = turn * LAYER_STEPS + part
    hidden_copy = pltpu.make_async_copy(xall.at[LAYERS], hidden, h_sem)

    def load_ffn(l, j):
        return pltpu.make_async_copy(wf_in.at[l, j], wf.at[j], wf_sem.at[j])

    def load_attention(l, i):
        rows = pl.ds(3 * WIDTH, WIDTH) if i == 1 else pl.ds(0, 3 * WIDTH)
        return pltpu.make_async_copy(wat_in.at[l, rows], wat.at[l, rows], wa_sem.at[l, i])

    last = LAYERS - 1

    @pl.when(step == 0)
    def _():
        for j in range(4):
            load_ffn(last, j).start()
        load_attention(last, 1).start()
        load_attention(last, 0).start()
        hidden_copy.start()
        grad_ref[...] = jnp.zeros_like(grad_ref)

    for k in range(1, LAYERS):
        @pl.when(step == k * LAYER_STEPS - ATT_STEPS)
        def _():
            for j in range(4):
                load_ffn(last - k, j).start()
            load_attention(last - k, 1).start()
            load_attention(last - k, 0).start()

        @pl.when(step == k * LAYER_STEPS)
        def _():
            for j in range(4):
                load_ffn(last - k, j).wait()
            load_attention(last - k, 1).wait()

        @pl.when(step == k * LAYER_STEPS + FFN_STEPS)
        def _():
            load_attention(last - k, 0).wait()

    @pl.when(step == FFN_STEPS)
    def _():
        load_attention(last, 0).wait()

    def ffn_part(dy, wait):
        here = pl.ds(pl.multiple_of(part * BLOCK, BLOCK), BLOCK)
        dh, do = ffn_back_unit(dy(here), x2_ref, r2_ref, n1_ref, r1_ref, gd_ref, wf, wat.at[layer, 3 * WIDTH:, :],
                               gain_ref[layer], wait)
        dhs[here, :] = dh
        dos[here, :] = do

    def wait_load(j):
        if j < 4:
            load_ffn(last, j).wait()
        else:
            load_attention(last, 1).wait()

    @pl.when(step == 0)
    def _():
        ffn_part(lambda here: cot_ref[...].astype(F32), wait_load)

    @pl.when((step > 0) & (step < FFN_STEPS))
    def _():
        ffn_part(lambda here: cot_ref[...].astype(F32), lambda j: None)

    @pl.when((step >= LAYER_STEPS) & (part < FFN_STEPS))
    def _():
        ffn_part(lambda here: dys[here, :], lambda j: None)

    @pl.when(part >= FFN_STEPS)
    def _():
        row, grp = split(part - FFN_STEPS)
        here = pl.ds(pl.multiple_of(row * SEQ, SEQ), SEQ)
        attend_back_unit(grp, dos.at[here], qkv_ref, o_ref, e_ref, rinv_ref, d_ref)

        @pl.when(grp == GROUPS - 1)
        def _():
            dq, dk, dv = (d_ref[:, WIDTH * i:WIDTH * (i + 1)] for i in range(3))
            du = (dot_nt(dq, b_ref[layer, 0]) + dot_nt(dv, b_ref[layer, 1])).astype(BF)
            u = u_ref[0]
            u2 = u + u
            ga = dot_tn(du, x_ref[0])
            gq = dot_tn(u2, dq)[:RANK]
            gv = dot_tn(u2, dv)[RANK:]
            grad_ref[layer] += jnp.concatenate([ga, gq, gv], axis=0)
            w = wat.at[layer]
            dx = (dhs[here, :] + dot_nt(dq, w[0:WIDTH, :]) + dot_nt(dk, w[WIDTH:2 * WIDTH, :])
                  + dot_nt(dv, w[2 * WIDTH:3 * WIDTH, :]) + dot_nt(du, a_ref[layer]))

            @pl.when(layer > 0)
            def _():
                dys[here, :] = dx

            @pl.when(layer == 0)
            def _():
                dx_ref[...] = dx

    @pl.when(step == LAYERS * LAYER_STEPS - 1)
    def _():
        hidden_copy.wait()


def backward(cot, saved, a, b, gains, wat, wf):
    qkv, u, o, e, rinv, n1, r1, gd, r2, xall = saved
    anywhere = pl.BlockSpec(memory_space=pl.ANY)
    layer_of = lambda t: LAYERS - 1 - t
    block_of = lambda p: jnp.minimum(p, FFN_STEPS - 1)
    unit_of = lambda p: split(jnp.maximum(p - FFN_STEPS, 0))
    row_of = lambda p: unit_of(p)[0]
    by_row = lambda width: pl.BlockSpec((1, SEQ, width), lambda t, p: (layer_of(t), row_of(p), 0))
    by_block = lambda width: pl.BlockSpec((1, BLOCK, width), lambda t, p: (layer_of(t), block_of(p), 0))
    whole = lambda v: pl.BlockSpec(v.shape, lambda t, p: (0,) * v.ndim, pipeline_mode=pl.Buffered(1))
    shape = jax.ShapeDtypeStruct
    dma = pltpu.SemaphoreType.DMA
    return pl.pallas_call(
        backward_kernel,
        grid=(LAYERS, LAYER_STEPS),
        in_specs=[
            pl.BlockSpec((BLOCK, WIDTH), lambda t, p: (jnp.where(t == 0, block_of(p), FFN_STEPS - 1), 0)),
            pl.BlockSpec((1, BLOCK, WIDTH), lambda t, p: (layer_of(t) + 1, block_of(p), 0)),
            by_block(128), by_block(WIDTH), by_block(128), by_block(4 * CHUNK),
            by_row(WIDTH), by_row(2 * RANK), by_row(3 * WIDTH), by_row(WIDTH),
            pl.BlockSpec((1, 1, GROUP, SEQ, SEQ), lambda t, p: (layer_of(t), *unit_of(p), 0, 0)),
            pl.BlockSpec((1, 1, HEADS, 8, SEQ), lambda t, p: (layer_of(t), row_of(p), 0, 0, 0)),
            whole(a), whole(b), whole(gains), anywhere, anywhere, anywhere,
        ],
        out_specs=[
            pl.BlockSpec((SEQ, WIDTH), lambda t, p: (jnp.where(t < LAYERS - 1, 0, row_of(p)), 0)),
            pl.BlockSpec((LAYERS, 4 * RANK, WIDTH), lambda t, p: (0, 0, 0)),
            anywhere,
        ],
        out_shape=[shape((TOKENS, WIDTH), F32), shape((LAYERS, 4 * RANK, WIDTH), F32), shape((TOKENS, WIDTH), BF)],
        scratch_shapes=[
            pltpu.VMEM((TOKENS, WIDTH), F32), pltpu.VMEM((TOKENS, WIDTH), BF), pltpu.VMEM((TOKENS, WIDTH), F32),
            pltpu.VMEM((SEQ, 3 * WIDTH), BF), pltpu.VMEM((LAYERS, 4 * WIDTH, WIDTH), BF),
            pltpu.VMEM((4, 2, WIDTH, CHUNK), BF),
            dma((LAYERS, 2)), dma((4,)), dma,
        ],
        compiler_params=params(2),
        name="backward",
    )(cot, xall, r2, n1, r1, gd, xall, u, qkv, o, e, rinv, a, b, gains, wat, wf, xall)


def local(axes, direct, tokens, lengths, attention, down, up, expand, project, gains, cotangent):
    a = jnp.concatenate([down[:, 0], down[:, 1]], axis=2)
    twice = up + up
    b = jnp.stack([jnp.pad(twice[:, 0], ((0, 0), (0, RANK), (0, 0))), jnp.pad(twice[:, 1], ((0, 0), (RANK, 0), (0, 0)))],
                  axis=1)
    if direct:
        att, ex, pr = attention, expand, project
    else:
        att = lax.all_gather(attention, axes, axis=1, tiled=True)
        w1 = lax.all_gather(expand, axes[1], axis=2, tiled=True).reshape(LAYERS, WIDTH, 4, CHUNK).transpose(0, 2, 1, 3)
        w2 = lax.all_gather(project, axes[1], axis=1, tiled=True).reshape(LAYERS, 4, CHUNK, WIDTH)
        ex = pr = jnp.stack([w1, w2], axis=2)
    *saved, wat, wf = forward(axes, direct, lengths, tokens, att, ex, pr, a, b, gains)
    if not direct:
        wat, wf = att, ex
    dx, grads, hidden = backward(cotangent, saved, a, b, gains, wat, wf)
    if direct:
        total = all_sum(axes, grads.reshape(32, -1, 128), 1).reshape(grads.shape)
    else:
        total = lax.psum(grads, axes)
    a_grad = total[:, :2 * RANK].reshape(LAYERS, 2, RANK, WIDTH).transpose(0, 1, 3, 2)
    b_grad = total[:, 2 * RANK:].reshape(LAYERS, 2, RANK, WIDTH)
    return hidden, dx, a_grad, b_grad


def solution(mesh):
    axes = tuple(mesh.axis_names)
    dp, tensor = axes
    direct = mesh.shape[dp] == 2 * Z_SIZE and mesh.shape[tensor] == 4
    placed = (
        P(axes, None), P(axes), P(None, axes, None), P(), P(),
        P(None, None, tensor), P(None, tensor, None), P(), P(axes, None),
    )
    return jax.shard_map(
        functools.partial(local, axes, direct),
        mesh=mesh,
        in_specs=placed,
        out_specs=(P(axes, None), P(axes, None), P(), P()),
        check_vma=False,
    )
```

```python
import functools
import jax
import jax.numpy as jnp
from jax import lax
from jax.experimental import pallas as pl
from jax.experimental.pallas import tpu as pltpu
from jax.sharding import PartitionSpec as P

WIDTH = 768
HEADS = 12
HEAD_DIM = 64
SEQ = 512
RANK = 8
EPS = 1e-05
CHUNK = 768
BF = jnp.bfloat16
F32 = jnp.float32
VMEM_LIMIT = 60 * 1024 * 1024
EXP2_SCALE = 1.4426950408889634 * HEAD_DIM ** (-0.5)


def dot(a, b):
    return jnp.dot(a, b, preferred_element_type=F32)


def dot_nt(a, b):
    return lax.dot_general(a, b, (((1,), (1,)), ((), ())), preferred_element_type=F32)


def dot_tn(a, b):
    return lax.dot_general(a, b, (((0,), (0,)), ((), ())), preferred_element_type=F32)


def mean_rows(v):
    return jnp.sum(v, axis=-1, keepdims=True) * (1.0 / WIDTH)


def params(n, collective=None):
    more = {} if collective is None else {"collective_id": collective, "has_side_effects": True}
    return pltpu.CompilerParams(
        dimension_semantics=("arbitrary",) * n, vmem_limit_bytes=VMEM_LIMIT, **more
    )


MESH = pl.DeviceIdType.MESH
Z_SIZE = 4


class Place:
    def __init__(self, axes):
        dp, t = lax.axis_index(axes[0]), lax.axis_index(axes[1])
        self.dp, self.t = dp, t
        self.z, self.x = dp // 2, dp % 2
        self.y, self.core = t // 2, t % 2
        self.to_core = (dp, t + 1 - 2 * self.core)
        self.to_y = (dp, t + 2 - 4 * self.y)
        self.to_x = (dp + 1 - 2 * self.x, t)
        self.to_zpair = (dp + 2 - 4 * (self.z % 2), t)
        self.to_up = (dp + 2, t)
        self.to_down = (dp - 2, t)


def greet(place, line):
    barrier = pltpu.get_barrier_semaphore()
    for device in (place.to_core, place.to_y, place.to_x):
        pl.semaphore_signal(barrier, inc=1, device_id=device, device_id_type=MESH)
    if line:
        @pl.when(place.z < Z_SIZE - 1)
        def _():
            pl.semaphore_signal(barrier, inc=1, device_id=place.to_up, device_id_type=MESH)

        @pl.when(place.z > 0)
        def _():
            pl.semaphore_signal(barrier, inc=1, device_id=place.to_down, device_id_type=MESH)

        inner = (place.z > 0) & (place.z < Z_SIZE - 1)

        @pl.when(inner)
        def _():
            pl.semaphore_wait(barrier, 5)

        @pl.when(jnp.logical_not(inner))
        def _():
            pl.semaphore_wait(barrier, 4)
    else:
        pl.semaphore_signal(barrier, inc=1, device_id=place.to_zpair, device_id_type=MESH)
        pl.semaphore_wait(barrier, 4)


def remote(src, dst, send, recv, device):
    return pltpu.make_async_remote_copy(
        src_ref=src, dst_ref=dst, send_sem=send, recv_sem=recv, device_id=device, device_id_type=MESH
    )


SLICE = 128
FFN_SEMS = [
    pltpu.SemaphoreType.DMA((3, 4)),
    pltpu.SemaphoreType.DMA((12,)),
    pltpu.SemaphoreType.DMA((14,)),
    pltpu.SemaphoreType.DMA((14,)),
]


def ffn_gather(place, layer, w1, w2, out, sems, what, tick=0):
    send, recv, core_send, core_recv = sems
    g = place.x * 2 + place.z % 2
    gd = 3 - g
    gx = (1 - place.x) * 2 + place.z % 2
    gz = place.x * 2 + 1 - place.z % 2

    def spot(slot, s):
        return out.at[slot + 1, s // 6, pl.ds(pl.multiple_of((s % 6) * SLICE, SLICE), SLICE)]

    def over_y(i):
        s = 3 * g + i if i < 3 else 3 * gd
        first = place.x == (0 if i < 3 else 1)
        for here, ref in ((first, w1), (jnp.logical_not(first), w2)):
            @pl.when(here)
            def _():
                src = ref.at[layer, pl.ds(pl.multiple_of((s % 6) * SLICE, SLICE), SLICE)]
                remote(src, spot(1, s), send.at[0, i], recv.at[s], place.to_y).start()

    def arrived(s):
        remote(spot(1, s), spot(1, s), send.at[0, 0], recv.at[s], place.to_y).wait_recv()

    def over(way, i, s):
        device = place.to_x if way == 1 else place.to_zpair
        remote(spot(1, s), spot(1, s), send.at[way, i], recv.at[s], device).start()

    def share(s):
        remote(spot(1, s), spot(2, s), core_send.at[s], core_recv.at[s], place.to_core).start()

    if what == "fy":
        over_y(tick)
    elif what == "fown":
        for m, ref in enumerate((w1, w2)):
            remote(ref.at[layer], out.at[1, m], core_send.at[12 + m], core_recv.at[12 + m], place.to_core).start()
    elif what == "fownin":
        for m, ref in enumerate((w1, w2)):
            remote(ref.at[layer], out.at[1, m], core_send.at[12 + m], core_recv.at[12 + m], place.to_core).wait()
    elif what == "fr" and tick < 4:
        s = 3 * g + tick - 1
        arrived(s)
        over(1, tick - 1, s)
        over(2, tick - 1, s)
        share(s)
        if tick == 3:
            for s in (3 * gx, 3 * gz):
                arrived(s)
                share(s)
    elif what == "fr" and tick == 4:
        s = 3 * gz + 1
        arrived(s)
        over(1, 3, s)
        share(s)
        for s in (3 * gd, 3 * gx + 1):
            arrived(s)
            share(s)
    elif what == "fr" and tick == 5:
        s = 3 * gx + 2
        arrived(s)
        over(2, 3, s)
        share(s)
        s = 3 * gz + 2
        arrived(s)
        share(s)
    elif what == "fr" and tick == 6:
        for s in (3 * gd + 1, 3 * gd + 2):
            arrived(s)
            share(s)
    else:
        for s in range(12):
            remote(spot(1, s), spot(2, s), core_send.at[s], core_recv.at[s], place.to_core).wait()
        for way in range(3):
            for i in range(4):
                remote(spot(1, 0), spot(1, 0), send.at[way, i], recv.at[0], place.to_y).wait_send()


ATT_SEMS = [
    pltpu.SemaphoreType.DMA((2, 4)),
    pltpu.SemaphoreType.DMA((4,)),
    pltpu.SemaphoreType.DMA((2, 4)),
    pltpu.SemaphoreType.DMA((2, 4)),
    pltpu.SemaphoreType.DMA((2, 4)),
    pltpu.SemaphoreType.DMA((2, 4)),
    pltpu.SemaphoreType.DMA((5, 4)),
    pltpu.SemaphoreType.DMA((5, 4)),
    pltpu.SemaphoreType.DMA,
]


def attention_gather(place, layer, block, out, sems, what, d=0):
    z_send, z_recv, n_send, n_recv, h_send, h_recv, c_send, c_recv, own_sem = sems
    rows = block.shape[1]
    half = rows // 2
    z, x, y, core = place.z, place.x, place.y, place.core
    late = Z_SIZE - 1

    def spot(sz, sx, sy, sc, start=0, size=rows):
        at = ((sz * 2 + sx) * 4 + sy * 2 + sc) * rows + start
        return out.at[pl.ds(pl.multiple_of(at, 16), size)]

    def line(sz):
        return spot(sz, x, y, core)

    def side(way, sz):
        return spot(sz, 1 - x, y, core) if way == 0 else spot(sz, x, 1 - y, core)

    def far(way, sz):
        return spot(sz, 1 - x, 1 - y, core, way * half, half)

    devices = (place.to_x, place.to_y)

    def at_distance(d, action, size):
        if d == 0:
            @pl.when(z < size)
            def _():
                action(z)

            return

        @pl.when(z >= d)
        def _():
            action(z - d)

        @pl.when(z + d < size)
        def _():
            action(z + d)

    def line_step(sz, own):
        mine = block.at[layer] if own else line(sz)
        if not own:
            remote(line(sz), line(sz), z_send.at[0, sz], z_recv.at[sz], place.to_core).wait_recv()

        @pl.when((sz <= z) & (z < Z_SIZE - 1))
        def _():
            remote(mine, line(sz), z_send.at[0, sz], z_recv.at[sz], place.to_up).start()

        @pl.when((sz >= z) & (z > 0))
        def _():
            remote(mine, line(sz), z_send.at[1, sz], z_recv.at[sz], place.to_down).start()

        if own:
            @pl.when(sz < late)
            def _():
                spread(sz, mine)
        else:
            @pl.when(sz < late)
            def _():
                spread(sz, line(sz))

    def spread(sz, mine):
        for way in range(2):
            remote(mine, line(sz), n_send.at[way, sz], n_recv.at[way, sz], devices[way]).start()
        remote(mine, line(sz), c_send.at[0, sz], c_recv.at[0, sz], place.to_core).start()

    def side_step(sz):
        for way in range(2):
            remote(side(way, sz), side(way, sz), n_send.at[way, sz], n_recv.at[way, sz], devices[way]).wait_recv()
            at = spot(sz, 1 - x, y, core, 0, half) if way == 0 else spot(sz, x, 1 - y, core, half, half)
            remote(at, at, h_send.at[way, sz], h_recv.at[way, sz], devices[1 - way]).start()
            remote(side(way, sz), side(way, sz), c_send.at[1 + way, sz], c_recv.at[1 + way, sz], place.to_core).start()

    def far_step(sz):
        for way in range(2):
            remote(far(way, sz), far(way, sz), h_send.at[way, sz], h_recv.at[way, sz], place.to_core).wait_recv()
            remote(far(way, sz), far(way, sz), c_send.at[3 + way, sz], c_recv.at[3 + way, sz], place.to_core).start()

    def finish(sz):
        @pl.when((sz <= z) & (z < Z_SIZE - 1))
        def _():
            remote(line(sz), line(sz), z_send.at[0, sz], z_recv.at[sz], place.to_core).wait_send()

        @pl.when((sz >= z) & (z > 0))
        def _():
            remote(line(sz), line(sz), z_send.at[1, sz], z_recv.at[sz], place.to_core).wait_send()

        for way in range(2):
            remote(line(sz), line(sz), n_send.at[way, sz], n_recv.at[way, sz], place.to_core).wait_send()
            remote(far(way, sz), far(way, sz), h_send.at[way, sz], h_recv.at[way, sz], place.to_core).wait_send()
        parts = (
            (line(sz), spot(sz, x, y, 1 - core)),
            (side(0, sz), spot(sz, 1 - x, y, 1 - core)),
            (side(1, sz), spot(sz, x, 1 - y, 1 - core)),
            (far(0, sz), spot(sz, 1 - x, 1 - y, 1 - core, 0, half)),
            (far(1, sz), spot(sz, 1 - x, 1 - y, 1 - core, half, half)),
        )
        for i, (mine, theirs) in enumerate(parts):
            remote(mine, theirs, c_send.at[i, sz], c_recv.at[i, sz], place.to_core).wait()

    own_copy = pltpu.make_async_copy(block.at[layer], line(z), own_sem)
    if what == "line":
        if d == 0:
            own_copy.start()
        at_distance(d, functools.partial(line_step, own=d == 0), Z_SIZE)
    if what == "side":
        at_distance(d, side_step, late)
    if what == "far":
        at_distance(d, far_step, late)
    if what == "fin012":
        own_copy.wait()
        for sz in range(late):
            finish(sz)
    if what == "line3":
        @pl.when(z == late)
        def _():
            spread(late, block.at[layer])

        @pl.when(z < late)
        def _():
            spread(late, line(late))
    if what == "side3":
        side_step(late)
    if what == "far3":
        far_step(late)
    if what == "fin3":
        finish(late)


def all_sum(axes, values, collective):
    layers, high, wide = values.shape
    tiles = high // 8
    owners = layers * tiles
    chips = 4 * Z_SIZE
    half = wide // 2

    def kernel(v_ref, out_ref, sums, box, other_half, core_sem, send, recv, send2, recv2):
        place = Place(axes)
        core = place.core
        me = place.dp * 2 + place.y
        barrier = pltpu.get_barrier_semaphore()
        mine = pl.ds(pl.multiple_of(core * half, 128), half)
        theirs = pl.ds(pl.multiple_of((1 - core) * half, 128), half)

        def chip(i):
            other = lax.rem(me + i, chips)
            return other, (other // 2, (other % 2) * 2 + core)

        def owner(k):
            z, x = k // 2, k % 2
            return k * 2 + (z + x) % 2, (k, (z + x) % 2 * 2 + core)

        my_part = place.dp
        is_owner = place.y == (place.z + place.x) % 2

        def part(ref, k, columns):
            return ref.at[k // tiles, pl.ds(pl.multiple_of(k % tiles * 8, 8), 8), columns]

        def signal(i, _):
            pl.semaphore_signal(barrier, inc=1, device_id=chip(i)[1], device_id_type=MESH)
            return 0

        pl.semaphore_signal(barrier, inc=1, device_id=place.to_core, device_id_type=MESH)
        lax.fori_loop(1, chips, signal, 0)
        pl.semaphore_wait(barrier, chips)
        swap = remote(v_ref.at[:, :, theirs], other_half, core_sem.at[0], core_sem.at[1], place.to_core)
        swap.start()
        swap.wait()
        sums[...] = v_ref[:, :, mine] + other_half[...]

        def to_owner(k, act):
            who, device = owner(k)

            @pl.when(who != me)
            def _():
                act(remote(part(sums, k, slice(None)), box.at[me], send.at[k], recv.at[me], device))

            return 0

        lax.fori_loop(0, owners, lambda k, _: to_owner(k, lambda c: c.start()), 0)

        def collect(i, _):
            other, device = chip(i)
            remote(box.at[other], box.at[other], send.at[0], recv.at[other], device).wait_recv()
            return 0

        def to_all(i, act):
            other, device = chip(i)
            spot = part(out_ref, my_part, mine)
            act(remote(spot, spot, send2.at[i], recv2.at[my_part], device))
            return 0

        @pl.when(is_owner)
        def _():
            lax.fori_loop(1, chips, collect, 0)
            at = pl.ds(pl.multiple_of(my_part % tiles * 8, 8), 8)
            box[me] = sums[my_part // tiles, at, :]
            out_ref[my_part // tiles, at, mine] = jnp.sum(box[...], axis=0)
            lax.fori_loop(1, chips, lambda i, _: to_all(i, lambda c: c.start()), 0)

        def arrived(k, _):
            who, device = owner(k)

            @pl.when(who != me)
            def _():
                spot = part(out_ref, k, mine)
                remote(spot, spot, send2.at[0], recv2.at[k], device).wait_recv()

            return 0

        lax.fori_loop(0, owners, arrived, 0)
        swap = remote(out_ref.at[:, :, mine], out_ref.at[:, :, mine], core_sem.at[2], core_sem.at[3], place.to_core)
        swap.start()
        lax.fori_loop(0, owners, lambda k, _: to_owner(k, lambda c: c.wait_send()), 0)

        @pl.when(is_owner)
        def _():
            lax.fori_loop(1, chips, lambda i, _: to_all(i, lambda c: c.wait_send()), 0)

        swap.wait_send()
        remote(out_ref.at[:, :, theirs], out_ref.at[:, :, theirs], core_sem.at[2], core_sem.at[3], place.to_core).wait_recv()

    dma = pltpu.SemaphoreType.DMA
    return pl.pallas_call(
        kernel,
        in_specs=[pl.BlockSpec(memory_space=pltpu.VMEM)],
        out_specs=pl.BlockSpec(memory_space=pltpu.VMEM),
        out_shape=jax.ShapeDtypeStruct(values.shape, F32),
        scratch_shapes=[
            pltpu.VMEM((layers, high, half), F32), pltpu.VMEM((chips, 8, half), F32), pltpu.VMEM((layers, high, half), F32),
            dma((4,)), dma((owners,)), dma((chips,)), dma((chips,)), dma((owners,)),
        ],
        compiler_params=pltpu.CompilerParams(collective_id=collective, has_side_effects=True),
        name="all_sum",
    )(values)


GROUP = 6
BLOCK = 256
GROUPS = HEADS // GROUP
TOKENS = 1024
ROWS = TOKENS // SEQ
ATT_STEPS = ROWS * GROUPS
FFN_STEPS = TOKENS // BLOCK
LAYER_STEPS = ATT_STEPS + FFN_STEPS
WIDE = 512
WIDE_STEPS = TOKENS // WIDE
FORWARD_STEPS = ROWS + 2 * WIDE_STEPS
LAYERS = 2


def norm_parts(v):
    c = v - mean_rows(v)
    r = lax.rsqrt(mean_rows(c * c) + EPS)
    return c * r, r


def attend_unit(row, length, xs, w, a, b, gain, qkv_ref, u_ref, o_ref, e_ref, rinv_ref, n1_ref, r1_ref, n1s, slot):
    here = pl.ds(pl.multiple_of(row * SEQ, SEQ), SEQ)
    x = xs[here, :]
    u = dot(x, a[...]).astype(BF)
    u_ref[0] = u
    for i in range(3):
        acc = dot(x, w[WIDTH * i:WIDTH * (i + 1), :])
        if i != 1:
            acc += dot(u, b[i // 2])
        qkv_ref[0, :, WIDTH * i:WIDTH * (i + 1)] = acc.astype(BF)
    key = lax.broadcasted_iota(jnp.int32, (SEQ, 128), 0)
    bound = jnp.where(key < length, 3.0e38, -8.0e9)
    lane = lax.broadcasted_iota(jnp.int32, (SEQ, 128), 1)
    low = lane < HEAD_DIM
    bound = jnp.concatenate([bound] * 4, axis=1)
    for pair in range(HEADS // 2):
        slot(pair)
        at = pair * 128
        q = qkv_ref[0, :, at:at + 128]
        k = qkv_ref[0, :, WIDTH + at:WIDTH + at + 128]
        v = qkv_ref[0, :, 2 * WIDTH + at:2 * WIDTH + at + 128]
        outs = []
        for half in range(2):
            mine = low if half == 0 else ~low
            qh = jnp.where(mine, q, jnp.zeros_like(q))
            vh = jnp.where(mine, v, jnp.ones_like(v))
            s = jnp.minimum(dot_nt(k, qh), bound)
            top = jnp.max(s, axis=0, keepdims=True)
            e = jnp.exp2((s - top) * EXP2_SCALE).astype(BF)
            e_ref[0, 0, pair * 2 + half] = e
            ot = dot_tn(vh, e)
            if half == 0:
                o_t, l = ot[:HEAD_DIM], ot[HEAD_DIM:HEAD_DIM + 8]
            else:
                o_t, l = ot[HEAD_DIM:], ot[0:8]
            r = 1.0 / l
            rinv_ref[0, 0, pair * 2 + half] = r
            outs.append(o_t * r[0:1])
        both = jnp.concatenate(outs, axis=0)
        o_ref[0, :, at:at + 128] = both.T.astype(BF)
    slot(HEADS // 2)
    m, r = norm_parts(xs[here, :].astype(F32) + dot(o_ref[0], w[3 * WIDTH:, :]))
    n1 = (m * gain).astype(BF)
    n1_ref[0] = n1
    n1s[here, :] = n1
    r1_ref[0] = jnp.broadcast_to(r, (SEQ, 128))


def ffn_unit(n1, f, chunks, w, gd_ref):
    for i, j in enumerate(chunks):
        z = dot(n1, w[j, 0])
        cdf = 0.5 + 0.5 * lax.erf(z * 0.7071067811865476)
        pdf = jnp.exp2(z * (z * (-0.5 * 1.4426950408889634))) * 0.3989422804014327
        gd_ref[0, :, CHUNK * i:CHUNK * (i + 1)] = (cdf + z * pdf).astype(BF)
        f = f + dot((z * cdf).astype(BF), w[j, 1])
    return f


def forward_kernel(axes, direct, len_ref, tok, att, ex, pr, a_ref, b_ref, gain_ref,
                   qkv_ref, u_ref, o_ref, e_ref, rinv_ref, n1_ref, r1_ref, gd_ref, r2_ref, xall, wat_out, wf_out,
                   xs, n1s, fs, wat, wf, x_sem, xo_sem, wa_sem, wf_sem, own_sem, *sems):
    layer, part = pl.program_id(0), pl.program_id(1)
    step = layer * FORWARD_STEPS + part
    x_in = pltpu.make_async_copy(tok, xs, x_sem.at[0])
    x_out = pltpu.make_async_copy(xs, xall.at[0], x_sem.at[1])

    def save_x(l, b):
        rows = pl.ds(pl.multiple_of(b * WIDE, WIDE), WIDE)
        return pltpu.make_async_copy(xs.at[rows], xall.at[l + 1, rows], xo_sem.at[b])

    def save_attention(l):
        return pltpu.make_async_copy(wat.at[l], wat_out.at[l], wa_sem.at[l])

    def save_ffn(l):
        return pltpu.make_async_copy(wf.at[l], wf_out.at[l], wf_sem.at[l])

    def own_ffn(l):
        return [pltpu.make_async_copy(r.at[l], wf.at[l, 0, m], own_sem.at[l, m]) for m, r in enumerate((ex, pr))]

    if direct:
        place = Place(axes)
        n_att = len(ATT_SEMS)
        n_ffn = len(FFN_SEMS)
        att_sems = [sems[:n_att], sems[n_att:2 * n_att]]
        sems = sems[2 * n_att:]
        ffn_sems = [sems[:n_ffn], sems[n_ffn:]]

        def run(job):
            what, l, *more = job
            if what in ("fy", "fown", "fownin", "fr", "ffin"):
                ffn_gather(place, l, ex, pr, wf.at[l], ffn_sems[l], what, *more)
            else:
                attention_gather(place, l, att, wat.at[l], att_sems[l], what, *more)
            if what == "fin3":
                save_attention(l).start()
            if what == "ffin":
                save_ffn(l).start()

    @pl.when(step == 0)
    def _():
        x_in.start()
        if direct:
            greet(place, True)
            for l in range(LAYERS):
                for c in own_ffn(l):
                    c.start()
            for job in SCHEDULE[0, 0]:
                run(job)
            for l in range(LAYERS):
                for c in own_ffn(l):
                    c.wait()
        else:
            whole = [pltpu.make_async_copy(att, wat, own_sem.at[0, 0]), pltpu.make_async_copy(ex, wf, own_sem.at[0, 1])]
            for c in whole:
                c.start()
            for c in whole:
                c.wait()
        x_in.wait()
        x_out.start()

    def slot(within):
        for (at, where), jobs in SCHEDULE.items():
            if direct and where == within and (at, where) != (0, 0):
                @pl.when(step == at)
                def _():
                    for job in jobs:
                        run(job)

    slot(0)

    @pl.when(part < ROWS)
    def _():
        attend_unit(part, len_ref[part], xs, wat.at[layer], a_ref.at[layer], b_ref.at[layer], gain_ref[layer, 0:1],
                    qkv_ref, u_ref, o_ref, e_ref, rinv_ref, n1_ref, r1_ref, n1s, lambda pair: slot(pair) if pair else None)

    @pl.when((part >= ROWS) & (part < ROWS + WIDE_STEPS))
    def _():
        @pl.when(step == ROWS)
        def _():
            x_out.wait()

        here = pl.ds(pl.multiple_of((part - ROWS) * WIDE, WIDE), WIDE)
        n1 = n1s[here, :]
        fs[here, :] = ffn_unit(n1, n1.astype(F32), (0, 1), wf.at[layer], gd_ref)

    @pl.when(part >= ROWS + WIDE_STEPS)
    def _():
        block = part - ROWS - WIDE_STEPS

        @pl.when(layer > 0)
        def _():
            save_x(layer - 1, block).wait()

        here = pl.ds(pl.multiple_of(block * WIDE, WIDE), WIDE)
        m, r = norm_parts(ffn_unit(n1s[here, :], fs[here, :], (2, 3), wf.at[layer], gd_ref))
        xs[here, :] = (m * gain_ref[layer, 1:2]).astype(BF)
        r2_ref[0] = jnp.broadcast_to(r, (WIDE, 128))
        save_x(layer, block).start()

    @pl.when(step == LAYERS * FORWARD_STEPS - 1)
    def _():
        for b in range(WIDE_STEPS):
            save_x(LAYERS - 1, b).wait()
        if direct:
            for l in range(LAYERS):
                save_attention(l).wait()
                save_ffn(l).wait()


SCHEDULE = {
    (0, 0): [
        ("line", 0, 0), ("fown", 1), ("fy", 0, 0), ("line", 0, 1), ("side", 0, 0), ("line", 0, 2),
        ("fown", 0), ("side", 0, 1), ("line", 0, 3), ("far", 0, 0), ("line3", 0), ("side", 0, 2),
        ("side", 0, 3), ("line", 1, 0), ("side3", 0), ("fy", 0, 1), ("far", 0, 1), ("fy", 0, 2), ("fy", 0, 3),
        ("line", 1, 1), ("far", 0, 2), ("far", 0, 3), ("fin012", 0), ("fr", 0, 1),
    ],
    (0, 2): [
        ("fownin", 0), ("far3", 0), ("fr", 0, 2),
    ],
    (0, 4): [
        ("line", 1, 2), ("fy", 1, 0), ("fin3", 0),
    ],
    (1, 0): [
        ("fr", 0, 3),
    ],
    (1, 2): [
        ("side", 1, 0), ("fr", 0, 4),
    ],
    (1, 4): [
        ("line", 1, 3), ("side", 1, 1), ("fr", 0, 5),
    ],
    (2, 0): [
        ("fownin", 1), ("side", 1, 2),
    ],
    (3, 0): [
        ("fr", 0, 6),
    ],
    (4, 0): [
        ("side", 1, 3), ("line3", 1), ("ffin", 0),
    ],
    (5, 0): [
        ("far", 1, 0), ("far", 1, 1), ("far", 1, 2), ("far", 1, 3), ("fy", 1, 1), ("fr", 1, 1),
    ],
    (6, 0): [
        ("side3", 1), ("fin012", 1), ("fy", 1, 2),
    ],
    (6, 2): [
        ("fy", 1, 3), ("fr", 1, 2), ("far3", 1),
    ],
    (6, 4): [
        ("fin3", 1),
    ],
    (7, 0): [
        ("fr", 1, 3),
    ],
    (7, 4): [
        ("fr", 1, 4), ("fr", 1, 5),
    ],
    (9, 0): [
        ("fr", 1, 6),
    ],
    (10, 0): [
        ("ffin", 1),
    ],
}


def forward(axes, direct, lengths, tokens, att, ex, pr, a, b, gains):
    anywhere = pl.BlockSpec(memory_space=pl.ANY)
    row_of = lambda p: jnp.minimum(p, ROWS - 1)
    by_row = lambda width: pl.BlockSpec((1, SEQ, width), lambda l, p: (l, row_of(p), 0))
    def half_of(p):
        i = jnp.maximum(p - ROWS, 0)
        half = jnp.where(i >= WIDE_STEPS, 1, 0)
        return i - half * WIDE_STEPS, half

    whole = lambda v: pl.BlockSpec(v.shape, lambda l, p: (0,) * v.ndim, pipeline_mode=pl.Buffered(1))
    shape = jax.ShapeDtypeStruct
    dma = pltpu.SemaphoreType.DMA
    return pl.pallas_call(
        functools.partial(forward_kernel, axes, direct),
        grid=(LAYERS, FORWARD_STEPS),
        in_specs=[pl.BlockSpec(memory_space=pltpu.SMEM)] + [anywhere] * 4 + [whole(a), whole(b), whole(gains)],
        out_specs=[
            by_row(3 * WIDTH), by_row(2 * RANK), by_row(WIDTH),
            pl.BlockSpec((1, 1, HEADS, SEQ, SEQ), lambda l, p: (l, row_of(p), 0, 0, 0)),
            pl.BlockSpec((1, 1, HEADS, 8, SEQ), lambda l, p: (l, row_of(p), 0, 0, 0)),
            by_row(WIDTH), by_row(128),
            pl.BlockSpec((1, WIDE, 2 * CHUNK), lambda l, p: (l, *half_of(p))),
            pl.BlockSpec((1, WIDE, 128), lambda l, p: (l, jnp.maximum(p - ROWS - WIDE_STEPS, 0), 0)),
            anywhere, anywhere, anywhere,
        ],
        out_shape=[
            shape((LAYERS, TOKENS, 3 * WIDTH), BF), shape((LAYERS, TOKENS, 2 * RANK), BF), shape((LAYERS, TOKENS, WIDTH), BF),
            shape((LAYERS, ROWS, HEADS, SEQ, SEQ), BF), shape((LAYERS, ROWS, HEADS, 8, SEQ), F32),
            shape((LAYERS, TOKENS, WIDTH), BF), shape((LAYERS, TOKENS, 128), F32),
            shape((LAYERS, TOKENS, 4 * CHUNK), BF), shape((LAYERS, TOKENS, 128), F32),
            shape((LAYERS + 1, TOKENS, WIDTH), BF),
            shape((LAYERS, 4 * WIDTH, WIDTH), BF), shape((LAYERS, 4, 2, WIDTH, CHUNK), BF),
        ],
        scratch_shapes=[
            pltpu.VMEM((TOKENS, WIDTH), BF), pltpu.VMEM((TOKENS, WIDTH), BF), pltpu.VMEM((TOKENS, WIDTH), F32),
            pltpu.VMEM((LAYERS, 4 * WIDTH, WIDTH), BF), pltpu.VMEM((LAYERS, 4, 2, WIDTH, CHUNK), BF),
            dma((2,)), dma((WIDE_STEPS,)), dma((LAYERS,)), dma((LAYERS,)), dma((LAYERS, 2)),
        ] + (ATT_SEMS * 2 + FFN_SEMS * 2 if direct else []),
        compiler_params=params(2, 0 if direct else None),
        name="forward",
    )(lengths, tokens, att, ex, pr, a, b, gains)


def norm_back(e, m, r):
    return r * (e - mean_rows(e) - m * mean_rows(e * m))


def ffn_back_unit(dy, x2_ref, r2_ref, n1_ref, r1_ref, gd_ref, w, wo, gains, wait):
    g1, g2 = gains[0:1], gains[1:2]
    dh2 = norm_back(dy * g2, x2_ref[0].astype(F32) * (1.0 / g2), r2_ref[0, :, 0:1])
    df = dh2.astype(BF)
    dn = dh2
    for j in range(4):
        wait(j)
        dz = (dot_nt(df, w[j, 1]) * gd_ref[0, :, CHUNK * j:CHUNK * (j + 1)].astype(F32)).astype(BF)
        dn = dn + dot_nt(dz, w[j, 0])
    dh = norm_back(dn * g1, n1_ref[0].astype(F32) * (1.0 / g1), r1_ref[0, :, 0:1])
    wait(4)
    return dh, dot_nt(dh.astype(BF), wo[...]).astype(BF)


def attend_back_unit(grp, do_ref, qkv_ref, o_ref, e_ref, rinv_ref, d_ref):
    lane = lax.broadcasted_iota(jnp.int32, (SEQ, 128), 1)
    low = lane < HEAD_DIM
    for pair in range(GROUP // 2):
        at = pl.multiple_of(grp * (GROUP * HEAD_DIM) + pair * 128, 128)
        q = qkv_ref[0, :, pl.ds(at, 128)]
        k = qkv_ref[0, :, pl.ds(WIDTH + at, 128)]
        v = qkv_ref[0, :, pl.ds(2 * WIDTH + at, 128)]
        head = grp * GROUP + pair * 2
        scale = jnp.concatenate([rinv_ref[0, 0, head]] * 8 + [rinv_ref[0, 0, head + 1]] * 8, axis=0).T
        dos = do_ref[:, pl.ds(at, 128)].astype(F32) * scale
        other = pltpu.roll(-dos * o_ref[0, :, pl.ds(at, 128)].astype(F32), HEAD_DIM, 1).astype(BF)
        dos = dos.astype(BF)
        dvs, dks, dqs = [], [], []
        for half in range(2):
            mine = low if half == 0 else ~low
            e = e_ref[0, 0, pair * 2 + half]
            dp = dot_nt(jnp.where(mine, v, jnp.ones_like(v)), jnp.where(mine, dos, other))
            ds = (dp * e.astype(F32)).astype(BF)
            dvs.append(dot(e, dos))
            dks.append(dot(ds, q))
            dqs.append(dot_tn(k, ds)[half * HEAD_DIM:(half + 1) * HEAD_DIM])
        d_ref[:, pl.ds(2 * WIDTH + at, 128)] = jnp.where(low, dvs[0], dvs[1]).astype(BF)
        d_ref[:, pl.ds(WIDTH + at, 128)] = (jnp.where(low, dks[0], dks[1]) * HEAD_DIM ** (-0.5)).astype(BF)
        d_ref[:, pl.ds(at, 128)] = (jnp.concatenate(dqs, axis=0) * HEAD_DIM ** (-0.5)).T.astype(BF)


def split(unit):
    row = sum(jnp.where(unit >= GROUPS * r, 1, 0) for r in range(1, ROWS))
    return row, unit - row * GROUPS


def backward_kernel(cot_ref, x2_ref, r2_ref, n1_ref, r1_ref, gd_ref, x_ref, u_ref, qkv_ref, o_ref, e_ref, rinv_ref,
                    a_ref, b_ref, gain_ref, wat_in, wf_in, xall,
                    dx_ref, grad_ref, hidden,
                    dhs, dos, dys, d_ref, wat, wf, wa_sem, wf_sem, h_sem):
    turn, part = pl.program_id(0), pl.program_id(1)
    layer = LAYERS - 1 - turn
    step = turn * LAYER_STEPS + part
    hidden_copy = pltpu.make_async_copy(xall.at[LAYERS], hidden, h_sem)

    def load_ffn(l, j):
        return pltpu.make_async_copy(wf_in.at[l, j], wf.at[j], wf_sem.at[j])

    def load_attention(l, i):
        rows = pl.ds(3 * WIDTH, WIDTH) if i == 1 else pl.ds(0, 3 * WIDTH)
        return pltpu.make_async_copy(wat_in.at[l, rows], wat.at[l, rows], wa_sem.at[l, i])

    last = LAYERS - 1

    @pl.when(step == 0)
    def _():
        for j in range(4):
            load_ffn(last, j).start()
        load_attention(last, 1).start()
        load_attention(last, 0).start()
        hidden_copy.start()
        grad_ref[...] = jnp.zeros_like(grad_ref)

    for k in range(1, LAYERS):
        @pl.when(step == k * LAYER_STEPS - ATT_STEPS)
        def _():
            for j in range(4):
                load_ffn(last - k, j).start()
            load_attention(last - k, 1).start()
            load_attention(last - k, 0).start()

        @pl.when(step == k * LAYER_STEPS)
        def _():
            for j in range(4):
                load_ffn(last - k, j).wait()
            load_attention(last - k, 1).wait()

        @pl.when(step == k * LAYER_STEPS + FFN_STEPS)
        def _():
            load_attention(last - k, 0).wait()

    @pl.when(step == FFN_STEPS)
    def _():
        load_attention(last, 0).wait()

    def ffn_part(dy, wait):
        here = pl.ds(pl.multiple_of(part * BLOCK, BLOCK), BLOCK)
        dh, do = ffn_back_unit(dy(here), x2_ref, r2_ref, n1_ref, r1_ref, gd_ref, wf, wat.at[layer, 3 * WIDTH:, :],
                               gain_ref[layer], wait)
        dhs[here, :] = dh
        dos[here, :] = do

    def wait_load(j):
        if j < 4:
            load_ffn(last, j).wait()
        else:
            load_attention(last, 1).wait()

    @pl.when(step == 0)
    def _():
        ffn_part(lambda here: cot_ref[...].astype(F32), wait_load)

    @pl.when((step > 0) & (step < FFN_STEPS))
    def _():
        ffn_part(lambda here: cot_ref[...].astype(F32), lambda j: None)

    @pl.when((step >= LAYER_STEPS) & (part < FFN_STEPS))
    def _():
        ffn_part(lambda here: dys[here, :], lambda j: None)

    @pl.when(part >= FFN_STEPS)
    def _():
        row, grp = split(part - FFN_STEPS)
        here = pl.ds(pl.multiple_of(row * SEQ, SEQ), SEQ)
        attend_back_unit(grp, dos.at[here], qkv_ref, o_ref, e_ref, rinv_ref, d_ref)

        @pl.when(grp == GROUPS - 1)
        def _():
            dq, dk, dv = (d_ref[:, WIDTH * i:WIDTH * (i + 1)] for i in range(3))
            du = (dot_nt(dq, b_ref[layer, 0]) + dot_nt(dv, b_ref[layer, 1])).astype(BF)
            u = u_ref[0]
            u2 = u + u
            ga = dot_tn(du, x_ref[0])
            gq = dot_tn(u2, dq)[:RANK]
            gv = dot_tn(u2, dv)[RANK:]
            grad_ref[layer] += jnp.concatenate([ga, gq, gv], axis=0)
            w = wat.at[layer]
            dx = (dhs[here, :] + dot_nt(dq, w[0:WIDTH, :]) + dot_nt(dk, w[WIDTH:2 * WIDTH, :])
                  + dot_nt(dv, w[2 * WIDTH:3 * WIDTH, :]) + dot_nt(du, a_ref[layer]))

            @pl.when(layer > 0)
            def _():
                dys[here, :] = dx

            @pl.when(layer == 0)
            def _():
                dx_ref[...] = dx

    @pl.when(step == LAYERS * LAYER_STEPS - 1)
    def _():
        hidden_copy.wait()


def backward(cot, saved, a, b, gains, wat, wf):
    qkv, u, o, e, rinv, n1, r1, gd, r2, xall = saved
    anywhere = pl.BlockSpec(memory_space=pl.ANY)
    layer_of = lambda t: LAYERS - 1 - t
    block_of = lambda p: jnp.minimum(p, FFN_STEPS - 1)
    unit_of = lambda p: split(jnp.maximum(p - FFN_STEPS, 0))
    row_of = lambda p: unit_of(p)[0]
    by_row = lambda width: pl.BlockSpec((1, SEQ, width), lambda t, p: (layer_of(t), row_of(p), 0))
    by_block = lambda width: pl.BlockSpec((1, BLOCK, width), lambda t, p: (layer_of(t), block_of(p), 0))
    whole = lambda v: pl.BlockSpec(v.shape, lambda t, p: (0,) * v.ndim, pipeline_mode=pl.Buffered(1))
    shape = jax.ShapeDtypeStruct
    dma = pltpu.SemaphoreType.DMA
    return pl.pallas_call(
        backward_kernel,
        grid=(LAYERS, LAYER_STEPS),
        in_specs=[
            pl.BlockSpec((BLOCK, WIDTH), lambda t, p: (jnp.where(t == 0, block_of(p), FFN_STEPS - 1), 0)),
            pl.BlockSpec((1, BLOCK, WIDTH), lambda t, p: (layer_of(t) + 1, block_of(p), 0)),
            by_block(128), by_block(WIDTH), by_block(128), by_block(4 * CHUNK),
            by_row(WIDTH), by_row(2 * RANK), by_row(3 * WIDTH), by_row(WIDTH),
            pl.BlockSpec((1, 1, GROUP, SEQ, SEQ), lambda t, p: (layer_of(t), *unit_of(p), 0, 0)),
            pl.BlockSpec((1, 1, HEADS, 8, SEQ), lambda t, p: (layer_of(t), row_of(p), 0, 0, 0)),
            whole(a), whole(b), whole(gains), anywhere, anywhere, anywhere,
        ],
        out_specs=[
            pl.BlockSpec((SEQ, WIDTH), lambda t, p: (jnp.where(t < LAYERS - 1, 0, row_of(p)), 0)),
            pl.BlockSpec((LAYERS, 4 * RANK, WIDTH), lambda t, p: (0, 0, 0)),
            anywhere,
        ],
        out_shape=[shape((TOKENS, WIDTH), F32), shape((LAYERS, 4 * RANK, WIDTH), F32), shape((TOKENS, WIDTH), BF)],
        scratch_shapes=[
            pltpu.VMEM((TOKENS, WIDTH), F32), pltpu.VMEM((TOKENS, WIDTH), BF), pltpu.VMEM((TOKENS, WIDTH), F32),
            pltpu.VMEM((SEQ, 3 * WIDTH), BF), pltpu.VMEM((LAYERS, 4 * WIDTH, WIDTH), BF),
            pltpu.VMEM((4, 2, WIDTH, CHUNK), BF),
            dma((LAYERS, 2)), dma((4,)), dma,
        ],
        compiler_params=params(2),
        name="backward",
    )(cot, xall, r2, n1, r1, gd, xall, u, qkv, o, e, rinv, a, b, gains, wat, wf, xall)


def local(axes, direct, tokens, lengths, attention, down, up, expand, project, gains, cotangent):
    a = jnp.concatenate([down[:, 0], down[:, 1]], axis=2)
    twice = up + up
    b = jnp.stack([jnp.pad(twice[:, 0], ((0, 0), (0, RANK), (0, 0))), jnp.pad(twice[:, 1], ((0, 0), (RANK, 0), (0, 0)))],
                  axis=1)
    if direct:
        att, ex, pr = attention, expand, project
    else:
        att = lax.all_gather(attention, axes, axis=1, tiled=True)
        w1 = lax.all_gather(expand, axes[1], axis=2, tiled=True).reshape(LAYERS, WIDTH, 4, CHUNK).transpose(0, 2, 1, 3)
        w2 = lax.all_gather(project, axes[1], axis=1, tiled=True).reshape(LAYERS, 4, CHUNK, WIDTH)
        ex = pr = jnp.stack([w1, w2], axis=2)
    *saved, wat, wf = forward(axes, direct, lengths, tokens, att, ex, pr, a, b, gains)
    if not direct:
        wat, wf = att, ex
    dx, grads, hidden = backward(cotangent, saved, a, b, gains, wat, wf)
    if direct:
        total = all_sum(axes, grads, 1)
    else:
        total = lax.psum(grads, axes)
    a_grad = total[:, :2 * RANK].reshape(LAYERS, 2, RANK, WIDTH).transpose(0, 1, 3, 2)
    b_grad = total[:, 2 * RANK:].reshape(LAYERS, 2, RANK, WIDTH)
    return hidden, dx, a_grad, b_grad


def solution(mesh):
    axes = tuple(mesh.axis_names)
    dp, tensor = axes
    direct = mesh.shape[dp] == 2 * Z_SIZE and mesh.shape[tensor] == 4
    placed = (
        P(axes, None), P(axes), P(None, axes, None), P(), P(),
        P(None, None, tensor), P(None, tensor, None), P(), P(axes, None),
    )
    return jax.shard_map(
        functools.partial(local, axes, direct),
        mesh=mesh,
        in_specs=placed,
        out_specs=(P(axes, None), P(axes, None), P(), P()),
        check_vma=False,
    )
```

```python
import functools
import jax
import jax.numpy as jnp
from jax import lax
from jax.experimental import pallas as pl
from jax.experimental.pallas import tpu as pltpu
from jax.sharding import PartitionSpec as P

WIDTH = 768
HEADS = 12
HEAD_DIM = 64
SEQ = 512
RANK = 8
EPS = 1e-05
CHUNK = 768
BF = jnp.bfloat16
F32 = jnp.float32
VMEM_LIMIT = 60 * 1024 * 1024
EXP2_SCALE = 1.4426950408889634 * HEAD_DIM ** (-0.5)


def dot(a, b):
    return jnp.dot(a, b, preferred_element_type=F32)


def dot_nt(a, b):
    return lax.dot_general(a, b, (((1,), (1,)), ((), ())), preferred_element_type=F32)


def dot_tn(a, b):
    return lax.dot_general(a, b, (((0,), (0,)), ((), ())), preferred_element_type=F32)


def mean_rows(v):
    return jnp.sum(v, axis=-1, keepdims=True) * (1.0 / WIDTH)


def params(n, collective=None):
    more = {} if collective is None else {"collective_id": collective, "has_side_effects": True}
    return pltpu.CompilerParams(
        dimension_semantics=("arbitrary",) * n, vmem_limit_bytes=VMEM_LIMIT, **more
    )


MESH = pl.DeviceIdType.MESH
Z_SIZE = 4


class Place:
    def __init__(self, axes):
        dp, t = lax.axis_index(axes[0]), lax.axis_index(axes[1])
        self.dp, self.t = dp, t
        self.z, self.x = dp // 2, dp % 2
        self.y, self.core = t // 2, t % 2
        self.to_core = (dp, t + 1 - 2 * self.core)
        self.to_y = (dp, t + 2 - 4 * self.y)
        self.to_x = (dp + 1 - 2 * self.x, t)
        self.to_zpair = (dp + 2 - 4 * (self.z % 2), t)
        self.to_up = (dp + 2, t)
        self.to_down = (dp - 2, t)


def greet(place, line):
    barrier = pltpu.get_barrier_semaphore()
    for device in (place.to_core, place.to_y, place.to_x):
        pl.semaphore_signal(barrier, inc=1, device_id=device, device_id_type=MESH)
    if line:
        @pl.when(place.z < Z_SIZE - 1)
        def _():
            pl.semaphore_signal(barrier, inc=1, device_id=place.to_up, device_id_type=MESH)

        @pl.when(place.z > 0)
        def _():
            pl.semaphore_signal(barrier, inc=1, device_id=place.to_down, device_id_type=MESH)

        inner = (place.z > 0) & (place.z < Z_SIZE - 1)

        @pl.when(inner)
        def _():
            pl.semaphore_wait(barrier, 5)

        @pl.when(jnp.logical_not(inner))
        def _():
            pl.semaphore_wait(barrier, 4)
    else:
        pl.semaphore_signal(barrier, inc=1, device_id=place.to_zpair, device_id_type=MESH)
        pl.semaphore_wait(barrier, 4)


def remote(src, dst, send, recv, device):
    return pltpu.make_async_remote_copy(
        src_ref=src, dst_ref=dst, send_sem=send, recv_sem=recv, device_id=device, device_id_type=MESH
    )


SLICE = 128
FFN_SEMS = [
    pltpu.SemaphoreType.DMA((3, 4)),
    pltpu.SemaphoreType.DMA((12,)),
    pltpu.SemaphoreType.DMA((14,)),
    pltpu.SemaphoreType.DMA((14,)),
]


def ffn_gather(place, layer, w1, w2, out, sems, what, tick=0):
    send, recv, core_send, core_recv = sems
    g = place.x * 2 + place.z % 2
    gd = 3 - g
    gx = (1 - place.x) * 2 + place.z % 2
    gz = place.x * 2 + 1 - place.z % 2

    def spot(slot, s):
        return out.at[slot + 1, s // 6, pl.ds(pl.multiple_of((s % 6) * SLICE, SLICE), SLICE)]

    def over_y(i):
        s = 3 * g + i if i < 3 else 3 * gd
        first = place.x == (0 if i < 3 else 1)
        for here, ref in ((first, w1), (jnp.logical_not(first), w2)):
            @pl.when(here)
            def _():
                src = ref.at[layer, pl.ds(pl.multiple_of((s % 6) * SLICE, SLICE), SLICE)]
                remote(src, spot(1, s), send.at[0, i], recv.at[s], place.to_y).start()

    def arrived(s):
        remote(spot(1, s), spot(1, s), send.at[0, 0], recv.at[s], place.to_y).wait_recv()

    def over(way, i, s):
        device = place.to_x if way == 1 else place.to_zpair
        remote(spot(1, s), spot(1, s), send.at[way, i], recv.at[s], device).start()

    def share(s):
        remote(spot(1, s), spot(2, s), core_send.at[s], core_recv.at[s], place.to_core).start()

    if what == "fy":
        over_y(tick)
    elif what == "fown":
        for m, ref in enumerate((w1, w2)):
            remote(ref.at[layer], out.at[1, m], core_send.at[12 + m], core_recv.at[12 + m], place.to_core).start()
    elif what == "fownin":
        for m, ref in enumerate((w1, w2)):
            remote(ref.at[layer], out.at[1, m], core_send.at[12 + m], core_recv.at[12 + m], place.to_core).wait()
    elif what == "fr" and tick < 4:
        s = 3 * g + tick - 1
        arrived(s)
        over(1, tick - 1, s)
        over(2, tick - 1, s)
        share(s)
        if tick == 3:
            for s in (3 * gx, 3 * gz):
                arrived(s)
                share(s)
    elif what == "fr" and tick == 4:
        s = 3 * gz + 1
        arrived(s)
        over(1, 3, s)
        share(s)
        for s in (3 * gd, 3 * gx + 1):
            arrived(s)
            share(s)
    elif what == "fr" and tick == 5:
        s = 3 * gx + 2
        arrived(s)
        over(2, 3, s)
        share(s)
        s = 3 * gz + 2
        arrived(s)
        share(s)
    elif what == "fr" and tick == 6:
        for s in (3 * gd + 1, 3 * gd + 2):
            arrived(s)
            share(s)
    else:
        for s in range(12):
            remote(spot(1, s), spot(2, s), core_send.at[s], core_recv.at[s], place.to_core).wait()
        for way in range(3):
            for i in range(4):
                remote(spot(1, 0), spot(1, 0), send.at[way, i], recv.at[0], place.to_y).wait_send()


ATT_SEMS = [
    pltpu.SemaphoreType.DMA((2, 4)),
    pltpu.SemaphoreType.DMA((4,)),
    pltpu.SemaphoreType.DMA((2, 4)),
    pltpu.SemaphoreType.DMA((2, 4)),
    pltpu.SemaphoreType.DMA((2, 4)),
    pltpu.SemaphoreType.DMA((2, 4)),
    pltpu.SemaphoreType.DMA((5, 4)),
    pltpu.SemaphoreType.DMA((5, 4)),
    pltpu.SemaphoreType.DMA,
]


def attention_gather(place, layer, block, out, sems, what, d=0):
    z_send, z_recv, n_send, n_recv, h_send, h_recv, c_send, c_recv, own_sem = sems
    rows = block.shape[1]
    half = rows // 2
    z, x, y, core = place.z, place.x, place.y, place.core
    late = Z_SIZE - 1

    def spot(sz, sx, sy, sc, start=0, size=rows):
        at = ((sz * 2 + sx) * 4 + sy * 2 + sc) * rows + start
        return out.at[pl.ds(pl.multiple_of(at, 16), size)]

    def line(sz):
        return spot(sz, x, y, core)

    def side(way, sz):
        return spot(sz, 1 - x, y, core) if way == 0 else spot(sz, x, 1 - y, core)

    def far(way, sz):
        return spot(sz, 1 - x, 1 - y, core, way * half, half)

    devices = (place.to_x, place.to_y)

    def at_distance(d, action, size):
        if d == 0:
            @pl.when(z < size)
            def _():
                action(z)

            return

        @pl.when(z >= d)
        def _():
            action(z - d)

        @pl.when(z + d < size)
        def _():
            action(z + d)

    def line_step(sz, own):
        mine = block.at[layer] if own else line(sz)
        if not own:
            remote(line(sz), line(sz), z_send.at[0, sz], z_recv.at[sz], place.to_core).wait_recv()

        @pl.when((sz <= z) & (z < Z_SIZE - 1))
        def _():
            remote(mine, line(sz), z_send.at[0, sz], z_recv.at[sz], place.to_up).start()

        @pl.when((sz >= z) & (z > 0))
        def _():
            remote(mine, line(sz), z_send.at[1, sz], z_recv.at[sz], place.to_down).start()

        if own:
            @pl.when(sz < late)
            def _():
                spread(sz, mine)
        else:
            @pl.when(sz < late)
            def _():
                spread(sz, line(sz))

    def spread(sz, mine):
        for way in range(2):
            remote(mine, line(sz), n_send.at[way, sz], n_recv.at[way, sz], devices[way]).start()
        remote(mine, line(sz), c_send.at[0, sz], c_recv.at[0, sz], place.to_core).start()

    def side_step(sz):
        for way in range(2):
            remote(side(way, sz), side(way, sz), n_send.at[way, sz], n_recv.at[way, sz], devices[way]).wait_recv()
            at = spot(sz, 1 - x, y, core, 0, half) if way == 0 else spot(sz, x, 1 - y, core, half, half)
            remote(at, at, h_send.at[way, sz], h_recv.at[way, sz], devices[1 - way]).start()
            remote(side(way, sz), side(way, sz), c_send.at[1 + way, sz], c_recv.at[1 + way, sz], place.to_core).start()

    def far_step(sz):
        for way in range(2):
            remote(far(way, sz), far(way, sz), h_send.at[way, sz], h_recv.at[way, sz], place.to_core).wait_recv()
            remote(far(way, sz), far(way, sz), c_send.at[3 + way, sz], c_recv.at[3 + way, sz], place.to_core).start()

    def finish(sz):
        @pl.when((sz <= z) & (z < Z_SIZE - 1))
        def _():
            remote(line(sz), line(sz), z_send.at[0, sz], z_recv.at[sz], place.to_core).wait_send()

        @pl.when((sz >= z) & (z > 0))
        def _():
            remote(line(sz), line(sz), z_send.at[1, sz], z_recv.at[sz], place.to_core).wait_send()

        for way in range(2):
            remote(line(sz), line(sz), n_send.at[way, sz], n_recv.at[way, sz], place.to_core).wait_send()
            remote(far(way, sz), far(way, sz), h_send.at[way, sz], h_recv.at[way, sz], place.to_core).wait_send()
        parts = (
            (line(sz), spot(sz, x, y, 1 - core)),
            (side(0, sz), spot(sz, 1 - x, y, 1 - core)),
            (side(1, sz), spot(sz, x, 1 - y, 1 - core)),
            (far(0, sz), spot(sz, 1 - x, 1 - y, 1 - core, 0, half)),
            (far(1, sz), spot(sz, 1 - x, 1 - y, 1 - core, half, half)),
        )
        for i, (mine, theirs) in enumerate(parts):
            remote(mine, theirs, c_send.at[i, sz], c_recv.at[i, sz], place.to_core).wait()

    own_copy = pltpu.make_async_copy(block.at[layer], line(z), own_sem)
    if what == "line":
        if d == 0:
            own_copy.start()
        at_distance(d, functools.partial(line_step, own=d == 0), Z_SIZE)
    if what == "side":
        at_distance(d, side_step, late)
    if what == "far":
        at_distance(d, far_step, late)
    if what == "fin012":
        own_copy.wait()
        for sz in range(late):
            finish(sz)
    if what == "line3":
        @pl.when(z == late)
        def _():
            spread(late, block.at[layer])

        @pl.when(z < late)
        def _():
            spread(late, line(late))
    if what == "side3":
        side_step(late)
    if what == "far3":
        far_step(late)
    if what == "fin3":
        finish(late)


def all_sum(axes, values, collective):
    layers, high, wide = values.shape
    tiles = high // 8
    owners = layers * tiles
    chips = 4 * Z_SIZE
    half = wide // 2

    def kernel(v_ref, out_ref, sums, box, other_half, core_sem, send, recv, send2, recv2):
        place = Place(axes)
        core = place.core
        me = place.dp * 2 + place.y
        barrier = pltpu.get_barrier_semaphore()
        mine = pl.ds(pl.multiple_of(core * half, 128), half)
        theirs = pl.ds(pl.multiple_of((1 - core) * half, 128), half)

        def chip(i):
            other = lax.rem(me + i, chips)
            return other, (other // 2, (other % 2) * 2 + core)

        def owner(k):
            z, x = k // 2, k % 2
            return k * 2 + (z + x) % 2, (k, (z + x) % 2 * 2 + core)

        my_part = place.dp
        is_owner = place.y == (place.z + place.x) % 2

        def part(ref, k, columns):
            return ref.at[k // tiles, pl.ds(pl.multiple_of(k % tiles * 8, 8), 8), columns]

        def signal(i, _):
            pl.semaphore_signal(barrier, inc=1, device_id=chip(i)[1], device_id_type=MESH)
            return 0

        pl.semaphore_signal(barrier, inc=1, device_id=place.to_core, device_id_type=MESH)
        lax.fori_loop(1, chips, signal, 0)
        pl.semaphore_wait(barrier, chips)
        swap = remote(v_ref.at[:, :, theirs], other_half, core_sem.at[0], core_sem.at[1], place.to_core)
        swap.start()
        swap.wait()
        sums[...] = v_ref[:, :, mine] + other_half[...]

        def to_owner(k, act):
            who, device = owner(k)

            @pl.when(who != me)
            def _():
                act(remote(part(sums, k, slice(None)), box.at[me], send.at[k], recv.at[me], device))

            return 0

        lax.fori_loop(0, owners, lambda k, _: to_owner(k, lambda c: c.start()), 0)

        def collect(i, _):
            other, device = chip(i)
            remote(box.at[other], box.at[other], send.at[0], recv.at[other], device).wait_recv()
            return 0

        def to_all(i, act):
            other, device = chip(i)
            spot = part(out_ref, my_part, mine)
            act(remote(spot, spot, send2.at[i], recv2.at[my_part], device))
            return 0

        @pl.when(is_owner)
        def _():
            lax.fori_loop(1, chips, collect, 0)
            at = pl.ds(pl.multiple_of(my_part % tiles * 8, 8), 8)
            box[me] = sums[my_part // tiles, at, :]
            out_ref[my_part // tiles, at, mine] = jnp.sum(box[...], axis=0)
            lax.fori_loop(1, chips, lambda i, _: to_all(i, lambda c: c.start()), 0)

        def arrived(k, _):
            who, device = owner(k)

            @pl.when(who != me)
            def _():
                spot = part(out_ref, k, mine)
                remote(spot, spot, send2.at[0], recv2.at[k], device).wait_recv()

            return 0

        lax.fori_loop(0, owners, arrived, 0)
        swap = remote(out_ref.at[:, :, mine], out_ref.at[:, :, mine], core_sem.at[2], core_sem.at[3], place.to_core)
        swap.start()
        lax.fori_loop(0, owners, lambda k, _: to_owner(k, lambda c: c.wait_send()), 0)

        @pl.when(is_owner)
        def _():
            lax.fori_loop(1, chips, lambda i, _: to_all(i, lambda c: c.wait_send()), 0)

        swap.wait_send()
        remote(out_ref.at[:, :, theirs], out_ref.at[:, :, theirs], core_sem.at[2], core_sem.at[3], place.to_core).wait_recv()

    dma = pltpu.SemaphoreType.DMA
    return pl.pallas_call(
        kernel,
        in_specs=[pl.BlockSpec(memory_space=pltpu.VMEM)],
        out_specs=pl.BlockSpec(memory_space=pltpu.VMEM),
        out_shape=jax.ShapeDtypeStruct(values.shape, F32),
        scratch_shapes=[
            pltpu.VMEM((layers, high, half), F32), pltpu.VMEM((chips, 8, half), F32), pltpu.VMEM((layers, high, half), F32),
            dma((4,)), dma((owners,)), dma((chips,)), dma((chips,)), dma((owners,)),
        ],
        compiler_params=pltpu.CompilerParams(collective_id=collective, has_side_effects=True),
        name="all_sum",
    )(values)


GROUP = 6
BLOCK = 256
GROUPS = HEADS // GROUP
TOKENS = 1024
ROWS = TOKENS // SEQ
ATT_STEPS = ROWS * GROUPS
FFN_STEPS = TOKENS // BLOCK
LAYER_STEPS = ATT_STEPS + FFN_STEPS
WIDE = 512
WIDE_STEPS = TOKENS // WIDE
FORWARD_STEPS = ROWS + 2 * WIDE_STEPS
LAYERS = 2


def norm_parts(v):
    c = v - mean_rows(v)
    r = lax.rsqrt(mean_rows(c * c) + EPS)
    return c * r, r


def attend_unit(row, length, xs, w, a, b, gain, qkv_ref, u_ref, o_ref, e_ref, rinv_ref, r1_ref, n1s, slot):
    here = pl.ds(pl.multiple_of(row * SEQ, SEQ), SEQ)
    x = xs[here, :]
    u = dot(x, a[...]).astype(BF)
    u_ref[0] = u
    for i in range(3):
        acc = dot(x, w[WIDTH * i:WIDTH * (i + 1), :])
        if i != 1:
            acc += dot(u, b[i // 2])
        qkv_ref[:, WIDTH * i:WIDTH * (i + 1)] = acc.astype(BF)
    key = lax.broadcasted_iota(jnp.int32, (SEQ, 128), 0)
    bound = jnp.where(key < length, 3.0e38, -8.0e9)
    lane = lax.broadcasted_iota(jnp.int32, (SEQ, 128), 1)
    low = lane < HEAD_DIM
    bound = jnp.concatenate([bound] * 4, axis=1)
    for pair in range(HEADS // 2):
        slot(pair)
        at = pair * 128
        q = qkv_ref[:, at:at + 128]
        k = qkv_ref[:, WIDTH + at:WIDTH + at + 128]
        v = qkv_ref[:, 2 * WIDTH + at:2 * WIDTH + at + 128]
        outs = []
        for half in range(2):
            mine = low if half == 0 else ~low
            qh = jnp.where(mine, q, jnp.zeros_like(q))
            vh = jnp.where(mine, v, jnp.ones_like(v))
            s = jnp.minimum(dot_nt(k, qh), bound)
            top = jnp.max(s, axis=0, keepdims=True)
            e = jnp.exp2((s - top) * EXP2_SCALE).astype(BF)
            e_ref[pair * 2 + half] = e
            ot = dot_tn(vh, e)
            if half == 0:
                o_t, l = ot[:HEAD_DIM], ot[HEAD_DIM:HEAD_DIM + 8]
            else:
                o_t, l = ot[HEAD_DIM:], ot[0:8]
            r = 1.0 / l
            rinv_ref[0, 0, pair * 2 + half] = r
            outs.append(o_t * r[0:1])
        both = jnp.concatenate(outs, axis=0)
        o_ref[0, :, at:at + 128] = both.T.astype(BF)
    slot(HEADS // 2)
    m, r = norm_parts(xs[here, :].astype(F32) + dot(o_ref[0], w[3 * WIDTH:, :]))
    n1 = (m * gain).astype(BF)
    n1s[here, :] = n1
    r1_ref[0] = jnp.broadcast_to(r, (SEQ, 128))


def ffn_unit(n1, f, chunks, w, gd_ref):
    for i, j in enumerate(chunks):
        z = dot(n1, w[j, 0])
        cdf = 0.5 + 0.5 * lax.erf(z * 0.7071067811865476)
        pdf = jnp.exp2(z * (z * (-0.5 * 1.4426950408889634))) * 0.3989422804014327
        gd_ref[0, :, CHUNK * i:CHUNK * (i + 1)] = (cdf + z * pdf).astype(BF)
        f = f + dot((z * cdf).astype(BF), w[j, 1])
    return f


def unit_columns(i):
    row = lax.broadcasted_iota(jnp.int32, (RANK, 2 * RANK), 0)
    column = lax.broadcasted_iota(jnp.int32, (RANK, 2 * RANK), 1)
    return jnp.where(column == row + RANK * i, 1.0, 0.0).astype(BF)


def forward_kernel(axes, direct, len_ref, tok, att, ex, pr, down_ref, up_ref, gain_ref,
                   qkv_out, u_ref, o_ref, e_out, rinv_ref, n1_out, r1_ref, gd_ref, r2_ref, xall, wat_out, wf_out, a_out, b_out,
                   qkv_s, e_s, a_ref, b_ref, xs, n1s, fs, wat, wf, row_sem, x_sem, xo_sem, wa_sem, wf_sem, own_sem, *sems):
    layer, part = pl.program_id(0), pl.program_id(1)
    step = layer * FORWARD_STEPS + part
    x_in = pltpu.make_async_copy(tok, xs, x_sem.at[0])
    x_out = pltpu.make_async_copy(xs, xall.at[0], x_sem.at[1])

    def save_x(l, b):
        rows = pl.ds(pl.multiple_of(b * WIDE, WIDE), WIDE)
        return pltpu.make_async_copy(xs.at[rows], xall.at[l + 1, rows], xo_sem.at[b])

    def save_row(l, row):
        rows = pl.ds(pl.multiple_of(row * SEQ, SEQ), SEQ)
        return (pltpu.make_async_copy(e_s.at[row], e_out.at[l, row], row_sem.at[0, row]),
                pltpu.make_async_copy(qkv_s.at[row], qkv_out.at[l, rows], row_sem.at[1, row]),
                pltpu.make_async_copy(n1s.at[rows], n1_out.at[l, rows], row_sem.at[3, row]))

    save_adapters = (pltpu.make_async_copy(a_ref, a_out, row_sem.at[2, 0]),
                     pltpu.make_async_copy(b_ref, b_out, row_sem.at[2, 1]))

    def save_attention(l):
        return pltpu.make_async_copy(wat.at[l], wat_out.at[l], wa_sem.at[l])

    def save_ffn(l):
        return pltpu.make_async_copy(wf.at[l], wf_out.at[l], wf_sem.at[l])

    def own_ffn(l):
        return [pltpu.make_async_copy(r.at[l], wf.at[l, 0, m], own_sem.at[l, m]) for m, r in enumerate((ex, pr))]

    if direct:
        place = Place(axes)
        n_att = len(ATT_SEMS)
        n_ffn = len(FFN_SEMS)
        att_sems = [sems[:n_att], sems[n_att:2 * n_att]]
        sems = sems[2 * n_att:]
        ffn_sems = [sems[:n_ffn], sems[n_ffn:]]

        def run(job):
            what, l, *more = job
            if what in ("fy", "fown", "fownin", "fr", "ffin"):
                ffn_gather(place, l, ex, pr, wf.at[l], ffn_sems[l], what, *more)
            else:
                attention_gather(place, l, att, wat.at[l], att_sems[l], what, *more)
            if what == "fin3":
                save_attention(l).start()
            if what == "ffin":
                save_ffn(l).start()

    @pl.when(step == 0)
    def _():
        x_in.start()
        for l in range(LAYERS):
            a_ref[l] = sum(dot_tn(down_ref[l, i], unit_columns(i)) for i in range(2)).astype(BF)
            for i in range(2):
                twice = up_ref[l, i].astype(F32) * 2.0
                zero = jnp.zeros_like(twice)
                b_ref[l, i] = jnp.concatenate([twice, zero] if i == 0 else [zero, twice], axis=0).astype(BF)
        for c in save_adapters:
            c.start()
        if direct:
            greet(place, True)
            for l in range(LAYERS):
                for c in own_ffn(l):
                    c.start()
            for job in SCHEDULE[0, 0]:
                run(job)
            for l in range(LAYERS):
                for c in own_ffn(l):
                    c.wait()
        else:
            whole = [pltpu.make_async_copy(att, wat, own_sem.at[0, 0]), pltpu.make_async_copy(ex, wf, own_sem.at[0, 1])]
            for c in whole:
                c.start()
            for c in whole:
                c.wait()
        x_in.wait()
        x_out.start()

    def slot(within):
        for (at, where), jobs in SCHEDULE.items():
            if direct and where == within and (at, where) != (0, 0):
                @pl.when(step == at)
                def _():
                    for job in jobs:
                        run(job)

    slot(0)

    @pl.when(part < ROWS)
    def _():
        @pl.when(layer > 0)
        def _():
            for c in save_row(layer - 1, part):
                c.wait()

        attend_unit(part, len_ref[part], xs, wat.at[layer], a_ref.at[layer], b_ref.at[layer], gain_ref[layer, 0:1],
                    qkv_s.at[part], u_ref, o_ref, e_s.at[part], rinv_ref, r1_ref, n1s,
                    lambda pair: slot(pair) if pair else None)
        for c in save_row(layer, part):
            c.start()

    @pl.when((part >= ROWS) & (part < ROWS + WIDE_STEPS))
    def _():
        @pl.when(step == ROWS)
        def _():
            x_out.wait()

        here = pl.ds(pl.multiple_of((part - ROWS) * WIDE, WIDE), WIDE)
        n1 = n1s[here, :]
        fs[here, :] = ffn_unit(n1, n1.astype(F32), (0, 1), wf.at[layer], gd_ref)

    @pl.when(part >= ROWS + WIDE_STEPS)
    def _():
        block = part - ROWS - WIDE_STEPS

        @pl.when(layer > 0)
        def _():
            save_x(layer - 1, block).wait()

        here = pl.ds(pl.multiple_of(block * WIDE, WIDE), WIDE)
        m, r = norm_parts(ffn_unit(n1s[here, :], fs[here, :], (2, 3), wf.at[layer], gd_ref))
        xs[here, :] = (m * gain_ref[layer, 1:2]).astype(BF)
        r2_ref[0] = jnp.broadcast_to(r, (WIDE, 128))
        save_x(layer, block).start()

    @pl.when(step == LAYERS * FORWARD_STEPS - 1)
    def _():
        for b in range(WIDE_STEPS):
            save_x(LAYERS - 1, b).wait()
        for c in save_adapters:
            c.wait()
        for row in range(ROWS):
            for c in save_row(LAYERS - 1, row):
                c.wait()
        if direct:
            for l in range(LAYERS):
                save_attention(l).wait()
                save_ffn(l).wait()


SCHEDULE = {
    (0, 0): [
        ("line", 0, 0), ("fown", 1), ("fy", 0, 0), ("line", 0, 1), ("side", 0, 0), ("line", 0, 2),
        ("fown", 0), ("side", 0, 1), ("line", 0, 3), ("far", 0, 0), ("line3", 0), ("side", 0, 2),
        ("side", 0, 3), ("line", 1, 0), ("side3", 0), ("fy", 0, 1), ("far", 0, 1), ("fy", 0, 2), ("fy", 0, 3),
        ("line", 1, 1), ("far", 0, 2), ("far", 0, 3), ("fin012", 0), ("fr", 0, 1),
    ],
    (0, 2): [
        ("fownin", 0), ("far3", 0), ("fr", 0, 2),
    ],
    (0, 4): [
        ("line", 1, 2), ("fy", 1, 0), ("fin3", 0),
    ],
    (1, 0): [
        ("fr", 0, 3),
    ],
    (1, 2): [
        ("side", 1, 0), ("fr", 0, 4),
    ],
    (1, 4): [
        ("line", 1, 3), ("side", 1, 1), ("fr", 0, 5),
    ],
    (2, 0): [
        ("fownin", 1), ("side", 1, 2),
    ],
    (3, 0): [
        ("fr", 0, 6),
    ],
    (4, 0): [
        ("side", 1, 3), ("line3", 1), ("ffin", 0),
    ],
    (5, 0): [
        ("far", 1, 0), ("far", 1, 1), ("far", 1, 2), ("far", 1, 3), ("fy", 1, 1), ("fr", 1, 1),
    ],
    (6, 0): [
        ("side3", 1), ("fin012", 1), ("fy", 1, 2),
    ],
    (6, 2): [
        ("fy", 1, 3), ("fr", 1, 2), ("far3", 1),
    ],
    (6, 4): [
        ("fin3", 1),
    ],
    (7, 0): [
        ("fr", 1, 3),
    ],
    (7, 4): [
        ("fr", 1, 4), ("fr", 1, 5),
    ],
    (9, 0): [
        ("fr", 1, 6),
    ],
    (10, 0): [
        ("ffin", 1),
    ],
}


def forward(axes, direct, lengths, tokens, att, ex, pr, down, up, gains):
    anywhere = pl.BlockSpec(memory_space=pl.ANY)
    row_of = lambda p: jnp.minimum(p, ROWS - 1)
    by_row = lambda width: pl.BlockSpec((1, SEQ, width), lambda l, p: (l, row_of(p), 0))
    def half_of(p):
        i = jnp.maximum(p - ROWS, 0)
        half = jnp.where(i >= WIDE_STEPS, 1, 0)
        return i - half * WIDE_STEPS, half

    whole = lambda v: pl.BlockSpec(v.shape, lambda l, p: (0,) * v.ndim, pipeline_mode=pl.Buffered(1))
    a_shape, b_shape = (LAYERS, WIDTH, 2 * RANK), (LAYERS, 2, 2 * RANK, WIDTH)
    shape = jax.ShapeDtypeStruct
    dma = pltpu.SemaphoreType.DMA
    return pl.pallas_call(
        functools.partial(forward_kernel, axes, direct),
        grid=(LAYERS, FORWARD_STEPS),
        in_specs=[pl.BlockSpec(memory_space=pltpu.SMEM)] + [anywhere] * 4 + [whole(down), whole(up), whole(gains)],
        out_specs=[
            anywhere, by_row(2 * RANK), by_row(WIDTH), anywhere,
            pl.BlockSpec((1, 1, HEADS, 8, SEQ), lambda l, p: (l, row_of(p), 0, 0, 0)),
            anywhere, by_row(128),
            pl.BlockSpec((1, WIDE, 2 * CHUNK), lambda l, p: (l, *half_of(p))),
            pl.BlockSpec((1, WIDE, 128), lambda l, p: (l, jnp.maximum(p - ROWS - WIDE_STEPS, 0), 0)),
            anywhere, anywhere, anywhere, anywhere, anywhere,
        ],
        out_shape=[
            shape((LAYERS, TOKENS, 3 * WIDTH), BF), shape((LAYERS, TOKENS, 2 * RANK), BF), shape((LAYERS, TOKENS, WIDTH), BF),
            shape((LAYERS, ROWS, HEADS, SEQ, SEQ), BF), shape((LAYERS, ROWS, HEADS, 8, SEQ), F32),
            shape((LAYERS, TOKENS, WIDTH), BF), shape((LAYERS, TOKENS, 128), F32),
            shape((LAYERS, TOKENS, 4 * CHUNK), BF), shape((LAYERS, TOKENS, 128), F32),
            shape((LAYERS + 1, TOKENS, WIDTH), BF),
            shape((LAYERS, 4 * WIDTH, WIDTH), BF), shape((LAYERS, 4, 2, WIDTH, CHUNK), BF), shape(a_shape, BF), shape(b_shape, BF),
        ],
        scratch_shapes=[
            pltpu.VMEM((ROWS, SEQ, 3 * WIDTH), BF), pltpu.VMEM((ROWS, HEADS, SEQ, SEQ), BF),
            pltpu.VMEM(a_shape, BF), pltpu.VMEM(b_shape, BF),
            pltpu.VMEM((TOKENS, WIDTH), BF), pltpu.VMEM((TOKENS, WIDTH), BF), pltpu.VMEM((TOKENS, WIDTH), F32),
            pltpu.VMEM((LAYERS, 4 * WIDTH, WIDTH), BF), pltpu.VMEM((LAYERS, 4, 2, WIDTH, CHUNK), BF),
            dma((4, ROWS)), dma((2,)), dma((WIDE_STEPS,)), dma((LAYERS,)), dma((LAYERS,)), dma((LAYERS, 2)),
        ] + (ATT_SEMS * 2 + FFN_SEMS * 2 if direct else []),
        compiler_params=params(2, 0 if direct else None),
        name="forward",
    )(lengths, tokens, att, ex, pr, down, up, gains)


def norm_back(e, m, r):
    return r * (e - mean_rows(e) - m * mean_rows(e * m))


def ffn_back_unit(dy, x2_ref, r2_ref, n1_ref, r1_ref, gd_ref, w, wo, gains, wait):
    g1, g2 = gains[0:1], gains[1:2]
    dh2 = norm_back(dy * g2, x2_ref[0].astype(F32) * (1.0 / g2), r2_ref[0, :, 0:1])
    df = dh2.astype(BF)
    dn = dh2
    for j in range(4):
        wait(j)
        dz = (dot_nt(df, w[j, 1]) * gd_ref[0, :, CHUNK * j:CHUNK * (j + 1)].astype(F32)).astype(BF)
        dn = dn + dot_nt(dz, w[j, 0])
    dh = norm_back(dn * g1, n1_ref[0].astype(F32) * (1.0 / g1), r1_ref[0, :, 0:1])
    wait(4)
    return dh, dot_nt(dh.astype(BF), wo[...]).astype(BF)


def attend_back_unit(grp, do_ref, qkv_ref, o_ref, e_ref, rinv_ref, d_ref):
    lane = lax.broadcasted_iota(jnp.int32, (SEQ, 128), 1)
    low = lane < HEAD_DIM
    for pair in range(GROUP // 2):
        at = pl.multiple_of(grp * (GROUP * HEAD_DIM) + pair * 128, 128)
        q = qkv_ref[0, :, pl.ds(at, 128)]
        k = qkv_ref[0, :, pl.ds(WIDTH + at, 128)]
        v = qkv_ref[0, :, pl.ds(2 * WIDTH + at, 128)]
        head = grp * GROUP + pair * 2
        scale = jnp.concatenate([rinv_ref[0, 0, head]] * 8 + [rinv_ref[0, 0, head + 1]] * 8, axis=0).T
        dos = do_ref[:, pl.ds(at, 128)].astype(F32) * scale
        other = pltpu.roll(-dos * o_ref[0, :, pl.ds(at, 128)].astype(F32), HEAD_DIM, 1).astype(BF)
        dos = dos.astype(BF)
        dvs, dks, dqs = [], [], []
        for half in range(2):
            mine = low if half == 0 else ~low
            e = e_ref[0, 0, pair * 2 + half]
            dp = dot_nt(jnp.where(mine, v, jnp.ones_like(v)), jnp.where(mine, dos, other))
            ds = (dp * e.astype(F32)).astype(BF)
            dvs.append(dot(e, dos))
            dks.append(dot(ds, q))
            dqs.append(dot_tn(k, ds)[half * HEAD_DIM:(half + 1) * HEAD_DIM])
        d_ref[:, pl.ds(2 * WIDTH + at, 128)] = jnp.where(low, dvs[0], dvs[1]).astype(BF)
        d_ref[:, pl.ds(WIDTH + at, 128)] = (jnp.where(low, dks[0], dks[1]) * HEAD_DIM ** (-0.5)).astype(BF)
        d_ref[:, pl.ds(at, 128)] = (jnp.concatenate(dqs, axis=0) * HEAD_DIM ** (-0.5)).T.astype(BF)


def split(unit):
    row = sum(jnp.where(unit >= GROUPS * r, 1, 0) for r in range(1, ROWS))
    return row, unit - row * GROUPS


def backward_kernel(cot_ref, x2_ref, r2_ref, n1_ref, r1_ref, gd_ref, x_ref, u_ref, qkv_ref, o_ref, e_ref, rinv_ref,
                    a_ref, b_ref, gain_ref, wat_in, wf_in, xall,
                    dx_ref, grad_ref, hidden,
                    dhs, dos, dys, d_ref, wat, wf, wa_sem, wf_sem, h_sem):
    turn, part = pl.program_id(0), pl.program_id(1)
    layer = LAYERS - 1 - turn
    step = turn * LAYER_STEPS + part
    hidden_copy = pltpu.make_async_copy(xall.at[LAYERS], hidden, h_sem)

    def load_ffn(l, j):
        return pltpu.make_async_copy(wf_in.at[l, j], wf.at[j], wf_sem.at[j])

    def load_attention(l, i):
        rows = pl.ds(3 * WIDTH, WIDTH) if i == 1 else pl.ds(0, 3 * WIDTH)
        return pltpu.make_async_copy(wat_in.at[l, rows], wat.at[l, rows], wa_sem.at[l, i])

    last = LAYERS - 1

    @pl.when(step == 0)
    def _():
        for j in range(4):
            load_ffn(last, j).start()
        load_attention(last, 1).start()
        load_attention(last, 0).start()
        hidden_copy.start()
        grad_ref[...] = jnp.zeros_like(grad_ref)

    for k in range(1, LAYERS):
        @pl.when(step == k * LAYER_STEPS - ATT_STEPS)
        def _():
            for j in range(4):
                load_ffn(last - k, j).start()
            load_attention(last - k, 1).start()
            load_attention(last - k, 0).start()

        @pl.when(step == k * LAYER_STEPS)
        def _():
            for j in range(4):
                load_ffn(last - k, j).wait()
            load_attention(last - k, 1).wait()

        @pl.when(step == k * LAYER_STEPS + FFN_STEPS)
        def _():
            load_attention(last - k, 0).wait()

    @pl.when(step == FFN_STEPS)
    def _():
        load_attention(last, 0).wait()

    def ffn_part(dy, wait):
        here = pl.ds(pl.multiple_of(part * BLOCK, BLOCK), BLOCK)
        dh, do = ffn_back_unit(dy(here), x2_ref, r2_ref, n1_ref, r1_ref, gd_ref, wf, wat.at[layer, 3 * WIDTH:, :],
                               gain_ref[layer], wait)
        dhs[here, :] = dh
        dos[here, :] = do

    def wait_load(j):
        if j < 4:
            load_ffn(last, j).wait()
        else:
            load_attention(last, 1).wait()

    @pl.when(step == 0)
    def _():
        ffn_part(lambda here: cot_ref[...].astype(F32), wait_load)

    @pl.when((step > 0) & (step < FFN_STEPS))
    def _():
        ffn_part(lambda here: cot_ref[...].astype(F32), lambda j: None)

    @pl.when((step >= LAYER_STEPS) & (part < FFN_STEPS))
    def _():
        ffn_part(lambda here: dys[here, :], lambda j: None)

    @pl.when(part >= FFN_STEPS)
    def _():
        row, grp = split(part - FFN_STEPS)
        here = pl.ds(pl.multiple_of(row * SEQ, SEQ), SEQ)
        attend_back_unit(grp, dos.at[here], qkv_ref, o_ref, e_ref, rinv_ref, d_ref)

        @pl.when(grp == GROUPS - 1)
        def _():
            dq, dk, dv = (d_ref[:, WIDTH * i:WIDTH * (i + 1)] for i in range(3))
            du = (dot_nt(dq, b_ref[layer, 0]) + dot_nt(dv, b_ref[layer, 1])).astype(BF)
            u = u_ref[0]
            u2 = u + u
            ga = dot_tn(du, x_ref[0])
            gq = dot_tn(u2, dq)[:RANK]
            gv = dot_tn(u2, dv)[RANK:]
            grad_ref[layer] += jnp.concatenate([ga, gq, gv], axis=0)
            w = wat.at[layer]
            dx = (dhs[here, :] + dot_nt(dq, w[0:WIDTH, :]) + dot_nt(dk, w[WIDTH:2 * WIDTH, :])
                  + dot_nt(dv, w[2 * WIDTH:3 * WIDTH, :]) + dot_nt(du, a_ref[layer]))

            @pl.when(layer > 0)
            def _():
                dys[here, :] = dx

            @pl.when(layer == 0)
            def _():
                dx_ref[...] = dx

    @pl.when(step == LAYERS * LAYER_STEPS - 1)
    def _():
        hidden_copy.wait()


def backward(cot, saved, a, b, gains, wat, wf):
    qkv, u, o, e, rinv, n1, r1, gd, r2, xall = saved
    anywhere = pl.BlockSpec(memory_space=pl.ANY)
    layer_of = lambda t: LAYERS - 1 - t
    block_of = lambda p: jnp.minimum(p, FFN_STEPS - 1)
    unit_of = lambda p: split(jnp.maximum(p - FFN_STEPS, 0))
    row_of = lambda p: unit_of(p)[0]
    by_row = lambda width: pl.BlockSpec((1, SEQ, width), lambda t, p: (layer_of(t), row_of(p), 0))
    by_block = lambda width: pl.BlockSpec((1, BLOCK, width), lambda t, p: (layer_of(t), block_of(p), 0))
    whole = lambda v: pl.BlockSpec(v.shape, lambda t, p: (0,) * v.ndim, pipeline_mode=pl.Buffered(1))
    shape = jax.ShapeDtypeStruct
    dma = pltpu.SemaphoreType.DMA
    return pl.pallas_call(
        backward_kernel,
        grid=(LAYERS, LAYER_STEPS),
        in_specs=[
            pl.BlockSpec((BLOCK, WIDTH), lambda t, p: (jnp.where(t == 0, block_of(p), FFN_STEPS - 1), 0)),
            pl.BlockSpec((1, BLOCK, WIDTH), lambda t, p: (layer_of(t) + 1, block_of(p), 0)),
            by_block(128), by_block(WIDTH), by_block(128), by_block(4 * CHUNK),
            by_row(WIDTH), by_row(2 * RANK), by_row(3 * WIDTH), by_row(WIDTH),
            pl.BlockSpec((1, 1, GROUP, SEQ, SEQ), lambda t, p: (layer_of(t), *unit_of(p), 0, 0)),
            pl.BlockSpec((1, 1, HEADS, 8, SEQ), lambda t, p: (layer_of(t), row_of(p), 0, 0, 0)),
            whole(a), whole(b), whole(gains), anywhere, anywhere, anywhere,
        ],
        out_specs=[
            pl.BlockSpec((SEQ, WIDTH), lambda t, p: (jnp.where(t < LAYERS - 1, 0, row_of(p)), 0)),
            pl.BlockSpec((LAYERS, 4 * RANK, WIDTH), lambda t, p: (0, 0, 0)),
            anywhere,
        ],
        out_shape=[shape((TOKENS, WIDTH), F32), shape((LAYERS, 4 * RANK, WIDTH), F32), shape((TOKENS, WIDTH), BF)],
        scratch_shapes=[
            pltpu.VMEM((TOKENS, WIDTH), F32), pltpu.VMEM((TOKENS, WIDTH), BF), pltpu.VMEM((TOKENS, WIDTH), F32),
            pltpu.VMEM((SEQ, 3 * WIDTH), BF), pltpu.VMEM((LAYERS, 4 * WIDTH, WIDTH), BF),
            pltpu.VMEM((4, 2, WIDTH, CHUNK), BF),
            dma((LAYERS, 2)), dma((4,)), dma,
        ],
        compiler_params=params(2),
        name="backward",
    )(cot, xall, r2, n1, r1, gd, xall, u, qkv, o, e, rinv, a, b, gains, wat, wf, xall)


def local(axes, direct, tokens, lengths, attention, down, up, expand, project, gains, cotangent):
    if direct:
        att, ex, pr = attention, expand, project
    else:
        att = lax.all_gather(attention, axes, axis=1, tiled=True)
        w1 = lax.all_gather(expand, axes[1], axis=2, tiled=True).reshape(LAYERS, WIDTH, 4, CHUNK).transpose(0, 2, 1, 3)
        w2 = lax.all_gather(project, axes[1], axis=1, tiled=True).reshape(LAYERS, 4, CHUNK, WIDTH)
        ex = pr = jnp.stack([w1, w2], axis=2)
    *saved, wat, wf, a, b = forward(axes, direct, lengths, tokens, att, ex, pr, down.swapaxes(2, 3), up, gains)
    if not direct:
        wat, wf = att, ex
    dx, grads, hidden = backward(cotangent, saved, a, b, gains, wat, wf)
    if direct:
        total = all_sum(axes, grads, 1)
    else:
        total = lax.psum(grads, axes)
    a_grad = total[:, :2 * RANK].reshape(LAYERS, 2, RANK, WIDTH).transpose(0, 1, 3, 2)
    b_grad = total[:, 2 * RANK:].reshape(LAYERS, 2, RANK, WIDTH)
    return hidden, dx, a_grad, b_grad


def solution(mesh):
    axes = tuple(mesh.axis_names)
    dp, tensor = axes
    direct = mesh.shape[dp] == 2 * Z_SIZE and mesh.shape[tensor] == 4
    placed = (
        P(axes, None), P(axes), P(None, axes, None), P(), P(),
        P(None, None, tensor), P(None, tensor, None), P(), P(axes, None),
    )
    return jax.shard_map(
        functools.partial(local, axes, direct),
        mesh=mesh,
        in_specs=placed,
        out_specs=(P(axes, None), P(axes, None), P(), P()),
        check_vma=False,
    )
```

```python
import functools
import jax
import jax.numpy as jnp
from jax import lax
from jax.experimental import pallas as pl
from jax.experimental.pallas import tpu as pltpu
from jax.sharding import PartitionSpec as P

WIDTH = 768
HEADS = 12
HEAD_DIM = 64
SEQ = 512
RANK = 8
EPS = 1e-05
CHUNK = 768
BF = jnp.bfloat16
F32 = jnp.float32
VMEM_LIMIT = 60 * 1024 * 1024
EXP2_SCALE = 1.4426950408889634 * HEAD_DIM ** (-0.5)


def dot(a, b):
    return jnp.dot(a, b, preferred_element_type=F32)


def dot_nt(a, b):
    return lax.dot_general(a, b, (((1,), (1,)), ((), ())), preferred_element_type=F32)


def dot_tn(a, b):
    return lax.dot_general(a, b, (((0,), (0,)), ((), ())), preferred_element_type=F32)


def mean_rows(v):
    return jnp.sum(v, axis=-1, keepdims=True) * (1.0 / WIDTH)


def params(n, collective=None):
    more = {} if collective is None else {"collective_id": collective, "has_side_effects": True}
    return pltpu.CompilerParams(
        dimension_semantics=("arbitrary",) * n, vmem_limit_bytes=VMEM_LIMIT, **more
    )


MESH = pl.DeviceIdType.MESH
Z_SIZE = 4


class Place:
    def __init__(self, axes):
        dp, t = lax.axis_index(axes[0]), lax.axis_index(axes[1])
        self.dp, self.t = dp, t
        self.z, self.x = dp // 2, dp % 2
        self.y, self.core = t // 2, t % 2
        self.to_core = (dp, t + 1 - 2 * self.core)
        self.to_y = (dp, t + 2 - 4 * self.y)
        self.to_x = (dp + 1 - 2 * self.x, t)
        self.to_zpair = (dp + 2 - 4 * (self.z % 2), t)
        self.to_up = (dp + 2, t)
        self.to_down = (dp - 2, t)


def greet(place, line):
    barrier = pltpu.get_barrier_semaphore()
    for device in (place.to_core, place.to_y, place.to_x):
        pl.semaphore_signal(barrier, inc=1, device_id=device, device_id_type=MESH)
    if line:
        @pl.when(place.z < Z_SIZE - 1)
        def _():
            pl.semaphore_signal(barrier, inc=1, device_id=place.to_up, device_id_type=MESH)

        @pl.when(place.z > 0)
        def _():
            pl.semaphore_signal(barrier, inc=1, device_id=place.to_down, device_id_type=MESH)

        inner = (place.z > 0) & (place.z < Z_SIZE - 1)

        @pl.when(inner)
        def _():
            pl.semaphore_wait(barrier, 5)

        @pl.when(jnp.logical_not(inner))
        def _():
            pl.semaphore_wait(barrier, 4)
    else:
        pl.semaphore_signal(barrier, inc=1, device_id=place.to_zpair, device_id_type=MESH)
        pl.semaphore_wait(barrier, 4)


def remote(src, dst, send, recv, device):
    return pltpu.make_async_remote_copy(
        src_ref=src, dst_ref=dst, send_sem=send, recv_sem=recv, device_id=device, device_id_type=MESH
    )


SLICE = 128
FFN_SEMS = [
    pltpu.SemaphoreType.DMA((3, 4)),
    pltpu.SemaphoreType.DMA((12,)),
    pltpu.SemaphoreType.DMA((14,)),
    pltpu.SemaphoreType.DMA((14,)),
]


def ffn_gather(place, layer, w1, w2, out, sems, what, tick=0):
    send, recv, core_send, core_recv = sems
    g = place.x * 2 + place.z % 2
    gd = 3 - g
    gx = (1 - place.x) * 2 + place.z % 2
    gz = place.x * 2 + 1 - place.z % 2

    def spot(slot, s):
        return out.at[slot + 1, s // 6, pl.ds(pl.multiple_of((s % 6) * SLICE, SLICE), SLICE)]

    def over_y(i):
        s = 3 * g + i if i < 3 else 3 * gd
        first = place.x == (0 if i < 3 else 1)
        for here, ref in ((first, w1), (jnp.logical_not(first), w2)):
            @pl.when(here)
            def _():
                src = ref.at[layer, pl.ds(pl.multiple_of((s % 6) * SLICE, SLICE), SLICE)]
                remote(src, spot(1, s), send.at[0, i], recv.at[s], place.to_y).start()

    def arrived(s):
        remote(spot(1, s), spot(1, s), send.at[0, 0], recv.at[s], place.to_y).wait_recv()

    def over(way, i, s):
        device = place.to_x if way == 1 else place.to_zpair
        remote(spot(1, s), spot(1, s), send.at[way, i], recv.at[s], device).start()

    def share(s):
        remote(spot(1, s), spot(2, s), core_send.at[s], core_recv.at[s], place.to_core).start()

    if what == "fy":
        over_y(tick)
    elif what == "fown":
        for m, ref in enumerate((w1, w2)):
            remote(ref.at[layer], out.at[1, m], core_send.at[12 + m], core_recv.at[12 + m], place.to_core).start()
    elif what == "fownin":
        for m, ref in enumerate((w1, w2)):
            remote(ref.at[layer], out.at[1, m], core_send.at[12 + m], core_recv.at[12 + m], place.to_core).wait()
    elif what == "fr" and tick < 4:
        s = 3 * g + tick - 1
        arrived(s)
        over(1, tick - 1, s)
        over(2, tick - 1, s)
        share(s)
        if tick == 3:
            for s in (3 * gx, 3 * gz):
                arrived(s)
                share(s)
    elif what == "fr" and tick == 4:
        s = 3 * gz + 1
        arrived(s)
        over(1, 3, s)
        share(s)
        for s in (3 * gd, 3 * gx + 1):
            arrived(s)
            share(s)
    elif what == "fr" and tick == 5:
        s = 3 * gx + 2
        arrived(s)
        over(2, 3, s)
        share(s)
        s = 3 * gz + 2
        arrived(s)
        share(s)
    elif what == "fr" and tick == 6:
        for s in (3 * gd + 1, 3 * gd + 2):
            arrived(s)
            share(s)
    else:
        for s in range(12):
            remote(spot(1, s), spot(2, s), core_send.at[s], core_recv.at[s], place.to_core).wait()
        for way in range(3):
            for i in range(4):
                remote(spot(1, 0), spot(1, 0), send.at[way, i], recv.at[0], place.to_y).wait_send()


ATT_SEMS = [
    pltpu.SemaphoreType.DMA((2, 4)),
    pltpu.SemaphoreType.DMA((4,)),
    pltpu.SemaphoreType.DMA((2, 4)),
    pltpu.SemaphoreType.DMA((2, 4)),
    pltpu.SemaphoreType.DMA((2, 4)),
    pltpu.SemaphoreType.DMA((2, 4)),
    pltpu.SemaphoreType.DMA((5, 4)),
    pltpu.SemaphoreType.DMA((5, 4)),
    pltpu.SemaphoreType.DMA,
]


def attention_gather(place, layer, block, out, sems, what, d=0):
    z_send, z_recv, n_send, n_recv, h_send, h_recv, c_send, c_recv, own_sem = sems
    rows = block.shape[1]
    half = rows // 2
    z, x, y, core = place.z, place.x, place.y, place.core
    late = Z_SIZE - 1

    def spot(sz, sx, sy, sc, start=0, size=rows):
        at = ((sz * 2 + sx) * 4 + sy * 2 + sc) * rows + start
        return out.at[pl.ds(pl.multiple_of(at, 16), size)]

    def line(sz):
        return spot(sz, x, y, core)

    def side(way, sz):
        return spot(sz, 1 - x, y, core) if way == 0 else spot(sz, x, 1 - y, core)

    def far(way, sz):
        return spot(sz, 1 - x, 1 - y, core, way * half, half)

    devices = (place.to_x, place.to_y)

    def at_distance(d, action, size):
        if d == 0:
            @pl.when(z < size)
            def _():
                action(z)

            return

        @pl.when(z >= d)
        def _():
            action(z - d)

        @pl.when(z + d < size)
        def _():
            action(z + d)

    def line_step(sz, own):
        mine = block.at[layer] if own else line(sz)
        if not own:
            remote(line(sz), line(sz), z_send.at[0, sz], z_recv.at[sz], place.to_core).wait_recv()

        @pl.when((sz <= z) & (z < Z_SIZE - 1))
        def _():
            remote(mine, line(sz), z_send.at[0, sz], z_recv.at[sz], place.to_up).start()

        @pl.when((sz >= z) & (z > 0))
        def _():
            remote(mine, line(sz), z_send.at[1, sz], z_recv.at[sz], place.to_down).start()

        if own:
            @pl.when(sz < late)
            def _():
                spread(sz, mine)
        else:
            @pl.when(sz < late)
            def _():
                spread(sz, line(sz))

    def spread(sz, mine):
        for way in range(2):
            remote(mine, line(sz), n_send.at[way, sz], n_recv.at[way, sz], devices[way]).start()
        remote(mine, line(sz), c_send.at[0, sz], c_recv.at[0, sz], place.to_core).start()

    def side_step(sz):
        for way in range(2):
            remote(side(way, sz), side(way, sz), n_send.at[way, sz], n_recv.at[way, sz], devices[way]).wait_recv()
            at = spot(sz, 1 - x, y, core, 0, half) if way == 0 else spot(sz, x, 1 - y, core, half, half)
            remote(at, at, h_send.at[way, sz], h_recv.at[way, sz], devices[1 - way]).start()
            remote(side(way, sz), side(way, sz), c_send.at[1 + way, sz], c_recv.at[1 + way, sz], place.to_core).start()

    def far_step(sz):
        for way in range(2):
            remote(far(way, sz), far(way, sz), h_send.at[way, sz], h_recv.at[way, sz], place.to_core).wait_recv()
            remote(far(way, sz), far(way, sz), c_send.at[3 + way, sz], c_recv.at[3 + way, sz], place.to_core).start()

    def finish(sz):
        @pl.when((sz <= z) & (z < Z_SIZE - 1))
        def _():
            remote(line(sz), line(sz), z_send.at[0, sz], z_recv.at[sz], place.to_core).wait_send()

        @pl.when((sz >= z) & (z > 0))
        def _():
            remote(line(sz), line(sz), z_send.at[1, sz], z_recv.at[sz], place.to_core).wait_send()

        for way in range(2):
            remote(line(sz), line(sz), n_send.at[way, sz], n_recv.at[way, sz], place.to_core).wait_send()
            remote(far(way, sz), far(way, sz), h_send.at[way, sz], h_recv.at[way, sz], place.to_core).wait_send()
        parts = (
            (line(sz), spot(sz, x, y, 1 - core)),
            (side(0, sz), spot(sz, 1 - x, y, 1 - core)),
            (side(1, sz), spot(sz, x, 1 - y, 1 - core)),
            (far(0, sz), spot(sz, 1 - x, 1 - y, 1 - core, 0, half)),
            (far(1, sz), spot(sz, 1 - x, 1 - y, 1 - core, half, half)),
        )
        for i, (mine, theirs) in enumerate(parts):
            remote(mine, theirs, c_send.at[i, sz], c_recv.at[i, sz], place.to_core).wait()

    own_copy = pltpu.make_async_copy(block.at[layer], line(z), own_sem)
    if what == "line":
        if d == 0:
            own_copy.start()
        at_distance(d, functools.partial(line_step, own=d == 0), Z_SIZE)
    if what == "side":
        at_distance(d, side_step, late)
    if what == "far":
        at_distance(d, far_step, late)
    if what == "fin012":
        own_copy.wait()
        for sz in range(late):
            finish(sz)
    if what == "line3":
        @pl.when(z == late)
        def _():
            spread(late, block.at[layer])

        @pl.when(z < late)
        def _():
            spread(late, line(late))
    if what == "side3":
        side_step(late)
    if what == "far3":
        far_step(late)
    if what == "fin3":
        finish(late)


def all_sum(axes, values, collective):
    layers, high, wide = values.shape
    tiles = high // 8
    owners = layers * tiles
    chips = 4 * Z_SIZE
    half = wide // 2

    def each(start, stop, body, carry):
        for i in range(start, stop):
            body(i, carry)

    def kernel(v_ref, out_ref, sums, box, other_half, core_sem, send, recv, send2, recv2):
        place = Place(axes)
        core = place.core
        me = place.dp * 2 + place.y
        barrier = pltpu.get_barrier_semaphore()
        mine = pl.ds(pl.multiple_of(core * half, 128), half)
        theirs = pl.ds(pl.multiple_of((1 - core) * half, 128), half)

        def chip(i):
            other = lax.rem(me + i, chips)
            return other, (other // 2, (other % 2) * 2 + core)

        def owner(k):
            z, x = k // 2, k % 2
            return k * 2 + (z + x) % 2, (k, (z + x) % 2 * 2 + core)

        my_part = place.dp
        is_owner = place.y == (place.z + place.x) % 2

        def part(ref, k, columns):
            return ref.at[k // tiles, pl.ds(pl.multiple_of(k % tiles * 8, 8), 8), columns]

        def signal(i, _):
            pl.semaphore_signal(barrier, inc=1, device_id=chip(i)[1], device_id_type=MESH)
            return 0

        pl.semaphore_signal(barrier, inc=1, device_id=place.to_core, device_id_type=MESH)
        each(1, chips, signal, 0)
        pl.semaphore_wait(barrier, chips)
        swap = remote(v_ref.at[:, :, theirs], other_half, core_sem.at[0], core_sem.at[1], place.to_core)
        swap.start()
        swap.wait()
        sums[...] = v_ref[:, :, mine] + other_half[...]

        def to_owner(k, act):
            who, device = owner(k)

            @pl.when(who != me)
            def _():
                act(remote(part(sums, k, slice(None)), box.at[me], send.at[k], recv.at[me], device))

            return 0

        each(0, owners, lambda k, _: to_owner(k, lambda c: c.start()), 0)

        def collect(i, _):
            other, device = chip(i)
            remote(box.at[other], box.at[other], send.at[0], recv.at[other], device).wait_recv()
            return 0

        def to_all(i, act):
            other, device = chip(i)
            spot = part(out_ref, my_part, mine)
            act(remote(spot, spot, send2.at[i], recv2.at[my_part], device))
            return 0

        @pl.when(is_owner)
        def _():
            each(1, chips, collect, 0)
            at = pl.ds(pl.multiple_of(my_part % tiles * 8, 8), 8)
            box[me] = sums[my_part // tiles, at, :]
            out_ref[my_part // tiles, at, mine] = jnp.sum(box[...], axis=0)
            each(1, chips, lambda i, _: to_all(i, lambda c: c.start()), 0)

        def arrived(k, _):
            who, device = owner(k)

            @pl.when(who != me)
            def _():
                spot = part(out_ref, k, mine)
                remote(spot, spot, send2.at[0], recv2.at[k], device).wait_recv()

            return 0

        each(0, owners, arrived, 0)
        swap = remote(out_ref.at[:, :, mine], out_ref.at[:, :, mine], core_sem.at[2], core_sem.at[3], place.to_core)
        swap.start()
        each(0, owners, lambda k, _: to_owner(k, lambda c: c.wait_send()), 0)

        @pl.when(is_owner)
        def _():
            each(1, chips, lambda i, _: to_all(i, lambda c: c.wait_send()), 0)

        swap.wait_send()
        remote(out_ref.at[:, :, theirs], out_ref.at[:, :, theirs], core_sem.at[2], core_sem.at[3], place.to_core).wait_recv()

    dma = pltpu.SemaphoreType.DMA
    return pl.pallas_call(
        kernel,
        in_specs=[pl.BlockSpec(memory_space=pltpu.VMEM)],
        out_specs=pl.BlockSpec(memory_space=pltpu.VMEM),
        out_shape=jax.ShapeDtypeStruct(values.shape, F32),
        scratch_shapes=[
            pltpu.VMEM((layers, high, half), F32), pltpu.VMEM((chips, 8, half), F32), pltpu.VMEM((layers, high, half), F32),
            dma((4,)), dma((owners,)), dma((chips,)), dma((chips,)), dma((owners,)),
        ],
        compiler_params=pltpu.CompilerParams(collective_id=collective, has_side_effects=True),
        name="all_sum",
    )(values)


GROUP = 6
BLOCK = 256
GROUPS = HEADS // GROUP
TOKENS = 1024
ROWS = TOKENS // SEQ
ATT_STEPS = ROWS * GROUPS
FFN_STEPS = TOKENS // BLOCK
LAYER_STEPS = ATT_STEPS + FFN_STEPS
WIDE = 512
WIDE_STEPS = TOKENS // WIDE
FORWARD_STEPS = ROWS + 2 * WIDE_STEPS
LAYERS = 2


def norm_parts(v):
    c = v - mean_rows(v)
    r = lax.rsqrt(mean_rows(c * c) + EPS)
    return c * r, r


def attend_unit(row, length, xs, w, a, b, gain, qkv_ref, u_ref, o_ref, e_ref, rinv_ref, r1_ref, n1s, slot):
    here = pl.ds(pl.multiple_of(row * SEQ, SEQ), SEQ)
    x = xs[here, :]
    u = dot(x, a[...]).astype(BF)
    u_ref[0] = u
    for i in range(3):
        acc = dot(x, w[WIDTH * i:WIDTH * (i + 1), :])
        if i != 1:
            acc += dot(u, b[i // 2])
        qkv_ref[:, WIDTH * i:WIDTH * (i + 1)] = acc.astype(BF)
    key = lax.broadcasted_iota(jnp.int32, (SEQ, 128), 0)
    bound = jnp.where(key < length, 3.0e38, -8.0e9)
    lane = lax.broadcasted_iota(jnp.int32, (SEQ, 128), 1)
    low = lane < HEAD_DIM
    bound = jnp.concatenate([bound] * 4, axis=1)
    for pair in range(HEADS // 2):
        slot(pair)
        at = pair * 128
        q = qkv_ref[:, at:at + 128]
        k = qkv_ref[:, WIDTH + at:WIDTH + at + 128]
        v = qkv_ref[:, 2 * WIDTH + at:2 * WIDTH + at + 128]
        outs = []
        for half in range(2):
            mine = low if half == 0 else ~low
            qh = jnp.where(mine, q, jnp.zeros_like(q))
            vh = jnp.where(mine, v, jnp.ones_like(v))
            s = jnp.minimum(dot_nt(k, qh), bound)
            top = jnp.max(s, axis=0, keepdims=True)
            e = jnp.exp2((s - top) * EXP2_SCALE).astype(BF)
            e_ref[pair * 2 + half] = e
            ot = dot_tn(vh, e)
            if half == 0:
                o_t, l = ot[:HEAD_DIM], ot[HEAD_DIM:HEAD_DIM + 8]
            else:
                o_t, l = ot[HEAD_DIM:], ot[0:8]
            r = 1.0 / l
            rinv_ref[0, 0, pair * 2 + half] = r
            outs.append(o_t * r[0:1])
        both = jnp.concatenate(outs, axis=0)
        o_ref[0, :, at:at + 128] = both.T.astype(BF)
    slot(HEADS // 2)
    m, r = norm_parts(xs[here, :].astype(F32) + dot(o_ref[0], w[3 * WIDTH:, :]))
    n1 = (m * gain).astype(BF)
    n1s[here, :] = n1
    r1_ref[0] = jnp.broadcast_to(r, (SEQ, 128))


def ffn_unit(n1, f, chunks, w, gd_ref):
    for i, j in enumerate(chunks):
        z = dot(n1, w[j, 0])
        cdf = 0.5 + 0.5 * lax.erf(z * 0.7071067811865476)
        pdf = jnp.exp2(z * (z * (-0.5 * 1.4426950408889634))) * 0.3989422804014327
        gd_ref[0, :, CHUNK * i:CHUNK * (i + 1)] = (cdf + z * pdf).astype(BF)
        f = f + dot((z * cdf).astype(BF), w[j, 1])
    return f


def unit_columns(i):
    row = lax.broadcasted_iota(jnp.int32, (RANK, 2 * RANK), 0)
    column = lax.broadcasted_iota(jnp.int32, (RANK, 2 * RANK), 1)
    return jnp.where(column == row + RANK * i, 1.0, 0.0).astype(BF)


def forward_kernel(axes, direct, len_ref, tok, att, ex, pr, down_ref, up_ref, gain_ref,
                   qkv_out, u_ref, o_ref, e_out, rinv_ref, n1_out, r1_ref, gd_ref, r2_ref, xall, wat_out, wf_out, a_out, b_out,
                   qkv_s, e_s, a_ref, b_ref, xs, n1s, fs, wat, wf, row_sem, x_sem, xo_sem, wa_sem, wf_sem, own_sem, *sems):
    layer, part = pl.program_id(0), pl.program_id(1)
    step = layer * FORWARD_STEPS + part
    x_in = pltpu.make_async_copy(tok, xs, x_sem.at[0])
    x_out = pltpu.make_async_copy(xs, xall.at[0], x_sem.at[1])

    def save_x(l, b):
        rows = pl.ds(pl.multiple_of(b * WIDE, WIDE), WIDE)
        return pltpu.make_async_copy(xs.at[rows], xall.at[l + 1, rows], xo_sem.at[b])

    def save_row(l, row):
        rows = pl.ds(pl.multiple_of(row * SEQ, SEQ), SEQ)
        return (pltpu.make_async_copy(e_s.at[row], e_out.at[l, row], row_sem.at[0, row]),
                pltpu.make_async_copy(qkv_s.at[row], qkv_out.at[l, rows], row_sem.at[1, row]),
                pltpu.make_async_copy(n1s.at[rows], n1_out.at[l, rows], row_sem.at[3, row]))

    save_adapters = (pltpu.make_async_copy(a_ref, a_out, row_sem.at[2, 0]),
                     pltpu.make_async_copy(b_ref, b_out, row_sem.at[2, 1]))

    def save_attention(l):
        return pltpu.make_async_copy(wat.at[l], wat_out.at[l], wa_sem.at[l])

    def save_ffn(l):
        return pltpu.make_async_copy(wf.at[l], wf_out.at[l], wf_sem.at[l])

    def own_ffn(l):
        return [pltpu.make_async_copy(r.at[l], wf.at[l, 0, m], own_sem.at[l, m]) for m, r in enumerate((ex, pr))]

    if direct:
        place = Place(axes)
        n_att = len(ATT_SEMS)
        n_ffn = len(FFN_SEMS)
        att_sems = [sems[:n_att], sems[n_att:2 * n_att]]
        sems = sems[2 * n_att:]
        ffn_sems = [sems[:n_ffn], sems[n_ffn:]]

        def run(job):
            what, l, *more = job
            if what in ("fy", "fown", "fownin", "fr", "ffin"):
                ffn_gather(place, l, ex, pr, wf.at[l], ffn_sems[l], what, *more)
            else:
                attention_gather(place, l, att, wat.at[l], att_sems[l], what, *more)
            if what == "fin3":
                save_attention(l).start()
            if what == "ffin":
                save_ffn(l).start()

    @pl.when(step == 0)
    def _():
        x_in.start()
        for l in range(LAYERS):
            a_ref[l] = sum(dot_tn(down_ref[l, i], unit_columns(i)) for i in range(2)).astype(BF)
            for i in range(2):
                twice = up_ref[l, i].astype(F32) * 2.0
                zero = jnp.zeros_like(twice)
                b_ref[l, i] = jnp.concatenate([twice, zero] if i == 0 else [zero, twice], axis=0).astype(BF)
        for c in save_adapters:
            c.start()
        if direct:
            greet(place, True)
            for l in range(LAYERS):
                for c in own_ffn(l):
                    c.start()
            for job in SCHEDULE[0, 0]:
                run(job)
            for l in range(LAYERS):
                for c in own_ffn(l):
                    c.wait()
        else:
            whole = [pltpu.make_async_copy(att, wat, own_sem.at[0, 0]), pltpu.make_async_copy(ex, wf, own_sem.at[0, 1])]
            for c in whole:
                c.start()
            for c in whole:
                c.wait()
        x_in.wait()
        x_out.start()

    def slot(within):
        for (at, where), jobs in SCHEDULE.items():
            if direct and where == within and (at, where) != (0, 0):
                @pl.when(step == at)
                def _():
                    for job in jobs:
                        run(job)

    slot(0)

    @pl.when(part < ROWS)
    def _():
        @pl.when(layer > 0)
        def _():
            for c in save_row(layer - 1, part):
                c.wait()

        attend_unit(part, len_ref[part], xs, wat.at[layer], a_ref.at[layer], b_ref.at[layer], gain_ref[layer, 0:1],
                    qkv_s.at[part], u_ref, o_ref, e_s.at[part], rinv_ref, r1_ref, n1s,
                    lambda pair: slot(pair) if pair else None)
        for c in save_row(layer, part):
            c.start()

    @pl.when((part >= ROWS) & (part < ROWS + WIDE_STEPS))
    def _():
        @pl.when(step == ROWS)
        def _():
            x_out.wait()

        here = pl.ds(pl.multiple_of((part - ROWS) * WIDE, WIDE), WIDE)
        n1 = n1s[here, :]
        fs[here, :] = ffn_unit(n1, n1.astype(F32), (0, 1), wf.at[layer], gd_ref)

    @pl.when(part >= ROWS + WIDE_STEPS)
    def _():
        block = part - ROWS - WIDE_STEPS

        @pl.when(layer > 0)
        def _():
            save_x(layer - 1, block).wait()

        here = pl.ds(pl.multiple_of(block * WIDE, WIDE), WIDE)
        m, r = norm_parts(ffn_unit(n1s[here, :], fs[here, :], (2, 3), wf.at[layer], gd_ref))
        xs[here, :] = (m * gain_ref[layer, 1:2]).astype(BF)
        r2_ref[0] = jnp.broadcast_to(r, (WIDE, 128))
        save_x(layer, block).start()

    @pl.when(step == LAYERS * FORWARD_STEPS - 1)
    def _():
        for b in range(WIDE_STEPS):
            save_x(LAYERS - 1, b).wait()
        for c in save_adapters:
            c.wait()
        for row in range(ROWS):
            for c in save_row(LAYERS - 1, row):
                c.wait()
        if direct:
            for l in range(LAYERS):
                save_attention(l).wait()
                save_ffn(l).wait()


SCHEDULE = {
    (0, 0): [
        ("line", 0, 0), ("fown", 1), ("fy", 0, 0), ("line", 0, 1), ("side", 0, 0), ("line", 0, 2),
        ("fown", 0), ("side", 0, 1), ("line", 0, 3), ("far", 0, 0), ("line3", 0), ("side", 0, 2),
        ("side", 0, 3), ("line", 1, 0), ("side3", 0), ("fy", 0, 1), ("far", 0, 1), ("fy", 0, 2), ("fy", 0, 3),
        ("line", 1, 1), ("far", 0, 2), ("far", 0, 3), ("fin012", 0), ("fr", 0, 1),
    ],
    (0, 2): [
        ("fownin", 0), ("far3", 0), ("fr", 0, 2),
    ],
    (0, 4): [
        ("line", 1, 2), ("fy", 1, 0), ("fin3", 0),
    ],
    (1, 0): [
        ("fr", 0, 3),
    ],
    (1, 2): [
        ("side", 1, 0), ("fr", 0, 4),
    ],
    (1, 4): [
        ("line", 1, 3), ("side", 1, 1), ("fr", 0, 5),
    ],
    (2, 0): [
        ("fownin", 1), ("side", 1, 2),
    ],
    (3, 0): [
        ("fr", 0, 6),
    ],
    (4, 0): [
        ("side", 1, 3), ("line3", 1), ("ffin", 0),
    ],
    (5, 0): [
        ("far", 1, 0), ("far", 1, 1), ("far", 1, 2), ("far", 1, 3), ("fy", 1, 1), ("fr", 1, 1),
    ],
    (6, 0): [
        ("side3", 1), ("fin012", 1), ("fy", 1, 2),
    ],
    (6, 2): [
        ("fy", 1, 3), ("fr", 1, 2), ("far3", 1),
    ],
    (6, 4): [
        ("fin3", 1),
    ],
    (7, 0): [
        ("fr", 1, 3),
    ],
    (7, 4): [
        ("fr", 1, 4), ("fr", 1, 5),
    ],
    (9, 0): [
        ("fr", 1, 6),
    ],
    (10, 0): [
        ("ffin", 1),
    ],
}


def forward(axes, direct, lengths, tokens, att, ex, pr, down, up, gains):
    anywhere = pl.BlockSpec(memory_space=pl.ANY)
    row_of = lambda p: jnp.minimum(p, ROWS - 1)
    by_row = lambda width: pl.BlockSpec((1, SEQ, width), lambda l, p: (l, row_of(p), 0))
    def half_of(p):
        i = jnp.maximum(p - ROWS, 0)
        half = jnp.where(i >= WIDE_STEPS, 1, 0)
        return i - half * WIDE_STEPS, half

    whole = lambda v: pl.BlockSpec(v.shape, lambda l, p: (0,) * v.ndim, pipeline_mode=pl.Buffered(1))
    a_shape, b_shape = (LAYERS, WIDTH, 2 * RANK), (LAYERS, 2, 2 * RANK, WIDTH)
    shape = jax.ShapeDtypeStruct
    dma = pltpu.SemaphoreType.DMA
    return pl.pallas_call(
        functools.partial(forward_kernel, axes, direct),
        grid=(LAYERS, FORWARD_STEPS),
        in_specs=[pl.BlockSpec(memory_space=pltpu.SMEM)] + [anywhere] * 4 + [whole(down), whole(up), whole(gains)],
        out_specs=[
            anywhere, by_row(2 * RANK), by_row(WIDTH), anywhere,
            pl.BlockSpec((1, 1, HEADS, 8, SEQ), lambda l, p: (l, row_of(p), 0, 0, 0)),
            anywhere, by_row(128),
            pl.BlockSpec((1, WIDE, 2 * CHUNK), lambda l, p: (l, *half_of(p))),
            pl.BlockSpec((1, WIDE, 128), lambda l, p: (l, jnp.maximum(p - ROWS - WIDE_STEPS, 0), 0)),
            anywhere, anywhere, anywhere, anywhere, anywhere,
        ],
        out_shape=[
            shape((LAYERS, TOKENS, 3 * WIDTH), BF), shape((LAYERS, TOKENS, 2 * RANK), BF), shape((LAYERS, TOKENS, WIDTH), BF),
            shape((LAYERS, ROWS, HEADS, SEQ, SEQ), BF), shape((LAYERS, ROWS, HEADS, 8, SEQ), F32),
            shape((LAYERS, TOKENS, WIDTH), BF), shape((LAYERS, TOKENS, 128), F32),
            shape((LAYERS, TOKENS, 4 * CHUNK), BF), shape((LAYERS, TOKENS, 128), F32),
            shape((LAYERS + 1, TOKENS, WIDTH), BF),
            shape((LAYERS, 4 * WIDTH, WIDTH), BF), shape((LAYERS, 4, 2, WIDTH, CHUNK), BF), shape(a_shape, BF), shape(b_shape, BF),
        ],
        scratch_shapes=[
            pltpu.VMEM((ROWS, SEQ, 3 * WIDTH), BF), pltpu.VMEM((ROWS, HEADS, SEQ, SEQ), BF),
            pltpu.VMEM(a_shape, BF), pltpu.VMEM(b_shape, BF),
            pltpu.VMEM((TOKENS, WIDTH), BF), pltpu.VMEM((TOKENS, WIDTH), BF), pltpu.VMEM((TOKENS, WIDTH), F32),
            pltpu.VMEM((LAYERS, 4 * WIDTH, WIDTH), BF), pltpu.VMEM((LAYERS, 4, 2, WIDTH, CHUNK), BF),
            dma((4, ROWS)), dma((2,)), dma((WIDE_STEPS,)), dma((LAYERS,)), dma((LAYERS,)), dma((LAYERS, 2)),
        ] + (ATT_SEMS * 2 + FFN_SEMS * 2 if direct else []),
        compiler_params=params(2, 0 if direct else None),
        name="forward",
    )(lengths, tokens, att, ex, pr, down, up, gains)


def norm_back(e, m, r):
    return r * (e - mean_rows(e) - m * mean_rows(e * m))


def ffn_back_unit(dy, x2_ref, r2_ref, n1_ref, r1_ref, gd_ref, w, wo, gains, wait):
    g1, g2 = gains[0:1], gains[1:2]
    dh2 = norm_back(dy * g2, x2_ref[0].astype(F32) * (1.0 / g2), r2_ref[0, :, 0:1])
    df = dh2.astype(BF)
    dn = dh2
    for j in range(4):
        wait(j)
        dz = (dot_nt(df, w[j, 1]) * gd_ref[0, :, CHUNK * j:CHUNK * (j + 1)].astype(F32)).astype(BF)
        dn = dn + dot_nt(dz, w[j, 0])
    dh = norm_back(dn * g1, n1_ref[0].astype(F32) * (1.0 / g1), r1_ref[0, :, 0:1])
    wait(4)
    return dh, dot_nt(dh.astype(BF), wo[...]).astype(BF)


def attend_back_unit(grp, do_ref, qkv_ref, o_ref, e_ref, rinv_ref, d_ref):
    lane = lax.broadcasted_iota(jnp.int32, (SEQ, 128), 1)
    low = lane < HEAD_DIM
    for pair in range(GROUP // 2):
        at = pl.multiple_of(grp * (GROUP * HEAD_DIM) + pair * 128, 128)
        q = qkv_ref[0, :, pl.ds(at, 128)]
        k = qkv_ref[0, :, pl.ds(WIDTH + at, 128)]
        v = qkv_ref[0, :, pl.ds(2 * WIDTH + at, 128)]
        head = grp * GROUP + pair * 2
        scale = jnp.concatenate([rinv_ref[0, 0, head]] * 8 + [rinv_ref[0, 0, head + 1]] * 8, axis=0).T
        dos = do_ref[:, pl.ds(at, 128)].astype(F32) * scale
        other = pltpu.roll(-dos * o_ref[0, :, pl.ds(at, 128)].astype(F32), HEAD_DIM, 1).astype(BF)
        dos = dos.astype(BF)
        dvs, dks, dqs = [], [], []
        for half in range(2):
            mine = low if half == 0 else ~low
            e = e_ref[0, 0, pair * 2 + half]
            dp = dot_nt(jnp.where(mine, v, jnp.ones_like(v)), jnp.where(mine, dos, other))
            ds = (dp * e.astype(F32)).astype(BF)
            dvs.append(dot(e, dos))
            dks.append(dot(ds, q))
            dqs.append(dot_tn(k, ds)[half * HEAD_DIM:(half + 1) * HEAD_DIM])
        d_ref[:, pl.ds(2 * WIDTH + at, 128)] = jnp.where(low, dvs[0], dvs[1]).astype(BF)
        d_ref[:, pl.ds(WIDTH + at, 128)] = (jnp.where(low, dks[0], dks[1]) * HEAD_DIM ** (-0.5)).astype(BF)
        d_ref[:, pl.ds(at, 128)] = (jnp.concatenate(dqs, axis=0) * HEAD_DIM ** (-0.5)).T.astype(BF)


def split(unit):
    row = sum(jnp.where(unit >= GROUPS * r, 1, 0) for r in range(1, ROWS))
    return row, unit - row * GROUPS


def backward_kernel(cot_ref, x2_ref, r2_ref, n1_ref, r1_ref, gd_ref, x_ref, u_ref, qkv_ref, o_ref, e_ref, rinv_ref,
                    a_ref, b_ref, gain_ref, wat_in, wf_in, xall,
                    dx_ref, grad_ref, hidden,
                    dhs, dos, dys, d_ref, wat, wf, wa_sem, wf_sem, h_sem):
    turn, part = pl.program_id(0), pl.program_id(1)
    layer = LAYERS - 1 - turn
    step = turn * LAYER_STEPS + part
    hidden_copy = pltpu.make_async_copy(xall.at[LAYERS], hidden, h_sem)

    def load_ffn(l, j):
        return pltpu.make_async_copy(wf_in.at[l, j], wf.at[j], wf_sem.at[j])

    def load_attention(l, i):
        rows = pl.ds(3 * WIDTH, WIDTH) if i == 1 else pl.ds(0, 3 * WIDTH)
        return pltpu.make_async_copy(wat_in.at[l, rows], wat.at[l, rows], wa_sem.at[l, i])

    last = LAYERS - 1

    @pl.when(step == 0)
    def _():
        for j in range(4):
            load_ffn(last, j).start()
        load_attention(last, 1).start()
        load_attention(last, 0).start()
        hidden_copy.start()
        grad_ref[...] = jnp.zeros_like(grad_ref)

    for k in range(1, LAYERS):
        @pl.when(step == k * LAYER_STEPS - ATT_STEPS)
        def _():
            for j in range(4):
                load_ffn(last - k, j).start()
            load_attention(last - k, 1).start()
            load_attention(last - k, 0).start()

        @pl.when(step == k * LAYER_STEPS)
        def _():
            for j in range(4):
                load_ffn(last - k, j).wait()
            load_attention(last - k, 1).wait()

        @pl.when(step == k * LAYER_STEPS + FFN_STEPS)
        def _():
            load_attention(last - k, 0).wait()

    @pl.when(step == FFN_STEPS)
    def _():
        load_attention(last, 0).wait()

    def ffn_part(dy, wait):
        here = pl.ds(pl.multiple_of(part * BLOCK, BLOCK), BLOCK)
        dh, do = ffn_back_unit(dy(here), x2_ref, r2_ref, n1_ref, r1_ref, gd_ref, wf, wat.at[layer, 3 * WIDTH:, :],
                               gain_ref[layer], wait)
        dhs[here, :] = dh
        dos[here, :] = do

    def wait_load(j):
        if j < 4:
            load_ffn(last, j).wait()
        else:
            load_attention(last, 1).wait()

    @pl.when(step == 0)
    def _():
        ffn_part(lambda here: cot_ref[...].astype(F32), wait_load)

    @pl.when((step > 0) & (step < FFN_STEPS))
    def _():
        ffn_part(lambda here: cot_ref[...].astype(F32), lambda j: None)

    @pl.when((step >= LAYER_STEPS) & (part < FFN_STEPS))
    def _():
        ffn_part(lambda here: dys[here, :], lambda j: None)

    @pl.when(part >= FFN_STEPS)
    def _():
        row, grp = split(part - FFN_STEPS)
        here = pl.ds(pl.multiple_of(row * SEQ, SEQ), SEQ)
        attend_back_unit(grp, dos.at[here], qkv_ref, o_ref, e_ref, rinv_ref, d_ref)

        @pl.when(grp == GROUPS - 1)
        def _():
            dq, dk, dv = (d_ref[:, WIDTH * i:WIDTH * (i + 1)] for i in range(3))
            du = (dot_nt(dq, b_ref[layer, 0]) + dot_nt(dv, b_ref[layer, 1])).astype(BF)
            u = u_ref[0]
            u2 = u + u
            ga = dot_tn(du, x_ref[0])
            gq = dot_tn(u2, dq)[:RANK]
            gv = dot_tn(u2, dv)[RANK:]
            grad_ref[layer] += jnp.concatenate([ga, gq, gv], axis=0)
            w = wat.at[layer]
            dx = (dhs[here, :] + dot_nt(dq, w[0:WIDTH, :]) + dot_nt(dk, w[WIDTH:2 * WIDTH, :])
                  + dot_nt(dv, w[2 * WIDTH:3 * WIDTH, :]) + dot_nt(du, a_ref[layer]))

            @pl.when(layer > 0)
            def _():
                dys[here, :] = dx

            @pl.when(layer == 0)
            def _():
                dx_ref[...] = dx

    @pl.when(step == LAYERS * LAYER_STEPS - 1)
    def _():
        hidden_copy.wait()


def backward(cot, saved, a, b, gains, wat, wf):
    qkv, u, o, e, rinv, n1, r1, gd, r2, xall = saved
    anywhere = pl.BlockSpec(memory_space=pl.ANY)
    layer_of = lambda t: LAYERS - 1 - t
    block_of = lambda p: jnp.minimum(p, FFN_STEPS - 1)
    unit_of = lambda p: split(jnp.maximum(p - FFN_STEPS, 0))
    row_of = lambda p: unit_of(p)[0]
    by_row = lambda width: pl.BlockSpec((1, SEQ, width), lambda t, p: (layer_of(t), row_of(p), 0))
    by_block = lambda width: pl.BlockSpec((1, BLOCK, width), lambda t, p: (layer_of(t), block_of(p), 0))
    whole = lambda v: pl.BlockSpec(v.shape, lambda t, p: (0,) * v.ndim, pipeline_mode=pl.Buffered(1))
    shape = jax.ShapeDtypeStruct
    dma = pltpu.SemaphoreType.DMA
    return pl.pallas_call(
        backward_kernel,
        grid=(LAYERS, LAYER_STEPS),
        in_specs=[
            pl.BlockSpec((BLOCK, WIDTH), lambda t, p: (jnp.where(t == 0, block_of(p), FFN_STEPS - 1), 0)),
            pl.BlockSpec((1, BLOCK, WIDTH), lambda t, p: (layer_of(t) + 1, block_of(p), 0)),
            by_block(128), by_block(WIDTH), by_block(128), by_block(4 * CHUNK),
            by_row(WIDTH), by_row(2 * RANK), by_row(3 * WIDTH), by_row(WIDTH),
            pl.BlockSpec((1, 1, GROUP, SEQ, SEQ), lambda t, p: (layer_of(t), *unit_of(p), 0, 0)),
            pl.BlockSpec((1, 1, HEADS, 8, SEQ), lambda t, p: (layer_of(t), row_of(p), 0, 0, 0)),
            whole(a), whole(b), whole(gains), anywhere, anywhere, anywhere,
        ],
        out_specs=[
            pl.BlockSpec((SEQ, WIDTH), lambda t, p: (jnp.where(t < LAYERS - 1, 0, row_of(p)), 0)),
            pl.BlockSpec((LAYERS, 4 * RANK, WIDTH), lambda t, p: (0, 0, 0)),
            anywhere,
        ],
        out_shape=[shape((TOKENS, WIDTH), F32), shape((LAYERS, 4 * RANK, WIDTH), F32), shape((TOKENS, WIDTH), BF)],
        scratch_shapes=[
            pltpu.VMEM((TOKENS, WIDTH), F32), pltpu.VMEM((TOKENS, WIDTH), BF), pltpu.VMEM((TOKENS, WIDTH), F32),
            pltpu.VMEM((SEQ, 3 * WIDTH), BF), pltpu.VMEM((LAYERS, 4 * WIDTH, WIDTH), BF),
            pltpu.VMEM((4, 2, WIDTH, CHUNK), BF),
            dma((LAYERS, 2)), dma((4,)), dma,
        ],
        compiler_params=params(2),
        name="backward",
    )(cot, xall, r2, n1, r1, gd, xall, u, qkv, o, e, rinv, a, b, gains, wat, wf, xall)


def local(axes, direct, tokens, lengths, attention, down, up, expand, project, gains, cotangent):
    if direct:
        att, ex, pr = attention, expand, project
    else:
        att = lax.all_gather(attention, axes, axis=1, tiled=True)
        w1 = lax.all_gather(expand, axes[1], axis=2, tiled=True).reshape(LAYERS, WIDTH, 4, CHUNK).transpose(0, 2, 1, 3)
        w2 = lax.all_gather(project, axes[1], axis=1, tiled=True).reshape(LAYERS, 4, CHUNK, WIDTH)
        ex = pr = jnp.stack([w1, w2], axis=2)
    *saved, wat, wf, a, b = forward(axes, direct, lengths, tokens, att, ex, pr, down.swapaxes(2, 3), up, gains)
    if not direct:
        wat, wf = att, ex
    dx, grads, hidden = backward(cotangent, saved, a, b, gains, wat, wf)
    if direct:
        total = all_sum(axes, grads, 1)
    else:
        total = lax.psum(grads, axes)
    a_grad = total[:, :2 * RANK].reshape(LAYERS, 2, RANK, WIDTH).transpose(0, 1, 3, 2)
    b_grad = total[:, 2 * RANK:].reshape(LAYERS, 2, RANK, WIDTH)
    return hidden, dx, a_grad, b_grad


def solution(mesh):
    axes = tuple(mesh.axis_names)
    dp, tensor = axes
    direct = mesh.shape[dp] == 2 * Z_SIZE and mesh.shape[tensor] == 4
    placed = (
        P(axes, None), P(axes), P(None, axes, None), P(), P(),
        P(None, None, tensor), P(None, tensor, None), P(), P(axes, None),
    )
    return jax.shard_map(
        functools.partial(local, axes, direct),
        mesh=mesh,
        in_specs=placed,
        out_specs=(P(axes, None), P(axes, None), P(), P()),
        check_vma=False,
    )
```
